32 devices in a mesh: dp: 8 (over z, x), row: 2 (over core), col: 2 (over y).
Axes of the slice: x: 2, y: 2, z: 4, core: 2. Of those that a mesh axis runs over, the one named last changes fastest.
Arguments:
- tokens: bfloat16 [25216, 768], P(('dp', 'row'), 'col'), may hold values from -6 to 6
- cotangent: bfloat16 [25216, 768], P(('dp', 'row'), 'col'), may hold values from -6 to 6
- ln1_gain: float32 [768], P('col'), may hold values from 0.1 to 1.9
- ln1_bias: float32 [768], P('col'), may hold values from -1.5 to 1.5
- qkv_weight: bfloat16 [768, 2304], P('col', 'row'), may hold values from -0.21875 to 0.21875
- qv_bias: float32 [1536], P('row'), may hold values from -1.5 to 1.5
- out_weight: bfloat16 [768, 768], P('row', 'col'), may hold values from -1.5 to 1.5
- out_bias: float32 [768], P('col'), may hold values from -1.5 to 1.5
- ln2_gain: float32 [768], P('col'), may hold values from 0.1 to 1.9
- ln2_bias: float32 [768], P('col'), may hold values from -1.5 to 1.5
- fc1_weight: bfloat16 [768, 3072], P('col', 'row'), may hold values from -0.21875 to 0.21875
- fc1_bias: float32 [3072], P('row'), may hold values from -1.5 to 1.5
- fc2_weight: bfloat16 [3072, 768], P('row', 'col'), may hold values from -0.109375 to 0.109375
- fc2_bias: float32 [768], P('col'), may hold values from -1.5 to 1.5
Outputs:
- result: bfloat16 [25216, 768], P(('dp', 'row'), 'col')
- input_grad: float32 [25216, 768], P(('dp', 'row'), 'col')
- ln1_gain_grad: float32 [768], P('col')
- ln1_bias_grad: float32 [768], P('col')
- qkv_weight_grad: float32 [768, 2304], P('col', 'row')
- qv_bias_grad: float32 [1536], P('row')
- out_weight_grad: float32 [768, 768], P('row', 'col')
- out_bias_grad: float32 [768], P('col')
- ln2_gain_grad: float32 [768], P('col')
- ln2_bias_grad: float32 [768], P('col')
- fc1_weight_grad: float32 [768, 3072], P('col', 'row')
- fc1_bias_grad: float32 [3072], P('row')
- fc2_weight_grad: float32 [3072, 768], P('row', 'col')
- fc2_bias_grad: float32 [768], P('col')
The draws below stay inside these ranges and needn't reach their ends.
All inputs are finite; a program needn't handle non-finite values.
Results may differ from the reference program's by a relative error of at most 0.011.
Values may be sent and summed in bfloat16 or wider, within the bound.
No kernel may reach another device: no remote copies, remote signals or barrier semaphores. Data moves between devices by JAX's collectives and lax.ppermute only.
A program may use at most 192 MiB of HBM per device.

```python
import jax
import jax.numpy as jnp
from jax import lax

D = 768
HEADS = 12
HEAD = 64
FF = 3072
SEQ = 197
IMG_DEV = 8
TOKENS = 25216
N_ROW = 2


def level_of(stream_key, dims, split, low, high):
    def one(position, blocks):
        heights = jax.random.uniform(jax.random.fold_in(jax.random.fold_in(stream_key, 6), position), (blocks,), jnp.float32, low / len(split), high / len(split))
        return jnp.repeat(jnp.exp(heights), dims[position] // blocks).reshape((-1,) + (1,) * (len(dims) - position - 1))

    factor_of = one(*split[0])
    for cut in split[1:]:
        factor_of = factor_of * one(*cut)
    return factor_of


def bell_draw(key, dims, deviation, reach, split=(), dtype=jnp.bfloat16):
    drawn = deviation * jax.random.normal(key, dims, jnp.float32)
    if split:
        drawn = drawn * level_of(key, dims, split, -0.22, 0.18)
    return jnp.clip(drawn, -reach, reach).astype(dtype)


def setup_inputs(seed: int = 0) -> dict:
    key_list = jax.random.split(jax.random.key(seed), 15)
    tokens = bell_draw(key_list[0], (TOKENS, D), 1.0, 6.0, ((0, 16), (1, 2)))
    cotangent = bell_draw(key_list[1], (TOKENS, D), 1.0, 6.0, ((0, 16), (1, 2)))
    ln1_gain = jnp.clip(1.0 + 0.18 * jax.random.normal(key_list[2], (D,), jnp.float32), 0.1, 1.9)
    ln1_bias = bell_draw(key_list[3], (D,), 0.3, 1.5, ((0, 2),), jnp.float32)
    qkv_weight = bell_draw(key_list[4], (D, 3 * D), D ** -0.5, 0.21875, ((0, 2), (1, 2)))
    qv_bias = bell_draw(key_list[5], (2 * D,), 0.3, 1.5, ((0, 2),), jnp.float32)
    out_weight = bell_draw(key_list[6], (D, D), (max(1, D * 4 // SEQ)) ** -0.5, 1.5, ((0, 2), (1, 2)))
    out_bias = bell_draw(key_list[7], (D,), 0.3, 1.5, ((0, 2),), jnp.float32)
    ln2_gain = jnp.clip(1.0 + 0.18 * jax.random.normal(key_list[8], (D,), jnp.float32), 0.1, 1.9)
    ln2_bias = bell_draw(key_list[9], (D,), 0.3, 1.5, ((0, 2),), jnp.float32)
    fc1_weight = bell_draw(key_list[10], (D, FF), D ** -0.5, 0.21875, ((0, 2), (1, 2)))
    fc1_bias = bell_draw(key_list[11], (FF,), 0.3, 1.5, ((0, 2),), jnp.float32)
    fc2_weight = bell_draw(key_list[12], (FF, D), FF ** -0.5, 0.109375, ((0, 2), (1, 2)))
    fc2_bias = bell_draw(key_list[13], (D,), 0.3, 1.5, ((0, 2),), jnp.float32)
    return {"tokens": tokens, "cotangent": cotangent, "ln1_gain": ln1_gain, "ln1_bias": ln1_bias, "qkv_weight": qkv_weight, "qv_bias": qv_bias, "out_weight": out_weight, "out_bias": out_bias, "ln2_gain": ln2_gain, "ln2_bias": ln2_bias, "fc1_weight": fc1_weight, "fc1_bias": fc1_bias, "fc2_weight": fc2_weight, "fc2_bias": fc2_bias}


@jax.custom_vjp
def low(v):
    return lax.optimization_barrier(v.astype(jnp.bfloat16)).astype(jnp.float32)

@jax.custom_vjp
def low_back(v):
    return v

def low_keep(v):
    return (low(v), None)

def low_pass(kept, grad):
    return (grad,)

def back_keep(v):
    return (v, None)

def back_low(kept, grad):
    return (low(grad),)
low.defvjp(low_keep, low_pass)
low_back.defvjp(back_keep, back_low)
EPSILON = 1e-06
HIGHEST = lax.Precision.HIGHEST

def matmul(left, right):
    return jnp.dot(left, right, precision=HIGHEST)

def normalize(stream, gain_row, shift_row):
    row_mean = lax.optimization_barrier(jnp.mean(stream, axis=-1, keepdims=True))
    centred = stream - row_mean
    variance = lax.optimization_barrier(jnp.mean(centred * centred, axis=-1, keepdims=True))
    return centred * lax.rsqrt(variance + EPSILON) * gain_row + shift_row

def encoder_layer(params, stream):
    ln1_gain, ln1_bias, qkv_weight, qv_bias, out_weight, out_bias, ln2_gain, ln2_bias, fc1_weight, fc1_bias, fc2_weight, fc2_bias = params
    token_count = stream.shape[0]
    images = token_count // SEQ
    normed = low(normalize(stream, ln1_gain, ln1_bias))
    bias_pairs = qv_bias.reshape(HEADS, 2, HEAD)
    triple = jnp.stack([bias_pairs[:, 0], jnp.zeros_like(bias_pairs[:, 0]), bias_pairs[:, 1]], axis=1)
    packed = matmul(normed, qkv_weight).reshape(token_count, HEADS, 3, HEAD) + triple
    packed = low_back(low(packed))
    packed = packed.reshape(images, SEQ, HEADS, 3, HEAD)
    queries = packed[:, :, :, 0]
    key_rows = packed[:, :, :, 1]
    values = packed[:, :, :, 2]
    scores = low_back(jnp.einsum('iqhe,ikhe->ihqk', queries, key_rows, precision=HIGHEST) * HEAD ** (-0.5))
    largest = lax.optimization_barrier(jnp.max(scores, axis=-1, keepdims=True))
    raised = jnp.exp(scores - largest)
    weights_soft = low(raised / lax.optimization_barrier(jnp.sum(raised, axis=-1, keepdims=True)))
    attended = jnp.einsum('ihqk,ikhe->iqhe', weights_soft, values, precision=HIGHEST).reshape(token_count, D)
    attended = low_back(low(attended))
    middle = stream + low_back(matmul(attended, out_weight) + out_bias)
    hidden_in = low(normalize(middle, ln2_gain, ln2_bias))
    before = low_back(matmul(hidden_in, fc1_weight) + fc1_bias)
    active = low(jax.nn.gelu(before, approximate=False))
    return middle + matmul(active, fc2_weight) + fc2_bias

def reference(tokens, cotangent, ln1_gain, ln1_bias, qkv_weight, qv_bias, out_weight, out_bias, ln2_gain, ln2_bias, fc1_weight, fc1_bias, fc2_weight, fc2_bias):
    params = tuple((member.astype(jnp.float32) for member in (ln1_gain, ln1_bias, qkv_weight, qv_bias, out_weight, out_bias, ln2_gain, ln2_bias, fc1_weight, fc1_bias, fc2_weight, fc2_bias)))
    group_rows = IMG_DEV * N_ROW * SEQ

    def forward(weights, stream):
        blocks = stream.reshape(-1, group_rows, D)

        def advance(carried, block_rows):
            return (carried, jax.checkpoint(encoder_layer)(weights, block_rows))
        ignored, outputs = lax.scan(advance, jnp.zeros((), jnp.float32), blocks)
        return outputs.reshape(stream.shape)
    result, pullback = jax.vjp(forward, params, tokens.astype(jnp.float32))
    gradients, input_grad = pullback(cotangent.astype(jnp.float32))
    return (result.astype(jnp.bfloat16), input_grad, gradients[0], gradients[1], gradients[2], gradients[3], gradients[4], gradients[5], gradients[6], gradients[7], gradients[8], gradients[9], gradients[10], gradients[11])
```

```python
from functools import partial

import jax
import jax.numpy as jnp
from jax import lax
from jax.experimental import pallas as pl
from jax.experimental.pallas import tpu as pltpu
from jax.sharding import PartitionSpec as P

HEAD = 64
SEQ = 197
PAD = 208
EPSILON = 1e-06
LEFT_INNER = (((0,), (0,)), ((), ()))
RIGHT_INNER = (((1,), (1,)), ((), ()))
BF16 = jnp.bfloat16
F32 = jnp.float32


def swap(values, axis):
    return lax.ppermute(values, axis, [(0, 1), (1, 0)])


def matmul(left, right):
    return jnp.dot(left, right, preferred_element_type=F32)


def matmul_left(left, right):
    return lax.dot_general(left, right, LEFT_INNER, preferred_element_type=F32)


def matmul_right(left, right):
    return lax.dot_general(left, right, RIGHT_INNER, preferred_element_type=F32)


def split_pair(c0, c1, c2):
    low = lax.broadcasted_iota(jnp.int32, c0.shape, 1) < HEAD
    queries = jnp.where(low, c0, c1)
    key_rows = pltpu.roll(jnp.where(low, c2, c0), HEAD, 1)
    values = jnp.where(low, c1, c2)
    return queries, key_rows, values, low


def attend_kernel(packed_ref, attended_ref, probs_ref):
    images = packed_ref.shape[0]
    for image in range(images):
        blocks = [packed_ref[image, :, 128 * j : 128 * (j + 1)].astype(F32) for j in range(3)]
        queries, key_rows, values, low = split_pair(*blocks)
        keys_low = key_rows.astype(BF16)
        values_low = values.astype(BF16)
        outs = []
        for head in range(2):
            chosen = low if head == 0 else jnp.logical_not(low)
            masked = jnp.where(chosen, queries * HEAD**-0.5, 0.0).astype(BF16)
            scores = matmul_right(masked, keys_low)
            real = lax.broadcasted_iota(jnp.int32, scores.shape, 1) < SEQ
            scores = jnp.where(real, scores, -1e30)
            raised = jnp.exp(scores - jnp.max(scores, axis=1, keepdims=True))
            probs = (raised * (1.0 / jnp.sum(raised, axis=1, keepdims=True))).astype(BF16)
            probs_ref[0, image, head] = probs
            outs.append(matmul(probs, values_low))
        attended_ref[image] = jnp.where(low, outs[0], outs[1]).astype(BF16)


def attend(packed):
    images, _, columns = packed.shape
    pairs = columns // (6 * HEAD)
    return pl.pallas_call(
        attend_kernel,
        grid=(pairs,),
        in_specs=[pl.BlockSpec((images, PAD, 6 * HEAD), lambda p: (0, 0, p))],
        out_specs=[
            pl.BlockSpec((images, PAD, 2 * HEAD), lambda p: (0, 0, p)),
            pl.BlockSpec((1, images, 2, PAD, PAD), lambda p: (p, 0, 0, 0, 0)),
        ],
        out_shape=[
            jax.ShapeDtypeStruct((images, PAD, columns // 3), BF16),
            jax.ShapeDtypeStruct((pairs, images, 2, PAD, PAD), BF16),
        ],
        compiler_params=pltpu.CompilerParams(vmem_limit_bytes=32 * 2**20),
        cost_estimate=pl.CostEstimate(flops=3 * 10**9, bytes_accessed=12 * 2**20, transcendentals=0),
    )(packed)


def attend_back_kernel(packed_ref, probs_ref, grad_ref, out_ref):
    images = packed_ref.shape[0]
    for image in range(images):
        blocks = [packed_ref[image, :, 128 * j : 128 * (j + 1)].astype(F32) for j in range(3)]
        queries, key_rows, values, low = split_pair(*blocks)
        values_low = values.astype(BF16)
        upstream = grad_ref[image].astype(F32)
        query_grad = key_grad = value_grad = 0.0
        for head in range(2):
            chosen = low if head == 0 else jnp.logical_not(low)
            up = jnp.where(chosen, upstream, 0.0).astype(BF16)
            query_head = jnp.where(chosen, queries * HEAD**-0.5, 0.0).astype(BF16)
            key_head = jnp.where(chosen, key_rows * HEAD**-0.5, 0.0).astype(BF16)
            probs = probs_ref[0, image, head]
            value_grad += matmul_left(probs, up)
            prob_grad = matmul_right(up, values_low)
            wide = probs.astype(F32)
            weighted = wide * prob_grad
            score_grad = (
                weighted - wide * jnp.sum(weighted, axis=1, keepdims=True)
            ).astype(BF16)
            query_grad += matmul(score_grad, key_head)
            key_grad += matmul_left(score_grad, query_head)
        key_turned = pltpu.roll(key_grad, HEAD, 1)
        out_ref[image, :, 0:128] = jnp.where(low, query_grad, key_turned).astype(BF16)
        out_ref[image, :, 128:256] = jnp.where(low, value_grad, query_grad).astype(BF16)
        out_ref[image, :, 256:384] = jnp.where(low, key_turned, value_grad).astype(BF16)


def attend_back(packed, probs, upstream):
    images, _, columns = packed.shape
    pairs = columns // (6 * HEAD)
    return pl.pallas_call(
        attend_back_kernel,
        grid=(pairs,),
        in_specs=[
            pl.BlockSpec((images, PAD, 6 * HEAD), lambda p: (0, 0, p)),
            pl.BlockSpec((1, images, 2, PAD, PAD), lambda p: (p, 0, 0, 0, 0)),
            pl.BlockSpec((images, PAD, 2 * HEAD), lambda p: (0, 0, p)),
        ],
        out_specs=pl.BlockSpec((images, PAD, 6 * HEAD), lambda p: (0, 0, p)),
        out_shape=jax.ShapeDtypeStruct(packed.shape, BF16),
        compiler_params=pltpu.CompilerParams(vmem_limit_bytes=32 * 2**20),
        cost_estimate=pl.CostEstimate(flops=8 * 10**9, bytes_accessed=16 * 2**20, transcendentals=0),
    )(packed, probs, upstream)


def normalize(stream, gain_row, shift_row):
    row_mean = jnp.mean(stream, axis=1, keepdims=True)
    centred = stream - row_mean
    inverse = lax.rsqrt(jnp.mean(centred * centred, axis=1, keepdims=True) + EPSILON)
    unit_rows = centred * inverse
    return unit_rows, inverse, (unit_rows * gain_row + shift_row).astype(BF16)


def normalize_back(upstream, unit_rows, inverse, gain_row):
    scaled = upstream * gain_row
    first = jnp.mean(scaled, axis=1, keepdims=True)
    second = jnp.mean(scaled * unit_rows, axis=1, keepdims=True)
    return (
        inverse * (scaled - first - unit_rows * second),
        jnp.sum(upstream * unit_rows, axis=0),
        jnp.sum(upstream, axis=0),
    )


def whole_weight(block, row_dim):
    tall = jnp.concatenate([block, swap(block, "col")], axis=1 - row_dim)
    return jnp.concatenate([tall, swap(tall, "row")], axis=row_dim)


def trade_half(total, axis, dim):
    own, other = jnp.split(total, 2, axis=dim)
    return own + swap(other.astype(BF16), axis).astype(F32)


def sum_images(total):
    size = lax.axis_size("dp")
    me = lax.axis_index("dp")
    shape = total.shape
    held = total.reshape(-1, shape[-1])
    steps = []
    step = 1
    while step < size:
        steps.append(step)
        step *= 2
    for step in steps:
        half = held.shape[0] // 2
        bit = (me // step) % 2
        own = lax.dynamic_slice_in_dim(held, bit * half, half, 0)
        other = lax.dynamic_slice_in_dim(held, (1 - bit) * half, half, 0)
        pairs = [(i, i ^ step) for i in range(size)]
        held = own + lax.ppermute(other.astype(BF16), "dp", pairs).astype(F32)
    held = held.astype(BF16)
    for step in reversed(steps):
        bit = (me // step) % 2
        pairs = [(i, i ^ step) for i in range(size)]
        other = lax.ppermute(held, "dp", pairs)
        held = jnp.where(
            bit == 0,
            jnp.concatenate([held, other], axis=0),
            jnp.concatenate([other, held], axis=0),
        )
    return held.reshape(shape).astype(F32)


def sum_weight(total, row_dim):
    return sum_images(trade_half(trade_half(total, "row", row_dim), "col", 1 - row_dim))


def sum_small(values):
    size = lax.axis_size("dp")
    step = 1
    while step < size:
        values = values + lax.ppermute(values, "dp", [(i, i ^ step) for i in range(size)])
        step *= 2
    return values


def per_device(
    tokens,
    cotangent,
    ln1_gain,
    ln1_bias,
    qkv_weight,
    qv_bias,
    out_weight,
    out_bias,
    ln2_gain,
    ln2_bias,
    fc1_weight,
    fc1_bias,
    fc2_weight,
    fc2_bias,
):
    col = lax.axis_index("col")
    half = tokens.shape[0] // 2
    images = half // SEQ
    rows = images * PAD

    def take_images(block):
        own = lax.dynamic_slice_in_dim(block, col * half, half, 0)
        other = lax.dynamic_slice_in_dim(block, (1 - col) * half, half, 0)
        joined = jnp.concatenate([own, swap(other, "col")], axis=1)
        padded = jnp.pad(joined.reshape(images, SEQ, -1), ((0, 0), (0, PAD - SEQ), (0, 0)))
        return padded.reshape(rows, -1)

    def give_images(block):
        cut = block.reshape(images, PAD, -1)[:, :SEQ].reshape(half, -1)
        own, other = jnp.split(cut, 2, axis=1)
        other = swap(other.astype(BF16), "col").astype(own.dtype)
        return jnp.where(
            col == 0,
            jnp.concatenate([own, other], axis=0),
            jnp.concatenate([other, own], axis=0),
        )

    stream = take_images(tokens).astype(F32)
    col_rows = jnp.stack([ln1_gain, ln1_bias, ln2_gain, ln2_bias, out_bias, fc2_bias])
    col_rows = jnp.concatenate([col_rows, swap(col_rows, "col")], axis=1)
    gain1, shift1, gain2, shift2, out_shift, fc2_shift = [col_rows[i] for i in range(6)]
    row_values = jnp.concatenate([qv_bias, fc1_bias])
    row_other = swap(row_values, "row")
    qv_size = qv_bias.shape[0]
    bias_pairs = jnp.concatenate([row_values[:qv_size], row_other[:qv_size]]).reshape(-1, 2, HEAD)
    triple = jnp.stack(
        [bias_pairs[:, 0], jnp.zeros_like(bias_pairs[:, 0]), bias_pairs[:, 1]], axis=1
    ).reshape(-1)
    fc1_shift = jnp.concatenate([row_values[qv_size:], row_other[qv_size:]])

    qkv_full = whole_weight(qkv_weight, 1)
    out_full = whole_weight(out_weight, 0)
    fc1_full = whole_weight(fc1_weight, 1)
    fc2_full = whole_weight(fc2_weight, 0)
    upstream = take_images(cotangent)

    unit1, inverse1, normed1 = normalize(stream, gain1, shift1)
    packed = (matmul(normed1, qkv_full) + triple).astype(BF16)
    shaped = packed.reshape(images, PAD, -1)
    attended, probs = attend(shaped)
    attended = attended.reshape(rows, -1)
    middle = stream + matmul(attended, out_full) + out_shift
    unit2, inverse2, normed2 = normalize(middle, gain2, shift2)
    before = matmul(normed2, fc1_full) + fc1_shift
    active, gelu_pull = jax.vjp(partial(jax.nn.gelu, approximate=False), before)
    active = active.astype(BF16)
    result = (middle + matmul(active, fc2_full) + fc2_shift).astype(BF16)

    fc2_wgrad = sum_weight(matmul_left(active, upstream), 0)
    fc2_bgrad = jnp.sum(upstream, axis=0, dtype=F32)
    before_grad = gelu_pull(matmul_right(upstream, fc2_full))[0].astype(BF16)
    fc1_wgrad = sum_weight(matmul_left(normed2, before_grad), 1)
    fc1_bgrad = jnp.sum(before_grad, axis=0, dtype=F32)
    normed2_grad = matmul_right(before_grad, fc1_full)
    middle_part, ln2_ggrad, ln2_bgrad = normalize_back(normed2_grad, unit2, inverse2, gain2)
    middle_grad = upstream.astype(F32) + middle_part
    middle_low = middle_grad.astype(BF16)
    out_wgrad = sum_weight(matmul_left(attended, middle_low), 0)
    out_bgrad = jnp.sum(middle_low, axis=0, dtype=F32)
    attended_grad = matmul_right(middle_low, out_full).astype(BF16)
    packed_grad = attend_back(shaped, probs, attended_grad.reshape(images, PAD, -1))
    packed_grad = packed_grad.reshape(rows, -1)
    qkv_wgrad = sum_weight(matmul_left(normed1, packed_grad), 1)
    packed_bgrad = jnp.sum(packed_grad, axis=0, dtype=F32)
    normed1_grad = matmul_right(packed_grad, qkv_full)
    input_part, ln1_ggrad, ln1_bgrad = normalize_back(normed1_grad, unit1, inverse1, gain1)
    input_grad = middle_grad + input_part

    bias_kinds = packed_bgrad.reshape(-1, 3, HEAD)
    qv_grad = jnp.stack([bias_kinds[:, 0], bias_kinds[:, 2]], axis=1).reshape(2, -1)
    by_row = jnp.concatenate([qv_grad, fc1_bgrad.reshape(2, -1)], axis=1)
    by_row = by_row[0] + swap(by_row[1], "row")
    by_row = by_row + swap(by_row, "col")
    by_col = jnp.stack([ln1_ggrad, ln1_bgrad, ln2_ggrad, ln2_bgrad, out_bgrad, fc2_bgrad])
    by_col = by_col.reshape(6, 2, -1)
    by_col = by_col[:, 0] + swap(by_col[:, 1], "col")
    by_col = by_col + swap(by_col, "row")
    small = sum_small(jnp.concatenate([by_row, by_col.reshape(-1)]))
    by_col = small[by_row.shape[0] :].reshape(6, -1)
    return (
        give_images(result),
        give_images(input_grad),
        by_col[0],
        by_col[1],
        qkv_wgrad,
        small[:qv_size],
        out_wgrad,
        by_col[4],
        by_col[2],
        by_col[3],
        fc1_wgrad,
        small[qv_size : by_row.shape[0]],
        fc2_wgrad,
        by_col[5],
    )


def solution(mesh):
    stream = P(("dp", "row"), "col")
    by_col, by_row = P("col"), P("row")
    wide, deep = P("col", "row"), P("row", "col")
    in_specs = (
        stream, stream, by_col, by_col, wide, by_row, deep, by_col,
        by_col, by_col, wide, by_row, deep, by_col,
    )
    return jax.shard_map(
        per_device, mesh=mesh, in_specs=in_specs, out_specs=in_specs, check_vma=False
    )
```

```python
from functools import partial

import jax
import jax.numpy as jnp
from jax import lax
from jax.experimental import pallas as pl
from jax.experimental.pallas import tpu as pltpu
from jax.sharding import PartitionSpec as P

HEAD = 64
SEQ = 197
PAD = 208
EXTRA = 32
EPSILON = 1e-06
LEFT_INNER = (((0,), (0,)), ((), ()))
RIGHT_INNER = (((1,), (1,)), ((), ()))
BF16 = jnp.bfloat16
F32 = jnp.float32


def swap(values, axis):
    return lax.ppermute(values, axis, [(0, 1), (1, 0)])


def matmul(left, right):
    return jnp.dot(left, right, preferred_element_type=F32)


def matmul_left(left, right):
    return lax.dot_general(left, right, LEFT_INNER, preferred_element_type=F32)


def matmul_right(left, right):
    return lax.dot_general(left, right, RIGHT_INNER, preferred_element_type=F32)


def split_pair(c0, c1, c2):
    low = lax.broadcasted_iota(jnp.int32, c0.shape, 1) < HEAD
    queries = jnp.where(low, c0, c1)
    key_rows = pltpu.roll(jnp.where(low, c2, c0), HEAD, 1)
    values = jnp.where(low, c1, c2)
    return queries, key_rows, values, low


def to_half(staged_ref, own_ref, far_ref):
    first_half = pl.program_id(0) < pl.num_programs(0) // 2

    @pl.when(first_half)
    def _():
        own_ref[...] = staged_ref[...]

    @pl.when(jnp.logical_not(first_half))
    def _():
        far_ref[...] = staged_ref[...]


def run_kernel(kernel, values, after, in_specs, out_specs, out_shape, **settings):
    values, after = list(values), jax.tree.leaves(after)
    count, skip = len(values), len(values) + len(after)
    outs = len(out_shape)

    def body(*refs):
        end_ref = refs[skip + outs]
        end_ref[...] = jnp.zeros_like(end_ref)
        kernel(*refs[:count], *refs[skip : skip + outs], *refs[skip + outs + 1 :])

    unread = [pl.BlockSpec(memory_space=pl.ANY)] * len(after)
    end = jax.ShapeDtypeStruct((8, 128), F32)
    return pl.pallas_call(
        body,
        in_specs=list(in_specs) + unread,
        out_specs=list(out_specs) + [whole_spec(end)],
        out_shape=list(out_shape) + [end],
        **settings,
    )(*values, *after)


def attend_kernel(packed_ref, own_ref, far_ref, probs_ref, staged_ref):
    images = packed_ref.shape[0] // PAD
    for image in range(images):
        rows = slice(image * PAD, (image + 1) * PAD)
        blocks = [packed_ref[rows, 128 * j : 128 * (j + 1)].astype(F32) for j in range(3)]
        queries, key_rows, values, low = split_pair(*blocks)
        keys_low = key_rows.astype(BF16)
        values_low = values.astype(BF16)
        outs = []
        for head in range(2):
            chosen = low if head == 0 else jnp.logical_not(low)
            masked = jnp.where(chosen, queries * HEAD**-0.5, 0.0).astype(BF16)
            scores = matmul_right(masked, keys_low)
            real = lax.broadcasted_iota(jnp.int32, scores.shape, 1) < SEQ
            scores = jnp.where(real, scores, -1e30)
            raised = jnp.exp(scores - jnp.max(scores, axis=1, keepdims=True))
            probs = (raised * (1.0 / jnp.sum(raised, axis=1, keepdims=True))).astype(BF16)
            probs_ref[0, image, head] = probs
            outs.append(matmul(probs, values_low))
        staged_ref[rows] = jnp.where(low, outs[0], outs[1]).astype(BF16)
    to_half(staged_ref, own_ref, far_ref)


def halves_specs(rows, width, steps):
    half = steps // 2
    return [
        pl.BlockSpec((rows, width), lambda p: (0, jnp.minimum(p, half - 1))),
        pl.BlockSpec((rows, width), lambda p: (0, jnp.maximum(p - half, 0))),
    ]


def attend(packed, after=()):
    rows, columns = packed.shape
    images, pairs = rows // PAD, columns // (6 * HEAD)
    return run_kernel(
        attend_kernel,
        [packed],
        after,
        grid=(pairs,),
        in_specs=[pl.BlockSpec((rows, 6 * HEAD), lambda p: (0, p))],
        out_specs=halves_specs(rows, 2 * HEAD, pairs)
        + [pl.BlockSpec((1, images, 2, PAD, PAD), lambda p: (p, 0, 0, 0, 0))],
        out_shape=[jax.ShapeDtypeStruct((rows, columns // 6), BF16)] * 2
        + [jax.ShapeDtypeStruct((pairs, images, 2, PAD, PAD), BF16)],
        scratch_shapes=[pltpu.VMEM((rows, 2 * HEAD), BF16)],
        compiler_params=pltpu.CompilerParams(vmem_limit_bytes=32 * 2**20),
        cost_estimate=pl.CostEstimate(flops=3 * 10**9, bytes_accessed=12 * 2**20, transcendentals=0),
    )


def attend_back_kernel(packed_ref, probs_ref, own_grad, far_grad, own_ref, far_ref, staged_ref):
    images = packed_ref.shape[0] // PAD
    first_half = pl.program_id(0) < pl.num_programs(0) // 2
    for image in range(images):
        rows = slice(image * PAD, (image + 1) * PAD)
        blocks = [packed_ref[rows, 128 * j : 128 * (j + 1)].astype(F32) for j in range(3)]
        queries, key_rows, values, low = split_pair(*blocks)
        values_low = values.astype(BF16)
        upstream = jnp.where(first_half, own_grad[rows].astype(F32), far_grad[rows].astype(F32))
        query_grad = key_grad = value_grad = 0.0
        for head in range(2):
            chosen = low if head == 0 else jnp.logical_not(low)
            up = jnp.where(chosen, upstream, 0.0).astype(BF16)
            query_head = jnp.where(chosen, queries * HEAD**-0.5, 0.0).astype(BF16)
            key_head = jnp.where(chosen, key_rows * HEAD**-0.5, 0.0).astype(BF16)
            probs = probs_ref[0, image, head]
            value_grad += matmul_left(probs, up)
            prob_grad = matmul_right(up, values_low)
            wide = probs.astype(F32)
            weighted = wide * prob_grad
            score_grad = (
                weighted - wide * jnp.sum(weighted, axis=1, keepdims=True)
            ).astype(BF16)
            query_grad += matmul(score_grad, key_head)
            key_grad += matmul_left(score_grad, query_head)
        key_turned = pltpu.roll(key_grad, HEAD, 1)
        staged_ref[rows, 0:128] = jnp.where(low, query_grad, key_turned).astype(BF16)
        staged_ref[rows, 128:256] = jnp.where(low, value_grad, query_grad).astype(BF16)
        staged_ref[rows, 256:384] = jnp.where(low, key_turned, value_grad).astype(BF16)
    to_half(staged_ref, own_ref, far_ref)


def attend_back(packed, probs, own_grad, far_grad, after=()):
    rows, columns = packed.shape
    images, pairs = rows // PAD, columns // (6 * HEAD)
    return run_kernel(
        attend_back_kernel,
        [packed, probs, own_grad, far_grad],
        after,
        grid=(pairs,),
        in_specs=[
            pl.BlockSpec((rows, 6 * HEAD), lambda p: (0, p)),
            pl.BlockSpec((1, images, 2, PAD, PAD), lambda p: (p, 0, 0, 0, 0)),
        ]
        + halves_specs(rows, 2 * HEAD, pairs),
        out_specs=halves_specs(rows, 6 * HEAD, pairs),
        out_shape=[jax.ShapeDtypeStruct((rows, columns // 2), BF16)] * 2,
        scratch_shapes=[pltpu.VMEM((rows, 6 * HEAD), BF16)],
        compiler_params=pltpu.CompilerParams(vmem_limit_bytes=32 * 2**20),
        cost_estimate=pl.CostEstimate(flops=8 * 10**9, bytes_accessed=16 * 2**20, transcendentals=0),
    )


def normalize(stream, gain_row, shift_row):
    row_mean = jnp.mean(stream, axis=1, keepdims=True)
    centred = stream - row_mean
    inverse = lax.rsqrt(jnp.mean(centred * centred, axis=1, keepdims=True) + EPSILON)
    unit_rows = centred * inverse
    return unit_rows, inverse, (unit_rows * gain_row + shift_row).astype(BF16)


def normalize_back(upstream, unit_rows, inverse, gain_row):
    scaled = upstream * gain_row
    first = jnp.mean(scaled, axis=1, keepdims=True)
    second = jnp.mean(scaled * unit_rows, axis=1, keepdims=True)
    return (
        inverse * (scaled - first - unit_rows * second),
        jnp.sum(upstream * unit_rows, axis=0, keepdims=True),
        jnp.sum(upstream, axis=0, keepdims=True),
    )


def side(first, second, axis):
    return jnp.concatenate([first[...], second[...]], axis=axis)


def whole_spec(values):
    return pl.BlockSpec(values.shape, lambda i: (0,) * values.ndim)


def row_spec(values, steps):
    return pl.BlockSpec((values.shape[0] // steps, values.shape[1]), lambda i: (i, 0))


def kernel_params(flops, moved):
    return {
        "compiler_params": pltpu.CompilerParams(vmem_limit_bytes=24 * 2**20),
        "cost_estimate": pl.CostEstimate(flops=flops, bytes_accessed=moved, transcendentals=0),
    }


def pad_images(col_ref, block_ref, arrived_ref, out_ref, own_wide, arrived_wide):
    half, width = arrived_ref.shape
    images = half // SEQ
    own_wide[: 2 * half] = block_ref[...].astype(F32)
    arrived_wide[:half] = arrived_ref[...].astype(F32)
    real = lax.broadcasted_iota(jnp.int32, (PAD, width), 0) < SEQ
    for image in range(images):
        rows = slice(image * PAD, (image + 1) * PAD)
        source = image * SEQ
        out_ref[rows, width:] = jnp.where(real, arrived_wide[source : source + PAD], 0.0).astype(BF16)
        for place in range(2):

            @pl.when(col_ref[0] == place)
            def _():
                begin = place * half + source
                out_ref[rows, :width] = jnp.where(real, own_wide[begin : begin + PAD], 0.0).astype(BF16)


def pad_scratch(half, width):
    extra = -(2 * half) % 8 + 16
    return [pltpu.VMEM((2 * half + extra, width), F32), pltpu.VMEM((half + 16 - half % 8, width), F32)]


def take_kernel(col_ref, block_ref, arrived_ref, out_ref, sum_ref, own_wide, arrived_wide):
    pad_images(col_ref, block_ref, arrived_ref, out_ref, own_wide, arrived_wide)
    sum_ref[...] = jnp.sum(out_ref[...].astype(F32), axis=0, keepdims=True)


def take_images(col, block, arrived, after=()):
    half, width = arrived.shape
    rows = half // SEQ * PAD
    return run_kernel(
        take_kernel,
        [col, block, arrived],
        after,
        grid=(1,),
        in_specs=[pl.BlockSpec(memory_space=pltpu.SMEM), whole_spec(block), whole_spec(arrived)],
        out_specs=[
            pl.BlockSpec((rows, 2 * width), lambda i: (0, 0)),
            pl.BlockSpec((1, 2 * width), lambda i: (0, 0)),
        ],
        out_shape=[
            jax.ShapeDtypeStruct((rows, 2 * width), BF16),
            jax.ShapeDtypeStruct((1, 2 * width), F32),
        ],
        scratch_shapes=pad_scratch(half, width),
        **kernel_params(10**6, 10 * half * width),
    )


def qkv_kernel(
    col_ref, block_ref, arrived_ref, vectors_ref, bias_ref, own, own_far, far, far_far,
    stream_ref, packed_ref, normed_ref, own_wide, arrived_wide,
):
    step, depth = packed_ref.shape[0], own.shape[0]

    @pl.when(pl.program_id(0) == 0)
    def _():
        pad_images(col_ref, block_ref, arrived_ref, stream_ref, own_wide, arrived_wide)

    begin = pl.multiple_of(pl.program_id(0) * step, 16)
    stream = stream_ref[pl.ds(begin, step)].astype(F32)
    normed = normalize(stream, vectors_ref[0:1], vectors_ref[1:2])[2]
    normed_ref[...] = normed
    columns = own.shape[1]
    packed = matmul(normed, side(own, far, 0)) + bias_ref[:, :columns]
    packed_ref[:, :columns] = packed.astype(BF16)
    packed = matmul(normed, side(own_far, far_far, 0)) + bias_ref[:, columns:]
    packed_ref[:, columns:] = packed.astype(BF16)


def widen_qkv(col, block, arrived, vectors, bias, blocks, after=()):
    half, width = arrived.shape
    rows, columns = half // SEQ * PAD, bias.shape[1]
    steps = 2
    stream = jax.ShapeDtypeStruct((rows, 2 * width), BF16)
    packed = jax.ShapeDtypeStruct((rows, columns), BF16)
    others = [block, arrived, vectors, bias, *blocks]
    return run_kernel(
        qkv_kernel,
        [col, *others],
        after,
        grid=(steps,),
        in_specs=[pl.BlockSpec(memory_space=pltpu.SMEM)] + [whole_spec(o) for o in others],
        out_specs=[whole_spec(stream), row_spec(packed, steps), row_spec(stream, steps)],
        out_shape=[stream, packed, stream],
        scratch_shapes=pad_scratch(half, width),
        **kernel_params(4 * rows * width * columns, 8 * rows * width),
    )


def out_kernel(stream_ref, left_ref, right_ref, vectors_ref, own, own_far, far, far_far, middle_ref, normed_ref):
    attended = side(left_ref, right_ref, 1)
    branch = jnp.concatenate(
        [matmul(attended, side(own, far, 0)), matmul(attended, side(own_far, far_far, 0))], axis=1
    )
    middle = stream_ref[...].astype(F32) + branch + vectors_ref[4:5]
    middle_ref[...] = middle
    normed_ref[...] = normalize(middle, vectors_ref[2:3], vectors_ref[3:4])[2]


def narrow_out(stream, left, right, vectors, blocks, after=()):
    rows, width = stream.shape
    steps = 2
    others = [vectors, *blocks]
    return run_kernel(
        out_kernel,
        [stream, left, right, *others],
        after,
        grid=(steps,),
        in_specs=[row_spec(v, steps) for v in (stream, left, right)] + [whole_spec(o) for o in others],
        out_specs=[row_spec(stream, steps)] * 2,
        out_shape=[
            jax.ShapeDtypeStruct((rows, width), F32),
            jax.ShapeDtypeStruct((rows, width), BF16),
        ],
        **kernel_params(2 * rows * width * width, 10 * rows * width),
    )


def gelu_kernel(acts_ref, own_top, own_low, far_top, far_low, own_bias, far_bias, *outs):
    for top_ref, low_ref, bias_ref, active_ref, slope_ref in (
        (own_top, own_low, own_bias, outs[0], outs[1]),
        (far_top, far_low, far_bias, outs[2], outs[3]),
    ):
        weight = side(top_ref, low_ref, 0)
        for begin in range(0, acts_ref.shape[0], PAD):
            chunk = slice(begin, begin + PAD)
            before = matmul(acts_ref[chunk], weight) + bias_ref[...]
            bell = jnp.exp2((before * before) * -0.7213475204444817)
            size = 1.0 + (0.3275911 * 0.5**0.5) * jnp.abs(before)
            guess = pl.reciprocal(size, approx=True)
            inv = guess * (2.0 - size * guess)
            poly = -0.726576735 + inv * 0.5307027145
            poly = 0.7107068705 + inv * poly
            poly = -0.142248368 + inv * poly
            poly = (0.127414796 + inv * poly) * inv
            tail = poly * bell
            chance = jnp.where(before < 0, tail, 1.0 - tail)
            active_ref[chunk] = (before * chance).astype(BF16)
            slope_ref[chunk] = (chance + before * (bell * 0.3989422804014327)).astype(BF16)


def widen_gelu(acts, blocks, own_bias, far_bias, after=()):
    rows, depth = acts.shape
    units = own_bias.shape[1]
    tile = 256
    wide = pl.BlockSpec((depth // 2, tile), lambda j: (0, j))
    line = pl.BlockSpec((1, tile), lambda j: (0, j))
    out = pl.BlockSpec((rows, tile), lambda j: (0, j))
    return run_kernel(
        gelu_kernel,
        [acts, *blocks, own_bias, far_bias],
        after,
        grid=(units // tile,),
        in_specs=[whole_spec(acts)] + [wide] * 4 + [line] * 2,
        out_specs=[out] * 4,
        out_shape=[jax.ShapeDtypeStruct((rows, units), BF16)] * 4,
        **kernel_params(4 * rows * depth * units, 16 * rows * units),
    )


def slope_kernel(up_ref, own_left, own_right, far_left, far_right, own_slope, far_slope, *outs):
    for left_ref, right_ref, slope_ref, out_ref, sum_ref in (
        (own_left, own_right, own_slope, outs[0], outs[1]),
        (far_left, far_right, far_slope, outs[2], outs[3]),
    ):
        grad = matmul_right(up_ref[...], side(left_ref, right_ref, 1))
        low = (grad * slope_ref[...].astype(F32)).astype(BF16)
        out_ref[...] = low
        sum_ref[...] = jnp.sum(low.astype(F32), axis=0, keepdims=True)


def widen_back(upstream, blocks, own_slope, far_slope, after=()):
    rows, depth = upstream.shape
    units = own_slope.shape[1]
    tile = 256
    deep = pl.BlockSpec((tile, depth // 2), lambda j: (j, 0))
    line = pl.BlockSpec((1, tile), lambda j: (0, j))
    out = pl.BlockSpec((rows, tile), lambda j: (0, j))
    return run_kernel(
        slope_kernel,
        [upstream, *blocks, own_slope, far_slope],
        after,
        grid=(units // tile,),
        in_specs=[whole_spec(upstream)] + [deep] * 4 + [out] * 2,
        out_specs=[out, line, out, line],
        out_shape=[
            jax.ShapeDtypeStruct((rows, units), BF16),
            jax.ShapeDtypeStruct((1, units), F32),
        ]
        * 2,
        **kernel_params(4 * rows * depth * units, 8 * rows * units),
    )


def pack_kernel(*refs):
    col_refs, (qv_ref, fc1_ref, col_out, row_out) = refs[:6], refs[6:]
    for i in range(6):
        col_out[i : i + 1] = col_refs[i][...]
    low = lax.broadcasted_iota(jnp.int32, (1, 128), 1) < HEAD
    for pair in range(qv_ref.shape[1] // 256):
        first = qv_ref[:, 256 * pair : 256 * pair + 128]
        second = qv_ref[:, 256 * pair + 128 : 256 * pair + 256]
        turned = [pltpu.roll(r, HEAD, 1) for r in (first, second)]
        begin = 384 * pair
        row_out[:, begin : begin + 128] = jnp.where(low, first, 0.0)
        row_out[:, begin + 128 : begin + 256] = jnp.where(low, turned[0], turned[1])
        row_out[:, begin + 256 : begin + 384] = jnp.where(low, 0.0, second)
    packed = qv_ref.shape[1] * 3 // 2
    row_out[:, packed:] = fc1_ref[...]


def pack_vectors(col_vectors, qv_bias, fc1_bias):
    values = [v[None] for v in (*col_vectors, qv_bias, fc1_bias)]
    width = qv_bias.shape[0] * 3 // 2 + fc1_bias.shape[0]
    outs = [
        jax.ShapeDtypeStruct((6, col_vectors[0].shape[0]), F32),
        jax.ShapeDtypeStruct((1, width), F32),
    ]
    return pl.pallas_call(
        pack_kernel,
        grid=(1,),
        in_specs=[whole_spec(v) for v in values],
        out_specs=[whole_spec(o) for o in outs],
        out_shape=outs,
        **kernel_params(1000, 50000),
    )(*values)


def middle_back_kernel(
    own_grad, far_grad, middle_ref, up_ref, vectors_ref,
    own, own_far, far, far_far, out_own, out_own_far, out_far, out_far_far,
    grad_ref, low_ref, own_out, far_out, sums_ref,
):
    left, right = own_grad[...], far_grad[...]
    normed_grad = jnp.concatenate(
        [
            matmul_right(left, own[...]) + matmul_right(right, own_far[...]),
            matmul_right(left, far[...]) + matmul_right(right, far_far[...]),
        ],
        axis=1,
    )
    unit, inverse, _ = normalize(middle_ref[...], vectors_ref[2:3], vectors_ref[3:4])
    part, gain_sum, shift_sum = normalize_back(normed_grad, unit, inverse, vectors_ref[2:3])
    grad = up_ref[...].astype(F32) + part
    low = grad.astype(BF16)
    grad_ref[...] = grad
    low_ref[...] = low
    own_out[...] = matmul_right(low, side(out_own, out_own_far, 1)).astype(BF16)
    far_out[...] = matmul_right(low, side(out_far, out_far_far, 1)).astype(BF16)
    sums = jnp.concatenate(
        [gain_sum, shift_sum, jnp.sum(low.astype(F32), axis=0, keepdims=True)], axis=0
    )

    @pl.when(pl.program_id(0) == 0)
    def _():
        sums_ref[...] = sums

    @pl.when(pl.program_id(0) > 0)
    def _():
        sums_ref[...] += sums


def middle_back(own_grad, far_grad, middle, upstream, vectors, fc1_blocks, out_blocks, after=()):
    rows, width = middle.shape
    steps = 2
    rowed = [own_grad, far_grad, middle, upstream]
    others = [vectors, *fc1_blocks, *out_blocks]
    head_cols = out_blocks[0].shape[0]
    low = jax.ShapeDtypeStruct((rows, width), BF16)
    heads = jax.ShapeDtypeStruct((rows, head_cols), BF16)
    sums = jax.ShapeDtypeStruct((3, width), F32)
    return run_kernel(
        middle_back_kernel,
        [*rowed, *others],
        after,
        grid=(steps,),
        in_specs=[row_spec(r, steps) for r in rowed] + [whole_spec(o) for o in others],
        out_specs=[row_spec(v, steps) for v in (middle, low, heads, heads)] + [whole_spec(sums)],
        out_shape=[jax.ShapeDtypeStruct((rows, width), F32), low, heads, heads, sums],
        **kernel_params(4 * rows * width * own_grad.shape[1], 24 * rows * width),
    )


def cut_images(index, images, values, wide_ref):
    for step in range(wide_ref.shape[0] // SEQ // images):

        @pl.when(index == step)
        def _():
            for image in range(images):
                begin = (step * images + image) * SEQ
                wide_ref[begin : begin + SEQ] = values[image * PAD : image * PAD + SEQ]


def input_back_kernel(
    own_grad, far_grad, stream_ref, middle_grad_ref, vectors_ref,
    own, own_far, far, far_far, keep_ref, give_ref, sums_ref, packed_sums_ref, give_wide,
):
    step = pl.program_id(0)
    images = stream_ref.shape[0] // PAD
    packed_grad = side(own_grad, far_grad, 1)
    normed_grad = jnp.concatenate(
        [
            matmul_right(packed_grad, side(own, own_far, 1)),
            matmul_right(packed_grad, side(far, far_far, 1)),
        ],
        axis=1,
    )
    unit, inverse, _ = normalize(stream_ref[...].astype(F32), vectors_ref[0:1], vectors_ref[1:2])
    part, gain_sum, shift_sum = normalize_back(normed_grad, unit, inverse, vectors_ref[0:1])
    grad = middle_grad_ref[...] + part
    width = keep_ref.shape[1]
    cut_images(step, images, grad[:, :width], keep_ref)
    cut_images(step, images, grad[:, width:], give_wide)
    sums = jnp.concatenate([gain_sum, shift_sum], axis=0)
    packed_sums = jnp.sum(packed_grad.astype(F32), axis=0, keepdims=True)

    @pl.when(step == 0)
    def _():
        sums_ref[...] = sums
        packed_sums_ref[...] = packed_sums

    @pl.when(step > 0)
    def _():
        sums_ref[...] += sums
        packed_sums_ref[...] += packed_sums

    @pl.when(step == pl.num_programs(0) - 1)
    def _():
        give_ref[...] = give_wide[...].astype(BF16)


def input_back(own_grad, far_grad, stream, middle_grad, vectors, blocks, after=()):
    rows, width = stream.shape
    steps = 2
    half = rows // PAD * SEQ
    rowed = [own_grad, far_grad, stream, middle_grad]
    others = [vectors, *blocks]
    outs = [
        jax.ShapeDtypeStruct((half, width // 2), F32),
        jax.ShapeDtypeStruct((half, width // 2), BF16),
        jax.ShapeDtypeStruct((2, width), F32),
        jax.ShapeDtypeStruct((1, 2 * own_grad.shape[1]), F32),
    ]
    return run_kernel(
        input_back_kernel,
        [*rowed, *others],
        after,
        grid=(steps,),
        in_specs=[row_spec(r, steps) for r in rowed] + [whole_spec(o) for o in others],
        out_specs=[whole_spec(o) for o in outs],
        out_shape=outs,
        scratch_shapes=[pltpu.VMEM((half, width // 2), F32)],
        **kernel_params(4 * rows * width * own_grad.shape[1], 20 * rows * width),
    )


def result_kernel(
    own_acts, far_acts, middle_ref, vectors_ref, own, own_far, far, far_far,
    keep_ref, give_ref, keep_wide, give_wide,
):
    step = pl.program_id(0)
    images = middle_ref.shape[0] // PAD
    width = keep_ref.shape[1]
    left, right = own_acts[...], far_acts[...]
    for weights, columns, wide_ref in (
        ((own, far), slice(0, width), keep_wide),
        ((own_far, far_far), slice(width, 2 * width), give_wide),
    ):
        branch = matmul(left, weights[0][...]) + matmul(right, weights[1][...])
        total = middle_ref[:, columns] + branch + vectors_ref[5:6, columns]
        cut_images(step, images, total, wide_ref)

    @pl.when(step == pl.num_programs(0) - 1)
    def _():
        keep_ref[...] = keep_wide[...].astype(BF16)
        give_ref[...] = give_wide[...].astype(BF16)


def narrow_result(own_acts, far_acts, middle, vectors, blocks, after=()):
    rows, width = middle.shape
    steps = 2
    half = rows // PAD * SEQ
    rowed = [own_acts, far_acts, middle]
    others = [vectors, *blocks]
    out = jax.ShapeDtypeStruct((half, width // 2), BF16)
    return run_kernel(
        result_kernel,
        [*rowed, *others],
        after,
        grid=(steps,),
        in_specs=[row_spec(r, steps) for r in rowed] + [whole_spec(o) for o in others],
        out_specs=[whole_spec(out)] * 2,
        out_shape=[out] * 2,
        scratch_shapes=[pltpu.VMEM((half, width // 2), F32)] * 2,
        **kernel_params(4 * rows * width * own_acts.shape[1], 12 * rows * width),
    )


def weight_grad_kernel(split_dim, left_own, left_other, right_own, right_other, keep_ref, send_ref):
    total = matmul_left(left_own[...], right_own[...])
    total += matmul_left(left_other[...], right_other[...])
    half = total.shape[split_dim] // 2
    if split_dim == 0:
        keep_ref[:half] = total[:half].astype(BF16)
        send_ref[:half] = total[half:].astype(BF16)
        extra = keep_ref.shape[0] - half
        if extra:
            keep_ref[half:] = jnp.zeros((extra, total.shape[1]), BF16)
            send_ref[half:] = jnp.zeros((extra, total.shape[1]), BF16)
    else:
        keep_ref[...] = total[:, :half].astype(BF16)
        send_ref[...] = total[:, half:].astype(BF16)


def weight_grad(left_own, left_other, right_own, right_other, split_dim, tile, extra=0, more=0, after=()):
    rows, height = left_own.shape
    width = right_own.shape[1]
    if split_dim == 0:
        left = pl.BlockSpec((rows, height), lambda j: (0, 0))
        right = pl.BlockSpec((rows, tile), lambda j: (0, j))
        out = pl.BlockSpec((height // 2 + extra, tile), lambda j: (0, j))
        shape, steps = (height // 2 + extra, width + more), width // tile
    else:
        left = pl.BlockSpec((rows, tile), lambda j: (0, j))
        right = pl.BlockSpec((rows, width), lambda j: (0, 0))
        out = pl.BlockSpec((tile, width // 2), lambda j: (j, 0))
        shape, steps = (height, width // 2), height // tile
    return run_kernel(
        partial(weight_grad_kernel, split_dim),
        [left_own, left_other, right_own, right_other],
        after,
        grid=(steps,),
        in_specs=[left, left, right, right],
        out_specs=[out, out],
        out_shape=[jax.ShapeDtypeStruct(shape, BF16)] * 2,
        **kernel_params(
            4 * rows * height * width, 4 * rows * (height + width) + 3 * height * width
        ),
    )


def out_grad_kernel(left_own, left_other, right_own, right_other, keep_in, send_in, keep_ref, send_ref):
    total = matmul_left(left_own[...], right_own[...])
    total += matmul_left(left_other[...], right_other[...])
    half = total.shape[1] // 2
    keep_ref[...] = total[:, :half].astype(BF16)
    send_ref[...] = total[:, half:].astype(BF16)


def out_weight_grad(left_own, left_other, right_own, right_other, keep, send, after=()):
    rows, height = left_own.shape
    values = [left_own, left_other, right_own, right_other]
    place = keep.shape[1] // height - 1
    out = pl.BlockSpec((height, height), lambda i: (0, place))
    unread = pl.BlockSpec(memory_space=pl.ANY)
    return run_kernel(
        out_grad_kernel,
        [*values, keep, send],
        after,
        grid=(1,),
        in_specs=[whole_spec(v) for v in values] + [unread, unread],
        out_specs=[out, out],
        out_shape=[jax.ShapeDtypeStruct(v.shape, v.dtype) for v in (keep, send)],
        input_output_aliases={4: 0, 5: 1},
        **kernel_params(8 * rows * height * height, 4 * rows * height),
    )


def together(*values):
    return lax.optimization_barrier(values)


def move(values, distance):
    size = lax.axis_size("dp")
    return lax.ppermute(values, "dp", [(i, i ^ distance) for i in range(size)])


def bit_of(distance):
    return (lax.axis_index("dp") // distance) % 2


def cut(values, index, parts):
    size = values.shape[0] // parts
    return lax.dynamic_slice_in_dim(values, index * size, size, 0)


def quarter(block):
    return cut(block, lax.axis_index("dp") % 4, 4)


def spread(piece):
    return piece, move(piece, 1), move(piece, 2), move(piece, 3)


def assemble(pieces):
    low, high = bit_of(1) == 1, bit_of(2) == 1
    first = [jnp.where(low, pieces[j ^ 1], pieces[j]) for j in range(4)]
    return jnp.concatenate([jnp.where(high, first[j ^ 2], first[j]) for j in range(4)], axis=0)


def in_order(bit, mine, other):
    return jnp.where(
        bit == 0,
        jnp.concatenate([mine, other], axis=0),
        jnp.concatenate([other, mine], axis=0),
    )


def added(first, second):
    return (first.astype(F32) + second.astype(F32)).astype(BF16)


class GradSum:
    def __init__(self, keep, send):
        self.keep, self.send = keep, send
        self.half = keep.shape[0] // 2
        self.bit = bit_of(1)
        size = lax.axis_size("dp")
        self.middle = [2**k for k in range(1, size.bit_length() - 2)]
        self.last = size // 2

    def start_first(self):
        keep_b, send_b = self.keep[self.half :], self.send[self.half :]
        out_a = swap(self.send[: self.half], "col")
        other = jnp.concatenate([cut(keep_b, 1 - self.bit, 2), cut(send_b, 1 - self.bit, 2)], axis=0)
        return out_a, move(other, 1)

    def start_second(self, arrived):
        from_col, from_dp = arrived
        keep_b, send_b = self.keep[self.half :], self.send[self.half :]
        quarter_rows = self.half // 2
        self.lower = added(cut(keep_b, self.bit, 2), from_dp[:quarter_rows])
        lower_send = added(cut(send_b, self.bit, 2), from_dp[quarter_rows:])
        keep_a = self.keep[: self.half]
        self.upper = added(cut(keep_a, self.bit, 2), cut(from_col, self.bit, 2))
        upper_send = added(cut(keep_a, 1 - self.bit, 2), cut(from_col, 1 - self.bit, 2))
        return swap(lower_send, "col"), move(upper_send, 1)

    def end_second(self, arrived):
        from_col, from_dp = arrived
        self.held = jnp.concatenate(
            [added(self.upper, from_dp), added(self.lower, from_col)], axis=0
        )

    def start_halving(self, distance):
        bit = bit_of(distance)
        self.kept = cut(self.held, bit, 2)
        return move(cut(self.held, 1 - bit, 2), distance)

    def end_halving(self, arrived):
        self.held = added(self.kept, arrived)

    def start_last(self):
        return move(self.held, self.last)

    def end_last(self, arrived):
        self.held = added(self.held, arrived)

    def start_doubling(self, distance):
        return move(self.held, distance)

    def end_doubling(self, distance, arrived):
        self.held = in_order(bit_of(distance), self.held, arrived)

    def start_whole(self):
        return move(self.held, 1)

    def end_whole(self, arrived):
        half = self.half // 2
        upper = in_order(self.bit, self.held[:half], arrived[:half])
        lower = in_order(self.bit, self.held[half:], arrived[half:])
        return jnp.concatenate([upper, lower], axis=0)


def per_device(
    tokens,
    cotangent,
    ln1_gain,
    ln1_bias,
    qkv_weight,
    qv_bias,
    out_weight,
    out_bias,
    ln2_gain,
    ln2_bias,
    fc1_weight,
    fc1_bias,
    fc2_weight,
    fc2_bias,
):
    col = lax.axis_index("col")
    col_scalar = jnp.full((1,), col, jnp.int32)
    half = tokens.shape[0] // 2
    qkv_cols = qkv_weight.shape[1]
    units = fc1_weight.shape[1]

    def give_half(block):
        return lax.dynamic_slice_in_dim(block, (1 - col) * half, half, 0)

    qkv_piece = swap(quarter(qkv_weight), "col")
    col_rows, row_values = pack_vectors(
        (ln1_gain, ln1_bias, ln2_gain, ln2_bias, out_bias, fc2_bias), qv_bias, fc1_bias
    )
    col_other = swap(col_rows, "col")
    row_other = swap(row_values, "row")
    qkv_swap = swap(qkv_weight, "row")
    fc1_out_give = jnp.concatenate([quarter(fc1_weight), quarter(out_weight)], axis=1)
    qkv_piece, fc1_out_give, token_give, fc2_give, cot_give = together(
        qkv_piece, fc1_out_give, give_half(tokens), quarter(fc2_weight), give_half(cotangent)
    )
    qkv_pieces = spread(qkv_piece)
    token_other = swap(token_give, "col")
    vectors = jnp.concatenate([col_rows, col_other], axis=1)
    qkv_bias = jnp.concatenate([row_values[:, :qkv_cols], row_other[:, :qkv_cols]], axis=1)

    qkv_pieces, token_other, fc1_out_give, vectors, qkv_bias = together(
        qkv_pieces, token_other, fc1_out_give, vectors, qkv_bias
    )
    qkv_far = assemble(qkv_pieces)
    qkv_far_swap = swap(qkv_far, "row")
    fc1_out_piece = swap(fc1_out_give, "col")
    qkv_blocks = [qkv_weight, qkv_swap, qkv_far, qkv_far_swap]
    stream, packed, normed1, end = widen_qkv(
        col_scalar, tokens, token_other, vectors, qkv_bias, qkv_blocks
    )

    end, fc1_out_piece, fc2_give = together(end, fc1_out_piece, fc2_give)
    fc1_out_pieces = spread(fc1_out_piece)
    fc2_piece = swap(fc2_give, "col")
    out_swap = swap(out_weight, "row")
    attended_mine, attended_away, probs, end = attend(packed, end)

    end, fc1_out_pieces, fc2_piece, out_swap, cot_give = together(
        end, fc1_out_pieces, fc2_piece, out_swap, cot_give
    )
    out_far = assemble([m[:, units:] for m in fc1_out_pieces])
    out_far_swap = swap(out_far, "row")
    fc2_pieces = spread(fc2_piece)
    cot_other = swap(cot_give, "col")
    fc1_far = assemble([m[:, :units] for m in fc1_out_pieces])
    fc1_far_swap = swap(fc1_far, "row")
    fc1_swap = swap(fc1_weight, "row")
    out_blocks = [out_weight, out_far, out_swap, out_far_swap]
    middle, normed2, end = narrow_out(
        stream, attended_mine, attended_away, vectors, out_blocks, end
    )

    end, fc1_swap, fc1_far_swap, fc2_swap = together(end, fc1_swap, fc1_far_swap, fc2_weight)
    fc2_swap = swap(fc2_swap, "row")
    fc1_blocks = [fc1_weight, fc1_far, fc1_swap, fc1_far_swap]
    active, slope, active_far, slope_far, end = widen_gelu(
        normed2, fc1_blocks, row_values[:, qkv_cols:], row_other[:, qkv_cols:], end
    )

    end, fc2_pieces, fc2_swap, cot_other = together(end, fc2_pieces, fc2_swap, cot_other)
    fc2_away = assemble(fc2_pieces)
    fc2_away_swap = swap(fc2_away, "row")
    active_other = swap(active_far, "row")
    upstream, fc2_bgrad, end = take_images(col_scalar, cotangent, cot_other, end)
    upstream_other = swap(upstream, "row")
    fc2_blocks = [fc2_weight, fc2_away, fc2_swap, fc2_away_swap]
    before_grad, before_sum, before_far, before_far_sum, end = widen_back(
        upstream, fc2_blocks, slope, slope_far, end
    )

    end, active_other, upstream_other = together(end, active_other, upstream_other)
    before_other = swap(before_far, "row")
    normed2_other = swap(normed2, "row")
    attended_other = swap(attended_away, "row")
    normed1_other = swap(normed1, "row")
    fc2_keep, fc2_send, end = weight_grad(
        active, active_other, upstream, upstream_other, 1, 256, after=end
    )

    sum2 = GradSum(fc2_keep, fc2_send)
    flying2 = sum2.start_first()
    middle_grad, middle_low, attended_grad, attended_grad_far, middle_sums, end = middle_back(
        before_grad,
        before_far,
        middle,
        upstream,
        vectors,
        [fc1_weight, fc1_swap, fc1_far, fc1_far_swap],
        out_blocks,
        end,
    )

    end, before_other, normed2_other, attended_other, normed1_other = together(
        end, before_other, normed2_other, attended_other, normed1_other
    )
    middle_other = swap(middle_low, "row")
    fc1_keep, fc1_send, end = weight_grad(
        normed2, normed2_other, before_grad, before_other, 0, 384, more=384, after=end
    )

    end, flying2, middle_other = together(end, flying2, middle_other)
    flying2 = sum2.start_second(flying2)
    fc1_keep, fc1_send, end = out_weight_grad(
        attended_mine, attended_other, middle_low, middle_other, fc1_keep, fc1_send, end
    )

    end, flying2 = together(end, flying2)
    sum1 = GradSum(fc1_keep, fc1_send)
    flying1 = sum1.start_first()
    sum2.end_second(flying2)
    middle_steps = sum2.middle
    for distance in middle_steps[:-1]:
        sum2.end_halving(sum2.start_halving(distance))
    flying2 = sum2.start_halving(middle_steps[-1])
    packed_grad, packed_grad_far, end = attend_back(
        packed, probs, attended_grad, attended_grad_far, end
    )

    end, flying1, flying2 = together(end, flying1, flying2)
    packed_other = swap(packed_grad_far, "row")
    flying1 = sum1.start_second(flying1)
    sum2.end_halving(flying2)
    flying2 = sum2.start_last()
    input_own, input_give, input_sums, packed_sums, end = input_back(
        packed_grad, packed_grad_far, stream, middle_grad, vectors, qkv_blocks, end
    )

    end, flying1, packed_other = together(end, flying1, packed_other)
    sum1.end_second(flying1)
    for distance in middle_steps[:-1]:
        sum1.end_halving(sum1.start_halving(distance))
    flying1 = sum1.start_halving(middle_steps[-1])
    kinds = packed_sums.reshape(-1, 3, HEAD)
    width = input_sums.shape[1]
    qv_grad = jnp.stack([kinds[:, 0], kinds[:, 2]], axis=1).reshape(2, -1, width)
    fc1_bgrad = jnp.stack([before_sum.reshape(-1, width), before_far_sum.reshape(-1, width)])
    by_row = jnp.concatenate([qv_grad, fc1_bgrad], axis=1)
    by_col = jnp.concatenate([input_sums, middle_sums, fc2_bgrad], axis=0)
    row_count = by_row.shape[1]
    small_other = swap(jnp.concatenate([by_row[1], by_col], axis=0), "row")
    qkv_keep, qkv_send, end = weight_grad(
        normed1, normed1_other, packed_grad, packed_other, 0, 384, EXTRA, after=end
    )

    end, flying1, flying2, small_other = together(end, flying1, flying2, small_other)
    by_row = (by_row[0] + small_other[:row_count]).reshape(-1, qkv_cols)
    by_col = by_col + small_other[row_count:]
    begin = qkv_keep.shape[0] - EXTRA
    both_cols = [
        jnp.concatenate([by_row, half_cols.reshape(-1, qkv_cols)], axis=0).astype(BF16)
        for half_cols in jnp.split(by_col, 2, axis=1)
    ]
    qkv_keep = lax.dynamic_update_slice(qkv_keep, both_cols[0], (begin, 0))
    qkv_send = lax.dynamic_update_slice(qkv_send, both_cols[1], (begin, 0))

    sum0 = GradSum(qkv_keep, qkv_send)
    flying0 = sum0.start_first()
    sum1.end_halving(flying1)
    flying1 = sum1.start_last()
    sum2.end_last(flying2)
    flying2 = sum2.start_doubling(middle_steps[-1])
    result_own, result_give, end = narrow_result(
        active, active_far, middle, vectors, fc2_blocks, end
    )

    flying0, flying1, flying2, end, input_give = together(
        flying0, flying1, flying2, end, input_give
    )
    flying0 = sum0.start_second(flying0)
    sum1.end_last(flying1)
    flying1 = sum1.start_doubling(middle_steps[-1])
    sum2.end_doubling(middle_steps[-1], flying2)
    for distance in reversed(middle_steps[:-1]):
        sum2.end_doubling(distance, sum2.start_doubling(distance))
    flying2 = sum2.start_whole()
    input_other = swap(input_give, "col")

    result_give, input_other, flying0, flying1, flying2 = together(
        result_give, input_other, flying0, flying1, flying2
    )
    sum0.end_second(flying0)
    for distance in middle_steps[:-1]:
        sum0.end_halving(sum0.start_halving(distance))
    flying0 = sum0.start_halving(middle_steps[-1])
    sum1.end_doubling(middle_steps[-1], flying1)
    for distance in reversed(middle_steps[:-1]):
        sum1.end_doubling(distance, sum1.start_doubling(distance))
    flying1 = sum1.start_whole()
    result_other = swap(result_give, "col")
    input_grad = in_order(col, input_own, input_other.astype(F32))

    flying0, result_other, input_grad = together(flying0, result_other, input_grad)
    sum0.end_halving(flying0)
    flying0 = sum0.start_last()
    fc2_wgrad = sum2.end_whole(flying2).astype(F32)
    result = in_order(col, result_own, result_other)

    flying0, flying1, result, fc2_wgrad = together(flying0, flying1, result, fc2_wgrad)
    sum0.end_last(flying0)
    flying0 = sum0.start_doubling(middle_steps[-1])
    fc1_out_grad = sum1.end_whole(flying1)

    flying0, fc1_out_grad = together(flying0, fc1_out_grad)
    sum0.end_doubling(middle_steps[-1], flying0)
    for distance in reversed(middle_steps[:-1]):
        sum0.end_doubling(distance, sum0.start_doubling(distance))
    flying0 = sum0.start_whole()
    qkv_whole = sum0.end_whole(flying0)
    qv_size = qv_bias.shape[0]
    rows_each = by_row.shape[0]
    vector_rows = qkv_whole[begin : begin + 2 * rows_each].astype(F32)
    by_row = vector_rows[:rows_each].reshape(-1)
    by_col = vector_rows[rows_each:].reshape(6, -1)
    return (
        result,
        input_grad,
        by_col[0],
        by_col[1],
        qkv_whole[:begin].astype(F32),
        by_row[:qv_size],
        fc1_out_grad[:, units:].astype(F32),
        by_col[4],
        by_col[2],
        by_col[3],
        fc1_out_grad[:, :units].astype(F32),
        by_row[qv_size:],
        fc2_wgrad,
        by_col[5],
    )


def solution(mesh):
    stream = P(("dp", "row"), "col")
    by_col, by_row = P("col"), P("row")
    wide, deep = P("col", "row"), P("row", "col")
    in_specs = (
        stream, stream, by_col, by_col, wide, by_row, deep, by_col,
        by_col, by_col, wide, by_row, deep, by_col,
    )
    return jax.shard_map(
        per_device, mesh=mesh, in_specs=in_specs, out_specs=in_specs, check_vma=False
    )
```

```python
from functools import partial

import jax
import jax.numpy as jnp
from jax import lax
from jax.experimental import pallas as pl
from jax.experimental.pallas import tpu as pltpu
from jax.sharding import PartitionSpec as P

HEAD = 64
SEQ = 197
PAD = 208
EXTRA = 32
EPSILON = 1e-06
LEFT_INNER = (((0,), (0,)), ((), ()))
RIGHT_INNER = (((1,), (1,)), ((), ()))
BF16 = jnp.bfloat16
F32 = jnp.float32


def swap(values, axis):
    return lax.ppermute(values, axis, [(0, 1), (1, 0)])


def matmul(left, right):
    return jnp.dot(left, right, preferred_element_type=F32)


def matmul_left(left, right):
    return lax.dot_general(left, right, LEFT_INNER, preferred_element_type=F32)


def matmul_right(left, right):
    return lax.dot_general(left, right, RIGHT_INNER, preferred_element_type=F32)


def split_pair(c0, c1, c2):
    low = lax.broadcasted_iota(jnp.int32, c0.shape, 1) < HEAD
    queries = jnp.where(low, c0, c1)
    key_rows = pltpu.roll(jnp.where(low, c2, c0), HEAD, 1)
    values = jnp.where(low, c1, c2)
    return queries, key_rows, values, low


def to_half(staged_ref, own_ref, far_ref):
    first_half = pl.program_id(0) < pl.num_programs(0) // 2

    @pl.when(first_half)
    def _():
        own_ref[...] = staged_ref[...]

    @pl.when(jnp.logical_not(first_half))
    def _():
        far_ref[...] = staged_ref[...]


def run_kernel(kernel, values, after, in_specs, out_specs, out_shape, **settings):
    values, after = list(values), jax.tree.leaves(after)
    count, skip = len(values), len(values) + len(after)
    outs = len(out_shape)

    def body(*refs):
        end_ref = refs[skip + outs]
        end_ref[...] = jnp.zeros_like(end_ref)
        kernel(*refs[:count], *refs[skip : skip + outs], *refs[skip + outs + 1 :])

    unread = [pl.BlockSpec(memory_space=pl.ANY)] * len(after)
    end = jax.ShapeDtypeStruct((8, 128), F32)
    return pl.pallas_call(
        body,
        in_specs=list(in_specs) + unread,
        out_specs=list(out_specs) + [whole_spec(end)],
        out_shape=list(out_shape) + [end],
        **settings,
    )(*values, *after)


def attend_kernel(packed_ref, own_ref, far_ref, probs_ref, staged_ref):
    images = packed_ref.shape[0] // PAD
    for image in range(images):
        rows = slice(image * PAD, (image + 1) * PAD)
        blocks = [packed_ref[rows, 128 * j : 128 * (j + 1)].astype(F32) for j in range(3)]
        queries, key_rows, values, low = split_pair(*blocks)
        keys_low = key_rows.astype(BF16)
        values_low = values.astype(BF16)
        outs = []
        for head in range(2):
            chosen = low if head == 0 else jnp.logical_not(low)
            masked = jnp.where(chosen, queries * HEAD**-0.5, 0.0).astype(BF16)
            scores = matmul_right(masked, keys_low)
            real = lax.broadcasted_iota(jnp.int32, scores.shape, 1) < SEQ
            scores = jnp.where(real, scores, -1e30)
            raised = jnp.exp(scores - jnp.max(scores, axis=1, keepdims=True))
            probs = (raised * (1.0 / jnp.sum(raised, axis=1, keepdims=True))).astype(BF16)
            probs_ref[0, image, head] = probs
            outs.append(matmul(probs, values_low))
        staged_ref[rows] = jnp.where(low, outs[0], outs[1]).astype(BF16)
    to_half(staged_ref, own_ref, far_ref)


def halves_specs(rows, width, steps):
    half = steps // 2
    return [
        pl.BlockSpec((rows, width), lambda p: (0, jnp.minimum(p, half - 1))),
        pl.BlockSpec((rows, width), lambda p: (0, jnp.maximum(p - half, 0))),
    ]


def attend(packed, after=()):
    rows, columns = packed.shape
    images, pairs = rows // PAD, columns // (6 * HEAD)
    return run_kernel(
        attend_kernel,
        [packed],
        after,
        grid=(pairs,),
        in_specs=[pl.BlockSpec((rows, 6 * HEAD), lambda p: (0, p))],
        out_specs=halves_specs(rows, 2 * HEAD, pairs)
        + [pl.BlockSpec((1, images, 2, PAD, PAD), lambda p: (p, 0, 0, 0, 0))],
        out_shape=[jax.ShapeDtypeStruct((rows, columns // 6), BF16)] * 2
        + [pltpu.HBM((pairs, images, 2, PAD, PAD), BF16)],
        scratch_shapes=[pltpu.VMEM((rows, 2 * HEAD), BF16)],
        compiler_params=pltpu.CompilerParams(vmem_limit_bytes=32 * 2**20),
        cost_estimate=pl.CostEstimate(flops=3 * 10**9, bytes_accessed=12 * 2**20, transcendentals=0),
    )


def attend_back_kernel(packed_ref, probs_ref, own_grad, far_grad, own_ref, far_ref, staged_ref):
    images = packed_ref.shape[0] // PAD
    first_half = pl.program_id(0) < pl.num_programs(0) // 2
    for image in range(images):
        rows = slice(image * PAD, (image + 1) * PAD)
        blocks = [packed_ref[rows, 128 * j : 128 * (j + 1)].astype(F32) for j in range(3)]
        queries, key_rows, values, low = split_pair(*blocks)
        values_low = values.astype(BF16)
        upstream = jnp.where(first_half, own_grad[rows].astype(F32), far_grad[rows].astype(F32))
        query_grad = key_grad = value_grad = 0.0
        for head in range(2):
            chosen = low if head == 0 else jnp.logical_not(low)
            up = jnp.where(chosen, upstream, 0.0).astype(BF16)
            query_head = jnp.where(chosen, queries * HEAD**-0.5, 0.0).astype(BF16)
            key_head = jnp.where(chosen, key_rows * HEAD**-0.5, 0.0).astype(BF16)
            probs = probs_ref[0, image, head]
            value_grad += matmul_left(probs, up)
            prob_grad = matmul_right(up, values_low)
            wide = probs.astype(F32)
            weighted = wide * prob_grad
            score_grad = (
                weighted - wide * jnp.sum(weighted, axis=1, keepdims=True)
            ).astype(BF16)
            query_grad += matmul(score_grad, key_head)
            key_grad += matmul_left(score_grad, query_head)
        key_turned = pltpu.roll(key_grad, HEAD, 1)
        staged_ref[rows, 0:128] = jnp.where(low, query_grad, key_turned).astype(BF16)
        staged_ref[rows, 128:256] = jnp.where(low, value_grad, query_grad).astype(BF16)
        staged_ref[rows, 256:384] = jnp.where(low, key_turned, value_grad).astype(BF16)
    to_half(staged_ref, own_ref, far_ref)


def attend_back(packed, probs, own_grad, far_grad, after=()):
    rows, columns = packed.shape
    images, pairs = rows // PAD, columns // (6 * HEAD)
    return run_kernel(
        attend_back_kernel,
        [packed, probs, own_grad, far_grad],
        after,
        grid=(pairs,),
        in_specs=[
            pl.BlockSpec((rows, 6 * HEAD), lambda p: (0, p)),
            pl.BlockSpec((1, images, 2, PAD, PAD), lambda p: (p, 0, 0, 0, 0)),
        ]
        + halves_specs(rows, 2 * HEAD, pairs),
        out_specs=halves_specs(rows, 6 * HEAD, pairs),
        out_shape=[jax.ShapeDtypeStruct((rows, columns // 2), BF16)] * 2,
        scratch_shapes=[pltpu.VMEM((rows, 6 * HEAD), BF16)],
        compiler_params=pltpu.CompilerParams(vmem_limit_bytes=32 * 2**20),
        cost_estimate=pl.CostEstimate(flops=8 * 10**9, bytes_accessed=16 * 2**20, transcendentals=0),
    )


def normalize(stream, gain_row, shift_row):
    row_mean = jnp.mean(stream, axis=1, keepdims=True)
    centred = stream - row_mean
    inverse = lax.rsqrt(jnp.mean(centred * centred, axis=1, keepdims=True) + EPSILON)
    unit_rows = centred * inverse
    return unit_rows, inverse, (unit_rows * gain_row + shift_row).astype(BF16)


def normalize_back(upstream, unit_rows, inverse, gain_row):
    scaled = upstream * gain_row
    first = jnp.mean(scaled, axis=1, keepdims=True)
    second = jnp.mean(scaled * unit_rows, axis=1, keepdims=True)
    return (
        inverse * (scaled - first - unit_rows * second),
        jnp.sum(upstream * unit_rows, axis=0, keepdims=True),
        jnp.sum(upstream, axis=0, keepdims=True),
    )


def side(first, second, axis):
    return jnp.concatenate([first[...], second[...]], axis=axis)


def whole_spec(values):
    return pl.BlockSpec(values.shape, lambda i: (0,) * len(values.shape))


def row_spec(values, steps):
    return pl.BlockSpec((values.shape[0] // steps, values.shape[1]), lambda i: (i, 0))


def kernel_params(flops, moved):
    return {
        "compiler_params": pltpu.CompilerParams(vmem_limit_bytes=24 * 2**20),
        "cost_estimate": pl.CostEstimate(flops=flops, bytes_accessed=moved, transcendentals=0),
    }


def pad_images(col_ref, block_ref, arrived_ref, out_ref, own_wide, arrived_wide):
    half, width = arrived_ref.shape
    images = half // SEQ
    own_wide[: 2 * half] = block_ref[...].astype(F32)
    arrived_wide[:half] = arrived_ref[...].astype(F32)
    real = lax.broadcasted_iota(jnp.int32, (PAD, width), 0) < SEQ
    for image in range(images):
        rows = slice(image * PAD, (image + 1) * PAD)
        source = image * SEQ
        out_ref[rows, width:] = jnp.where(real, arrived_wide[source : source + PAD], 0.0).astype(BF16)
        for place in range(2):

            @pl.when(col_ref[0] == place)
            def _():
                begin = place * half + source
                out_ref[rows, :width] = jnp.where(real, own_wide[begin : begin + PAD], 0.0).astype(BF16)


def pad_scratch(half, width):
    extra = -(2 * half) % 8 + 16
    return [pltpu.VMEM((2 * half + extra, width), F32), pltpu.VMEM((half + 16 - half % 8, width), F32)]


def take_kernel(col_ref, block_ref, arrived_ref, out_ref, sum_ref, own_wide, arrived_wide):
    pad_images(col_ref, block_ref, arrived_ref, out_ref, own_wide, arrived_wide)
    sum_ref[...] = jnp.sum(out_ref[...].astype(F32), axis=0, keepdims=True)


def take_images(col, block, arrived, after=()):
    half, width = arrived.shape
    rows = half // SEQ * PAD
    return run_kernel(
        take_kernel,
        [col, block, arrived],
        after,
        grid=(1,),
        in_specs=[pl.BlockSpec(memory_space=pltpu.SMEM), whole_spec(block), whole_spec(arrived)],
        out_specs=[
            pl.BlockSpec((rows, 2 * width), lambda i: (0, 0)),
            pl.BlockSpec((1, 2 * width), lambda i: (0, 0)),
        ],
        out_shape=[
            jax.ShapeDtypeStruct((rows, 2 * width), BF16),
            jax.ShapeDtypeStruct((1, 2 * width), F32),
        ],
        scratch_shapes=pad_scratch(half, width),
        **kernel_params(10**6, 10 * half * width),
    )


def qkv_kernel(
    col_ref, block_ref, arrived_ref, vectors_ref, bias_ref, own, own_far, far, far_far,
    stream_ref, packed_ref, normed_ref, own_wide, arrived_wide,
):
    step, depth = packed_ref.shape[0], own.shape[0]

    @pl.when(pl.program_id(0) == 0)
    def _():
        pad_images(col_ref, block_ref, arrived_ref, stream_ref, own_wide, arrived_wide)

    begin = pl.multiple_of(pl.program_id(0) * step, 16)
    stream = stream_ref[pl.ds(begin, step)].astype(F32)
    normed = normalize(stream, vectors_ref[0:1], vectors_ref[1:2])[2]
    normed_ref[...] = normed
    columns = own.shape[1]
    packed = matmul(normed, side(own, far, 0)) + bias_ref[:, :columns]
    packed_ref[:, :columns] = packed.astype(BF16)
    packed = matmul(normed, side(own_far, far_far, 0)) + bias_ref[:, columns:]
    packed_ref[:, columns:] = packed.astype(BF16)


def widen_qkv(col, block, arrived, vectors, bias, blocks, after=()):
    half, width = arrived.shape
    rows, columns = half // SEQ * PAD, bias.shape[1]
    steps = 2
    stream = jax.ShapeDtypeStruct((rows, 2 * width), BF16)
    packed = jax.ShapeDtypeStruct((rows, columns), BF16)
    others = [block, arrived, vectors, bias, *blocks]
    return run_kernel(
        qkv_kernel,
        [col, *others],
        after,
        grid=(steps,),
        in_specs=[pl.BlockSpec(memory_space=pltpu.SMEM)] + [whole_spec(o) for o in others],
        out_specs=[whole_spec(stream), row_spec(packed, steps), row_spec(stream, steps)],
        out_shape=[stream, packed, stream],
        scratch_shapes=pad_scratch(half, width),
        **kernel_params(4 * rows * width * columns, 8 * rows * width),
    )


def out_kernel(stream_ref, left_ref, right_ref, vectors_ref, own, own_far, far, far_far, middle_ref, normed_ref):
    attended = side(left_ref, right_ref, 1)
    branch = jnp.concatenate(
        [matmul(attended, side(own, far, 0)), matmul(attended, side(own_far, far_far, 0))], axis=1
    )
    middle = stream_ref[...].astype(F32) + branch + vectors_ref[4:5]
    middle_ref[...] = middle
    normed_ref[...] = normalize(middle, vectors_ref[2:3], vectors_ref[3:4])[2]


def narrow_out(stream, left, right, vectors, blocks, after=()):
    rows, width = stream.shape
    steps = 2
    others = [vectors, *blocks]
    return run_kernel(
        out_kernel,
        [stream, left, right, *others],
        after,
        grid=(steps,),
        in_specs=[row_spec(v, steps) for v in (stream, left, right)] + [whole_spec(o) for o in others],
        out_specs=[row_spec(stream, steps)] * 2,
        out_shape=[
            pltpu.HBM((rows, width), F32),
            jax.ShapeDtypeStruct((rows, width), BF16),
        ],
        **kernel_params(2 * rows * width * width, 10 * rows * width),
    )


def gelu_kernel(acts_ref, own_top, own_low, far_top, far_low, own_bias, far_bias, *outs):
    for top_ref, low_ref, bias_ref, active_ref, slope_ref in (
        (own_top, own_low, own_bias, outs[0], outs[1]),
        (far_top, far_low, far_bias, outs[2], outs[3]),
    ):
        weight = side(top_ref, low_ref, 0)
        for begin in range(0, acts_ref.shape[0], PAD):
            chunk = slice(begin, begin + PAD)
            before = matmul(acts_ref[chunk], weight) + bias_ref[...]
            bell = jnp.exp2((before * before) * -0.7213475204444817)
            size = 1.0 + (0.3275911 * 0.5**0.5) * jnp.abs(before)
            guess = pl.reciprocal(size, approx=True)
            inv = guess * (2.0 - size * guess)
            poly = -0.726576735 + inv * 0.5307027145
            poly = 0.7107068705 + inv * poly
            poly = -0.142248368 + inv * poly
            poly = (0.127414796 + inv * poly) * inv
            tail = poly * bell
            chance = jnp.where(before < 0, tail, 1.0 - tail)
            active_ref[chunk] = (before * chance).astype(BF16)
            slope_ref[chunk] = (chance + before * (bell * 0.3989422804014327)).astype(BF16)


def widen_gelu(acts, blocks, own_bias, far_bias, after=()):
    rows, depth = acts.shape
    units = own_bias.shape[1]
    tile = 256
    wide = pl.BlockSpec((depth // 2, tile), lambda j: (0, j))
    line = pl.BlockSpec((1, tile), lambda j: (0, j))
    out = pl.BlockSpec((rows, tile), lambda j: (0, j))
    return run_kernel(
        gelu_kernel,
        [acts, *blocks, own_bias, far_bias],
        after,
        grid=(units // tile,),
        in_specs=[whole_spec(acts)] + [wide] * 4 + [line] * 2,
        out_specs=[out] * 4,
        out_shape=[
            pltpu.HBM((rows, units), BF16),
            jax.ShapeDtypeStruct((rows, units), BF16),
        ]
        * 2,
        **kernel_params(4 * rows * depth * units, 16 * rows * units),
    )


def slope_kernel(up_ref, own_left, own_right, far_left, far_right, own_slope, far_slope, *outs):
    for left_ref, right_ref, slope_ref, out_ref, sum_ref in (
        (own_left, own_right, own_slope, outs[0], outs[1]),
        (far_left, far_right, far_slope, outs[2], outs[3]),
    ):
        grad = matmul_right(up_ref[...], side(left_ref, right_ref, 1))
        low = (grad * slope_ref[...].astype(F32)).astype(BF16)
        out_ref[...] = low
        sum_ref[...] = jnp.sum(low.astype(F32), axis=0, keepdims=True)


def widen_back(upstream, blocks, own_slope, far_slope, after=()):
    rows, depth = upstream.shape
    units = own_slope.shape[1]
    tile = 256
    deep = pl.BlockSpec((tile, depth // 2), lambda j: (j, 0))
    line = pl.BlockSpec((1, tile), lambda j: (0, j))
    out = pl.BlockSpec((rows, tile), lambda j: (0, j))
    return run_kernel(
        slope_kernel,
        [upstream, *blocks, own_slope, far_slope],
        after,
        grid=(units // tile,),
        in_specs=[whole_spec(upstream)] + [deep] * 4 + [out] * 2,
        out_specs=[out, line, out, line],
        out_shape=[
            pltpu.HBM((rows, units), BF16),
            jax.ShapeDtypeStruct((1, units), F32),
        ]
        * 2,
        **kernel_params(4 * rows * depth * units, 8 * rows * units),
    )


def pack_kernel(*refs):
    col_refs, (qv_ref, fc1_ref, col_out, row_out) = refs[:6], refs[6:]
    for i in range(6):
        col_out[i : i + 1] = col_refs[i][...].reshape(1, -1)
    low = lax.broadcasted_iota(jnp.int32, (1, 128), 1) < HEAD
    for pair in range(qv_ref.shape[0] // 256):
        first = qv_ref[256 * pair : 256 * pair + 128].reshape(1, -1)
        second = qv_ref[256 * pair + 128 : 256 * pair + 256].reshape(1, -1)
        turned = [pltpu.roll(r, HEAD, 1) for r in (first, second)]
        begin = 384 * pair
        row_out[:, begin : begin + 128] = jnp.where(low, first, 0.0)
        row_out[:, begin + 128 : begin + 256] = jnp.where(low, turned[0], turned[1])
        row_out[:, begin + 256 : begin + 384] = jnp.where(low, 0.0, second)
    packed = qv_ref.shape[0] * 3 // 2
    row_out[:, packed:] = fc1_ref[...].reshape(1, -1)


def pack_vectors(col_vectors, qv_bias, fc1_bias):
    values = [in_hbm(v) for v in (*col_vectors, qv_bias, fc1_bias)]
    width = qv_bias.shape[0] * 3 // 2 + fc1_bias.shape[0]
    outs = [
        jax.ShapeDtypeStruct((6, col_vectors[0].shape[0]), F32),
        jax.ShapeDtypeStruct((1, width), F32),
    ]
    return pl.pallas_call(
        pack_kernel,
        grid=(1,),
        in_specs=[whole_spec(v) for v in values],
        out_specs=[whole_spec(o) for o in outs],
        out_shape=outs,
        **kernel_params(1000, 50000),
    )(*values)


def middle_back_kernel(
    own_grad, far_grad, middle_ref, up_ref, vectors_ref,
    own, own_far, far, far_far, out_own, out_own_far, out_far, out_far_far,
    grad_ref, low_ref, own_out, far_out, sums_ref,
):
    left, right = own_grad[...], far_grad[...]
    normed_grad = jnp.concatenate(
        [
            matmul_right(left, own[...]) + matmul_right(right, own_far[...]),
            matmul_right(left, far[...]) + matmul_right(right, far_far[...]),
        ],
        axis=1,
    )
    unit, inverse, _ = normalize(middle_ref[...], vectors_ref[2:3], vectors_ref[3:4])
    part, gain_sum, shift_sum = normalize_back(normed_grad, unit, inverse, vectors_ref[2:3])
    grad = up_ref[...].astype(F32) + part
    low = grad.astype(BF16)
    grad_ref[...] = grad
    low_ref[...] = low
    own_out[...] = matmul_right(low, side(out_own, out_own_far, 1)).astype(BF16)
    far_out[...] = matmul_right(low, side(out_far, out_far_far, 1)).astype(BF16)
    sums = jnp.concatenate(
        [gain_sum, shift_sum, jnp.sum(low.astype(F32), axis=0, keepdims=True)], axis=0
    )

    @pl.when(pl.program_id(0) == 0)
    def _():
        sums_ref[...] = sums

    @pl.when(pl.program_id(0) > 0)
    def _():
        sums_ref[...] += sums


def middle_back(own_grad, far_grad, middle, upstream, vectors, fc1_blocks, out_blocks, after=()):
    rows, width = middle.shape
    steps = 2
    rowed = [own_grad, far_grad, middle, upstream]
    others = [vectors, *fc1_blocks, *out_blocks]
    head_cols = out_blocks[0].shape[0]
    low = jax.ShapeDtypeStruct((rows, width), BF16)
    heads = pltpu.HBM((rows, head_cols), BF16)
    sums = jax.ShapeDtypeStruct((3, width), F32)
    return run_kernel(
        middle_back_kernel,
        [*rowed, *others],
        after,
        grid=(steps,),
        in_specs=[row_spec(r, steps) for r in rowed] + [whole_spec(o) for o in others],
        out_specs=[row_spec(v, steps) for v in (middle, low, heads, heads)] + [whole_spec(sums)],
        out_shape=[pltpu.HBM((rows, width), F32), low, heads, heads, sums],
        **kernel_params(4 * rows * width * own_grad.shape[1], 24 * rows * width),
    )


def cut_images(index, images, values, wide_ref):
    for step in range(wide_ref.shape[0] // SEQ // images):

        @pl.when(index == step)
        def _():
            for image in range(images):
                begin = (step * images + image) * SEQ
                wide_ref[begin : begin + SEQ] = values[image * PAD : image * PAD + SEQ]


def input_back_kernel(
    own_grad, far_grad, stream_ref, middle_grad_ref, vectors_ref,
    own, own_far, far, far_far, keep_ref, give_ref, sums_ref, packed_sums_ref, give_wide,
):
    step = pl.program_id(0)
    images = stream_ref.shape[0] // PAD
    packed_grad = side(own_grad, far_grad, 1)
    normed_grad = jnp.concatenate(
        [
            matmul_right(packed_grad, side(own, own_far, 1)),
            matmul_right(packed_grad, side(far, far_far, 1)),
        ],
        axis=1,
    )
    unit, inverse, _ = normalize(stream_ref[...].astype(F32), vectors_ref[0:1], vectors_ref[1:2])
    part, gain_sum, shift_sum = normalize_back(normed_grad, unit, inverse, vectors_ref[0:1])
    grad = middle_grad_ref[...] + part
    width = keep_ref.shape[1]
    cut_images(step, images, grad[:, :width], keep_ref)
    cut_images(step, images, grad[:, width:], give_wide)
    sums = jnp.concatenate([gain_sum, shift_sum], axis=0)
    packed_sums = jnp.sum(packed_grad.astype(F32), axis=0, keepdims=True)

    @pl.when(step == 0)
    def _():
        sums_ref[...] = sums
        packed_sums_ref[...] = packed_sums

    @pl.when(step > 0)
    def _():
        sums_ref[...] += sums
        packed_sums_ref[...] += packed_sums

    @pl.when(step == pl.num_programs(0) - 1)
    def _():
        give_ref[...] = give_wide[...].astype(BF16)


def input_back(own_grad, far_grad, stream, middle_grad, vectors, blocks, after=()):
    rows, width = stream.shape
    steps = 2
    half = rows // PAD * SEQ
    rowed = [own_grad, far_grad, stream, middle_grad]
    others = [vectors, *blocks]
    outs = [
        jax.ShapeDtypeStruct((half, width // 2), F32),
        jax.ShapeDtypeStruct((half, width // 2), BF16),
        jax.ShapeDtypeStruct((2, width), F32),
        jax.ShapeDtypeStruct((1, 2 * own_grad.shape[1]), F32),
    ]
    return run_kernel(
        input_back_kernel,
        [*rowed, *others],
        after,
        grid=(steps,),
        in_specs=[row_spec(r, steps) for r in rowed] + [whole_spec(o) for o in others],
        out_specs=[whole_spec(o) for o in outs],
        out_shape=outs,
        scratch_shapes=[pltpu.VMEM((half, width // 2), F32)],
        **kernel_params(4 * rows * width * own_grad.shape[1], 20 * rows * width),
    )


def result_kernel(
    own_acts, far_acts, middle_ref, vectors_ref, own, own_far, far, far_far,
    keep_ref, give_ref, keep_wide, give_wide,
):
    step = pl.program_id(0)
    images = middle_ref.shape[0] // PAD
    width = keep_ref.shape[1]
    left, right = own_acts[...], far_acts[...]
    for weights, columns, wide_ref in (
        ((own, far), slice(0, width), keep_wide),
        ((own_far, far_far), slice(width, 2 * width), give_wide),
    ):
        branch = matmul(left, weights[0][...]) + matmul(right, weights[1][...])
        total = middle_ref[:, columns] + branch + vectors_ref[5:6, columns]
        cut_images(step, images, total, wide_ref)

    @pl.when(step == pl.num_programs(0) - 1)
    def _():
        keep_ref[...] = keep_wide[...].astype(BF16)
        give_ref[...] = give_wide[...].astype(BF16)


def narrow_result(own_acts, far_acts, middle, vectors, blocks, after=()):
    rows, width = middle.shape
    steps = 2
    half = rows // PAD * SEQ
    rowed = [own_acts, far_acts, middle]
    others = [vectors, *blocks]
    out = jax.ShapeDtypeStruct((half, width // 2), BF16)
    return run_kernel(
        result_kernel,
        [*rowed, *others],
        after,
        grid=(steps,),
        in_specs=[row_spec(r, steps) for r in rowed] + [whole_spec(o) for o in others],
        out_specs=[whole_spec(out)] * 2,
        out_shape=[out] * 2,
        scratch_shapes=[pltpu.VMEM((half, width // 2), F32)] * 2,
        **kernel_params(4 * rows * width * own_acts.shape[1], 12 * rows * width),
    )


def in_hbm(values):
    return pltpu.with_memory_space_constraint(values, pltpu.HBM)


def weight_grad_kernel(split_dim, left_own, left_other, right_own, right_other, keep_ref, send_ref):
    total = matmul_left(left_own[...], right_own[...])
    total += matmul_left(left_other[...], right_other[...])
    half = total.shape[split_dim] // 2
    if split_dim == 0:
        keep_ref[:half] = total[:half].astype(BF16)
        send_ref[:half] = total[half:].astype(BF16)
        extra = keep_ref.shape[0] - half
        if extra:
            keep_ref[half:] = jnp.zeros((extra, total.shape[1]), BF16)
            send_ref[half:] = jnp.zeros((extra, total.shape[1]), BF16)
    else:
        keep_ref[...] = total[:, :half].astype(BF16)
        send_ref[...] = total[:, half:].astype(BF16)


def weight_grad(left_own, left_other, right_own, right_other, split_dim, tile, extra=0, more=0, after=()):
    rows, height = left_own.shape
    width = right_own.shape[1]
    if split_dim == 0:
        left = pl.BlockSpec((rows, height), lambda j: (0, 0))
        right = pl.BlockSpec((rows, tile), lambda j: (0, j))
        out = pl.BlockSpec((height // 2 + extra, tile), lambda j: (0, j))
        shape, steps = (height // 2 + extra, width + more), width // tile
    else:
        left = pl.BlockSpec((rows, tile), lambda j: (0, j))
        right = pl.BlockSpec((rows, width), lambda j: (0, 0))
        out = pl.BlockSpec((tile, width // 2), lambda j: (j, 0))
        shape, steps = (height, width // 2), height // tile
    return run_kernel(
        partial(weight_grad_kernel, split_dim),
        [in_hbm(v) for v in (left_own, left_other, right_own, right_other)],
        after,
        grid=(steps,),
        in_specs=[left, left, right, right],
        out_specs=[out, out],
        out_shape=[jax.ShapeDtypeStruct(shape, BF16)] * 2,
        **kernel_params(
            4 * rows * height * width, 4 * rows * (height + width) + 3 * height * width
        ),
    )


def out_grad_kernel(left_own, left_other, right_own, right_other, keep_in, send_in, keep_ref, send_ref):
    total = matmul_left(left_own[...], right_own[...])
    total += matmul_left(left_other[...], right_other[...])
    half = total.shape[1] // 2
    keep_ref[...] = total[:, :half].astype(BF16)
    send_ref[...] = total[:, half:].astype(BF16)


def out_weight_grad(left_own, left_other, right_own, right_other, keep, send, after=()):
    rows, height = left_own.shape
    values = [left_own, left_other, right_own, right_other]
    place = keep.shape[1] // height - 1
    out = pl.BlockSpec((height, height), lambda i: (0, place))
    unread = pl.BlockSpec(memory_space=pl.ANY)
    return run_kernel(
        out_grad_kernel,
        [*values, keep, send],
        after,
        grid=(1,),
        in_specs=[whole_spec(v) for v in values] + [unread, unread],
        out_specs=[out, out],
        out_shape=[jax.ShapeDtypeStruct(v.shape, v.dtype) for v in (keep, send)],
        input_output_aliases={4: 0, 5: 1},
        **kernel_params(8 * rows * height * height, 4 * rows * height),
    )


def together(*values):
    return lax.optimization_barrier(values)


def move(values, distance):
    size = lax.axis_size("dp")
    return lax.ppermute(values, "dp", [(i, i ^ distance) for i in range(size)])


def bit_of(distance):
    return (lax.axis_index("dp") // distance) % 2


def cut(values, index, parts):
    size = values.shape[0] // parts
    return lax.dynamic_slice_in_dim(values, index * size, size, 0)


def quarter(block):
    return cut(block, lax.axis_index("dp") % 4, 4)


def spread(piece):
    return piece, move(piece, 1), move(piece, 2), move(piece, 3)


def assemble(pieces):
    low, high = bit_of(1) == 1, bit_of(2) == 1
    first = [jnp.where(low, pieces[j ^ 1], pieces[j]) for j in range(4)]
    return jnp.concatenate([jnp.where(high, first[j ^ 2], first[j]) for j in range(4)], axis=0)


def in_order(bit, mine, other):
    return jnp.where(
        bit == 0,
        jnp.concatenate([mine, other], axis=0),
        jnp.concatenate([other, mine], axis=0),
    )


def added(first, second):
    return (first.astype(F32) + second.astype(F32)).astype(BF16)


class GradSum:
    def __init__(self, keep, send):
        self.keep, self.send = keep, send
        self.half = keep.shape[0] // 2
        self.bit = bit_of(1)
        size = lax.axis_size("dp")
        self.middle = [2**k for k in range(1, size.bit_length() - 2)]
        self.last = size // 2

    def start_first(self):
        keep_b, send_b = self.keep[self.half :], self.send[self.half :]
        out_a = swap(self.send[: self.half], "col")
        other = jnp.concatenate([cut(keep_b, 1 - self.bit, 2), cut(send_b, 1 - self.bit, 2)], axis=0)
        return out_a, move(other, 1)

    def start_second(self, arrived):
        from_col, from_dp = arrived
        keep_b, send_b = self.keep[self.half :], self.send[self.half :]
        quarter_rows = self.half // 2
        self.lower = added(cut(keep_b, self.bit, 2), from_dp[:quarter_rows])
        lower_send = added(cut(send_b, self.bit, 2), from_dp[quarter_rows:])
        keep_a = self.keep[: self.half]
        self.upper = added(cut(keep_a, self.bit, 2), cut(from_col, self.bit, 2))
        upper_send = added(cut(keep_a, 1 - self.bit, 2), cut(from_col, 1 - self.bit, 2))
        return swap(lower_send, "col"), move(upper_send, 1)

    def end_second(self, arrived):
        from_col, from_dp = arrived
        self.held = jnp.concatenate(
            [added(self.upper, from_dp), added(self.lower, from_col)], axis=0
        )

    def start_halving(self, distance):
        bit = bit_of(distance)
        self.kept = cut(self.held, bit, 2)
        return move(cut(self.held, 1 - bit, 2), distance)

    def end_halving(self, arrived):
        self.held = added(self.kept, arrived)

    def start_last(self):
        return move(self.held, self.last)

    def end_last(self, arrived):
        self.held = added(self.held, arrived)

    def start_doubling(self, distance):
        return move(self.held, distance)

    def end_doubling(self, distance, arrived):
        self.held = in_order(bit_of(distance), self.held, arrived)

    def start_whole(self):
        return move(self.held, 1)

    def end_whole(self, arrived):
        half = self.half // 2
        upper = in_order(self.bit, self.held[:half], arrived[:half])
        lower = in_order(self.bit, self.held[half:], arrived[half:])
        return jnp.concatenate([upper, lower], axis=0)


def per_device(
    tokens,
    cotangent,
    ln1_gain,
    ln1_bias,
    qkv_weight,
    qv_bias,
    out_weight,
    out_bias,
    ln2_gain,
    ln2_bias,
    fc1_weight,
    fc1_bias,
    fc2_weight,
    fc2_bias,
):
    col = lax.axis_index("col")
    col_scalar = jnp.full((1,), col, jnp.int32)
    half = tokens.shape[0] // 2
    qkv_cols = qkv_weight.shape[1]
    units = fc1_weight.shape[1]

    def give_half(block):
        return lax.dynamic_slice_in_dim(block, (1 - col) * half, half, 0)

    qkv_piece = swap(quarter(qkv_weight), "col")
    col_rows, row_values = pack_vectors(
        (ln1_gain, ln1_bias, ln2_gain, ln2_bias, out_bias, fc2_bias), qv_bias, fc1_bias
    )
    col_other = swap(col_rows, "col")
    row_other = swap(row_values, "row")
    qkv_swap = swap(qkv_weight, "row")
    fc1_out_give = jnp.concatenate([quarter(fc1_weight), quarter(out_weight)], axis=1)
    qkv_piece, col_other, row_other, token_give = together(
        qkv_piece, col_other, row_other, give_half(tokens)
    )
    qkv_pieces = spread(qkv_piece)
    token_other = swap(token_give, "col")
    vectors = jnp.concatenate([col_rows, col_other], axis=1)
    qkv_bias = jnp.concatenate([row_values[:, :qkv_cols], row_other[:, :qkv_cols]], axis=1)

    qkv_pieces, token_other, fc1_out_give, vectors, qkv_bias, fc2_give, cot_give = together(
        qkv_pieces,
        token_other,
        fc1_out_give,
        vectors,
        qkv_bias,
        quarter(fc2_weight),
        give_half(cotangent),
    )
    qkv_far = assemble(qkv_pieces)
    qkv_far_swap = swap(qkv_far, "row")
    fc1_out_piece = swap(fc1_out_give, "col")
    qkv_blocks = [qkv_weight, qkv_swap, qkv_far, qkv_far_swap]
    stream, packed, normed1, end = widen_qkv(
        col_scalar, tokens, token_other, vectors, qkv_bias, qkv_blocks
    )

    end, fc1_out_piece, fc2_give = together(end, fc1_out_piece, fc2_give)
    fc1_out_pieces = spread(fc1_out_piece)
    fc2_piece = swap(fc2_give, "col")
    out_swap = swap(out_weight, "row")
    attended_mine, attended_away, probs, end = attend(packed, end)

    end, fc1_out_pieces, fc2_piece, out_swap, cot_give = together(
        end, fc1_out_pieces, fc2_piece, out_swap, cot_give
    )
    out_far = assemble([m[:, units:] for m in fc1_out_pieces])
    out_far_swap = swap(out_far, "row")
    fc2_pieces = spread(fc2_piece)
    cot_other = swap(cot_give, "col")
    fc1_far = assemble([m[:, :units] for m in fc1_out_pieces])
    fc1_far_swap = swap(fc1_far, "row")
    fc1_swap = swap(fc1_weight, "row")
    out_blocks = [out_weight, out_far, out_swap, out_far_swap]
    middle, normed2, end = narrow_out(
        stream, attended_mine, attended_away, vectors, out_blocks, end
    )

    end, fc1_swap, fc1_far_swap, fc2_swap = together(end, fc1_swap, fc1_far_swap, fc2_weight)
    fc2_swap = swap(fc2_swap, "row")
    fc1_blocks = [fc1_weight, fc1_far, fc1_swap, fc1_far_swap]
    active, slope, active_far, slope_far, end = widen_gelu(
        normed2, fc1_blocks, row_values[:, qkv_cols:], row_other[:, qkv_cols:], end
    )

    end, fc2_pieces, fc2_swap, cot_other = together(end, fc2_pieces, fc2_swap, cot_other)
    fc2_away = assemble(fc2_pieces)
    fc2_away_swap = swap(fc2_away, "row")
    active_other = swap(active_far, "row")
    upstream, fc2_bgrad, end = take_images(col_scalar, cotangent, cot_other, end)
    upstream_other = swap(upstream, "row")
    fc2_blocks = [fc2_weight, fc2_away, fc2_swap, fc2_away_swap]
    before_grad, before_sum, before_far, before_far_sum, end = widen_back(
        upstream, fc2_blocks, slope, slope_far, end
    )

    end, active_other, upstream_other = together(end, active_other, upstream_other)
    before_other = swap(before_far, "row")
    normed2_other = swap(normed2, "row")
    attended_other = swap(attended_away, "row")
    normed1_other = swap(normed1, "row")
    fc2_keep, fc2_send, end = weight_grad(
        active, active_other, upstream, upstream_other, 1, 256, after=end
    )

    sum2 = GradSum(fc2_keep, fc2_send)
    flying2 = sum2.start_first()
    middle_grad, middle_low, attended_grad, attended_grad_far, middle_sums, end = middle_back(
        before_grad,
        before_far,
        middle,
        upstream,
        vectors,
        [fc1_weight, fc1_swap, fc1_far, fc1_far_swap],
        out_blocks,
        end,
    )

    end, flying2, before_other, normed2_other, attended_other, normed1_other = together(
        end, flying2, before_other, normed2_other, attended_other, normed1_other
    )
    flying2 = sum2.start_second(flying2)
    middle_other = swap(middle_low, "row")
    fc1_keep, fc1_send, end = weight_grad(
        normed2, normed2_other, before_grad, before_other, 0, 384, more=384, after=end
    )

    end, flying2, middle_other = together(end, flying2, middle_other)
    sum2.end_second(flying2)
    middle_steps = sum2.middle
    for distance in middle_steps[:-1]:
        sum2.end_halving(sum2.start_halving(distance))
    flying2 = sum2.start_halving(middle_steps[-1])
    fc1_keep, fc1_send, end = out_weight_grad(
        attended_mine, attended_other, middle_low, middle_other, fc1_keep, fc1_send, end
    )

    end, flying2 = together(end, flying2)
    sum1 = GradSum(fc1_keep, fc1_send)
    flying1 = sum1.start_first()
    sum2.end_halving(flying2)
    flying2 = sum2.start_last()
    packed_grad, packed_grad_far, end = attend_back(
        packed, probs, attended_grad, attended_grad_far, end
    )

    end, flying1, flying2 = together(end, flying1, flying2)
    packed_other = swap(packed_grad_far, "row")
    flying1 = sum1.start_second(flying1)
    sum2.end_last(flying2)
    flying2 = sum2.start_doubling(middle_steps[-1])
    input_own, input_give, input_sums, packed_sums, end = input_back(
        packed_grad, packed_grad_far, stream, middle_grad, vectors, qkv_blocks, end
    )

    end, flying1, flying2, packed_other = together(end, flying1, flying2, packed_other)
    sum1.end_second(flying1)
    for distance in middle_steps[:-1]:
        sum1.end_halving(sum1.start_halving(distance))
    flying1 = sum1.start_halving(middle_steps[-1])
    sum2.end_doubling(middle_steps[-1], flying2)
    for distance in reversed(middle_steps[:-1]):
        sum2.end_doubling(distance, sum2.start_doubling(distance))
    flying2 = sum2.start_whole()
    kinds = packed_sums.reshape(-1, 3, HEAD)
    width = input_sums.shape[1]
    qv_grad = jnp.stack([kinds[:, 0], kinds[:, 2]], axis=1).reshape(2, -1, width)
    fc1_bgrad = jnp.stack([before_sum.reshape(-1, width), before_far_sum.reshape(-1, width)])
    by_row = jnp.concatenate([qv_grad, fc1_bgrad], axis=1)
    by_col = jnp.concatenate([input_sums, middle_sums, fc2_bgrad], axis=0)
    row_count = by_row.shape[1]
    small_other = swap(jnp.concatenate([by_row[1], by_col], axis=0), "row")
    qkv_keep, qkv_send, end = weight_grad(
        normed1, normed1_other, packed_grad, packed_other, 0, 384, EXTRA, after=end
    )

    end, flying1, small_other = together(end, flying1, small_other)
    by_row = (by_row[0] + small_other[:row_count]).reshape(-1, qkv_cols)
    by_col = by_col + small_other[row_count:]
    begin = qkv_keep.shape[0] - EXTRA
    both_cols = [
        jnp.concatenate([by_row, half_cols.reshape(-1, qkv_cols)], axis=0).astype(BF16)
        for half_cols in jnp.split(by_col, 2, axis=1)
    ]
    qkv_keep = lax.dynamic_update_slice(qkv_keep, both_cols[0], (begin, 0))
    qkv_send = lax.dynamic_update_slice(qkv_send, both_cols[1], (begin, 0))

    sum0 = GradSum(qkv_keep, qkv_send)
    flying0 = sum0.start_first()
    sum1.end_halving(flying1)
    flying1 = sum1.start_last()
    result_own, result_give, end = narrow_result(
        active, active_far, middle, vectors, fc2_blocks, end
    )

    flying0, result_give = together(flying0, result_give)
    flying0 = sum0.start_second(flying0)

    flying0, flying1, flying2, input_give = together(flying0, flying1, flying2, input_give)
    sum0.end_second(flying0)
    for distance in middle_steps[:-1]:
        sum0.end_halving(sum0.start_halving(distance))
    flying0 = sum0.start_halving(middle_steps[-1])
    sum1.end_last(flying1)
    flying1 = sum1.start_doubling(middle_steps[-1])
    input_other = swap(input_give, "col")
    fc2_wgrad = sum2.end_whole(flying2).astype(F32)

    (flying0,) = together(flying0)
    sum0.end_halving(flying0)
    flying0 = sum0.start_last()
    sum1.end_doubling(middle_steps[-1], flying1)
    for distance in reversed(middle_steps[:-1]):
        sum1.end_doubling(distance, sum1.start_doubling(distance))
    flying1 = sum1.start_whole()

    input_other, result_give = together(input_other, result_give)
    result_other = swap(result_give, "col")
    (flying0,) = together(flying0)
    sum0.end_last(flying0)
    flying0 = sum0.start_doubling(middle_steps[-1])
    input_grad = in_order(col, input_own, input_other.astype(F32))

    flying0, result_other = together(flying0, result_other)
    sum0.end_doubling(middle_steps[-1], flying0)
    for distance in reversed(middle_steps[:-1]):
        sum0.end_doubling(distance, sum0.start_doubling(distance))
    flying0 = sum0.start_whole()
    fc1_out_grad = sum1.end_whole(flying1)
    result = in_order(col, result_own, result_other)
    qkv_whole = sum0.end_whole(flying0)
    qv_size = qv_bias.shape[0]
    rows_each = by_row.shape[0]
    vector_rows = qkv_whole[begin : begin + 2 * rows_each].astype(F32)
    by_row = vector_rows[:rows_each].reshape(-1)
    by_col = vector_rows[rows_each:].reshape(6, -1)
    return (
        result,
        input_grad,
        by_col[0],
        by_col[1],
        qkv_whole[:begin].astype(F32),
        by_row[:qv_size],
        fc1_out_grad[:, units:].astype(F32),
        by_col[4],
        by_col[2],
        by_col[3],
        fc1_out_grad[:, :units].astype(F32),
        by_row[qv_size:],
        fc2_wgrad,
        by_col[5],
    )


def solution(mesh):
    stream = P(("dp", "row"), "col")
    by_col, by_row = P("col"), P("row")
    wide, deep = P("col", "row"), P("row", "col")
    in_specs = (
        stream, stream, by_col, by_col, wide, by_row, deep, by_col,
        by_col, by_col, wide, by_row, deep, by_col,
    )
    return jax.shard_map(
        per_device, mesh=mesh, in_specs=in_specs, out_specs=in_specs, check_vma=False
    )
```

```python
from functools import partial

import jax
import jax.numpy as jnp
from jax import lax
from jax.experimental import pallas as pl
from jax.experimental.pallas import tpu as pltpu
from jax.sharding import PartitionSpec as P

HEAD = 64
SEQ = 197
PAD = 208
EXTRA = 32
EPSILON = 1e-06
LEFT_INNER = (((0,), (0,)), ((), ()))
RIGHT_INNER = (((1,), (1,)), ((), ()))
BF16 = jnp.bfloat16
F32 = jnp.float32


def swap(values, axis):
    return lax.ppermute(values, axis, [(0, 1), (1, 0)])


def matmul(left, right):
    return jnp.dot(left, right, preferred_element_type=F32)


def matmul_left(left, right):
    return lax.dot_general(left, right, LEFT_INNER, preferred_element_type=F32)


def matmul_right(left, right):
    return lax.dot_general(left, right, RIGHT_INNER, preferred_element_type=F32)


def split_pair(c0, c1, c2):
    low = lax.broadcasted_iota(jnp.int32, c0.shape, 1) < HEAD
    queries = jnp.where(low, c0, c1)
    key_rows = pltpu.roll(jnp.where(low, c2, c0), HEAD, 1)
    values = jnp.where(low, c1, c2)
    return queries, key_rows, values, low


def to_half(staged_ref, own_ref, far_ref):
    first_half = pl.program_id(0) < pl.num_programs(0) // 2

    @pl.when(first_half)
    def _():
        own_ref[...] = staged_ref[...]

    @pl.when(jnp.logical_not(first_half))
    def _():
        far_ref[...] = staged_ref[...]


def run_kernel(kernel, values, after, in_specs, out_specs, out_shape, **settings):
    values, after = list(values), jax.tree.leaves(after)
    count, skip = len(values), len(values) + len(after)
    outs = len(out_shape)

    def body(*refs):
        end_ref = refs[skip + outs]
        end_ref[...] = jnp.zeros_like(end_ref)
        kernel(*refs[:count], *refs[skip : skip + outs], *refs[skip + outs + 1 :])

    unread = [pl.BlockSpec(memory_space=pl.ANY)] * len(after)
    end = jax.ShapeDtypeStruct((8, 128), F32)
    return pl.pallas_call(
        body,
        in_specs=list(in_specs) + unread,
        out_specs=list(out_specs) + [whole_spec(end)],
        out_shape=list(out_shape) + [end],
        **settings,
    )(*values, *after)


def in_hbm(values):
    return pltpu.with_memory_space_constraint(values, pltpu.HBM)


def attend_kernel(packed_ref, own_ref, far_ref, probs_ref, staged_ref):
    images = packed_ref.shape[0] // PAD
    for image in range(images):
        rows = slice(image * PAD, (image + 1) * PAD)
        blocks = [packed_ref[rows, 128 * j : 128 * (j + 1)].astype(F32) for j in range(3)]
        queries, key_rows, values, low = split_pair(*blocks)
        keys_low = key_rows.astype(BF16)
        values_low = values.astype(BF16)
        outs = []
        for head in range(2):
            chosen = low if head == 0 else jnp.logical_not(low)
            masked = jnp.where(chosen, queries * HEAD**-0.5, 0.0).astype(BF16)
            scores = matmul_right(masked, keys_low)
            real = lax.broadcasted_iota(jnp.int32, scores.shape, 1) < SEQ
            scores = jnp.where(real, scores, -1e30)
            raised = jnp.exp(scores - jnp.max(scores, axis=1, keepdims=True))
            probs = (raised * (1.0 / jnp.sum(raised, axis=1, keepdims=True))).astype(BF16)
            probs_ref[0, image, head] = probs
            outs.append(matmul(probs, values_low))
        staged_ref[rows] = jnp.where(low, outs[0], outs[1]).astype(BF16)
    to_half(staged_ref, own_ref, far_ref)


def halves_specs(rows, width, steps):
    half = steps // 2
    return [
        pl.BlockSpec((rows, width), lambda p: (0, jnp.minimum(p, half - 1))),
        pl.BlockSpec((rows, width), lambda p: (0, jnp.maximum(p - half, 0))),
    ]


def attend(packed, after=()):
    rows, columns = packed.shape
    images, pairs = rows // PAD, columns // (6 * HEAD)
    return run_kernel(
        attend_kernel,
        [packed],
        after,
        grid=(pairs,),
        in_specs=[pl.BlockSpec((rows, 6 * HEAD), lambda p: (0, p))],
        out_specs=halves_specs(rows, 2 * HEAD, pairs)
        + [pl.BlockSpec((1, images, 2, PAD, PAD), lambda p: (p, 0, 0, 0, 0))],
        out_shape=[jax.ShapeDtypeStruct((rows, columns // 6), BF16)] * 2
        + [pltpu.HBM((pairs, images, 2, PAD, PAD), BF16)],
        scratch_shapes=[pltpu.VMEM((rows, 2 * HEAD), BF16)],
        compiler_params=pltpu.CompilerParams(vmem_limit_bytes=32 * 2**20),
        cost_estimate=pl.CostEstimate(flops=3 * 10**9, bytes_accessed=12 * 2**20, transcendentals=0),
    )


def attend_back_kernel(packed_ref, probs_ref, own_grad, far_grad, own_ref, far_ref, staged_ref):
    images = packed_ref.shape[0] // PAD
    first_half = pl.program_id(0) < pl.num_programs(0) // 2
    for image in range(images):
        rows = slice(image * PAD, (image + 1) * PAD)
        blocks = [packed_ref[rows, 128 * j : 128 * (j + 1)].astype(F32) for j in range(3)]
        queries, key_rows, values, low = split_pair(*blocks)
        values_low = values.astype(BF16)
        upstream = jnp.where(first_half, own_grad[rows].astype(F32), far_grad[rows].astype(F32))
        query_grad = key_grad = value_grad = 0.0
        for head in range(2):
            chosen = low if head == 0 else jnp.logical_not(low)
            up = jnp.where(chosen, upstream, 0.0).astype(BF16)
            query_head = jnp.where(chosen, queries * HEAD**-0.5, 0.0).astype(BF16)
            key_head = jnp.where(chosen, key_rows * HEAD**-0.5, 0.0).astype(BF16)
            probs = probs_ref[0, image, head]
            value_grad += matmul_left(probs, up)
            prob_grad = matmul_right(up, values_low)
            wide = probs.astype(F32)
            weighted = wide * prob_grad
            score_grad = (
                weighted - wide * jnp.sum(weighted, axis=1, keepdims=True)
            ).astype(BF16)
            query_grad += matmul(score_grad, key_head)
            key_grad += matmul_left(score_grad, query_head)
        key_turned = pltpu.roll(key_grad, HEAD, 1)
        staged_ref[rows, 0:128] = jnp.where(low, query_grad, key_turned).astype(BF16)
        staged_ref[rows, 128:256] = jnp.where(low, value_grad, query_grad).astype(BF16)
        staged_ref[rows, 256:384] = jnp.where(low, key_turned, value_grad).astype(BF16)
    to_half(staged_ref, own_ref, far_ref)


def attend_back(packed, probs, own_grad, far_grad, after=()):
    rows, columns = packed.shape
    images, pairs = rows // PAD, columns // (6 * HEAD)
    return run_kernel(
        attend_back_kernel,
        [packed, probs, own_grad, far_grad],
        after,
        grid=(pairs,),
        in_specs=[
            pl.BlockSpec((rows, 6 * HEAD), lambda p: (0, p)),
            pl.BlockSpec((1, images, 2, PAD, PAD), lambda p: (p, 0, 0, 0, 0)),
        ]
        + halves_specs(rows, 2 * HEAD, pairs),
        out_specs=halves_specs(rows, 6 * HEAD, pairs),
        out_shape=[jax.ShapeDtypeStruct((rows, columns // 2), BF16)] * 2,
        scratch_shapes=[pltpu.VMEM((rows, 6 * HEAD), BF16)],
        compiler_params=pltpu.CompilerParams(vmem_limit_bytes=32 * 2**20),
        cost_estimate=pl.CostEstimate(flops=8 * 10**9, bytes_accessed=16 * 2**20, transcendentals=0),
    )


def normalize(stream, gain_row, shift_row):
    row_mean = jnp.mean(stream, axis=1, keepdims=True)
    centred = stream - row_mean
    inverse = lax.rsqrt(jnp.mean(centred * centred, axis=1, keepdims=True) + EPSILON)
    unit_rows = centred * inverse
    return unit_rows, inverse, (unit_rows * gain_row + shift_row).astype(BF16)


def normalize_back(upstream, unit_rows, inverse, gain_row):
    scaled = upstream * gain_row
    first = jnp.mean(scaled, axis=1, keepdims=True)
    second = jnp.mean(scaled * unit_rows, axis=1, keepdims=True)
    return (
        inverse * (scaled - first - unit_rows * second),
        jnp.sum(upstream * unit_rows, axis=0, keepdims=True),
        jnp.sum(upstream, axis=0, keepdims=True),
    )


def side(first, second, axis):
    return jnp.concatenate([first[...], second[...]], axis=axis)


def whole_spec(values):
    return pl.BlockSpec(values.shape, lambda i: (0,) * len(values.shape))


def row_spec(values, steps):
    return pl.BlockSpec((values.shape[0] // steps, values.shape[1]), lambda i: (i, 0))


def kernel_params(flops, moved):
    return {
        "compiler_params": pltpu.CompilerParams(vmem_limit_bytes=24 * 2**20),
        "cost_estimate": pl.CostEstimate(flops=flops, bytes_accessed=moved, transcendentals=0),
    }


def pad_images(col_ref, block_ref, arrived_ref, out_ref, own_wide, arrived_wide):
    half, width = arrived_ref.shape
    images = half // SEQ
    own_wide[: 2 * half] = block_ref[...].astype(F32)
    arrived_wide[:half] = arrived_ref[...].astype(F32)
    real = lax.broadcasted_iota(jnp.int32, (PAD, width), 0) < SEQ
    for image in range(images):
        rows = slice(image * PAD, (image + 1) * PAD)
        source = image * SEQ
        out_ref[rows, width:] = jnp.where(real, arrived_wide[source : source + PAD], 0.0).astype(BF16)
        for place in range(2):

            @pl.when(col_ref[0] == place)
            def _():
                begin = place * half + source
                out_ref[rows, :width] = jnp.where(real, own_wide[begin : begin + PAD], 0.0).astype(BF16)


def pad_scratch(half, width):
    extra = -(2 * half) % 8 + 16
    return [pltpu.VMEM((2 * half + extra, width), F32), pltpu.VMEM((half + 16 - half % 8, width), F32)]


def take_kernel(col_ref, block_ref, arrived_ref, out_ref, sum_ref, own_wide, arrived_wide):
    pad_images(col_ref, block_ref, arrived_ref, out_ref, own_wide, arrived_wide)
    sum_ref[...] = jnp.sum(out_ref[...].astype(F32), axis=0, keepdims=True)


def take_images(col, block, arrived, after=()):
    half, width = arrived.shape
    rows = half // SEQ * PAD
    return run_kernel(
        take_kernel,
        [col, in_hbm(block), in_hbm(arrived)],
        after,
        grid=(1,),
        in_specs=[pl.BlockSpec(memory_space=pltpu.SMEM), whole_spec(block), whole_spec(arrived)],
        out_specs=[
            pl.BlockSpec((rows, 2 * width), lambda i: (0, 0)),
            pl.BlockSpec((1, 2 * width), lambda i: (0, 0)),
        ],
        out_shape=[
            jax.ShapeDtypeStruct((rows, 2 * width), BF16),
            jax.ShapeDtypeStruct((1, 2 * width), F32),
        ],
        scratch_shapes=pad_scratch(half, width),
        **kernel_params(10**6, 10 * half * width),
    )


def qkv_kernel(
    col_ref, block_ref, arrived_ref, vectors_ref, bias_ref, own, own_far, far, far_far,
    stream_ref, packed_ref, normed_ref, own_wide, arrived_wide,
):
    step, depth = packed_ref.shape[0], own.shape[0]

    @pl.when(pl.program_id(0) == 0)
    def _():
        pad_images(col_ref, block_ref, arrived_ref, stream_ref, own_wide, arrived_wide)

    begin = pl.multiple_of(pl.program_id(0) * step, 16)
    stream = stream_ref[pl.ds(begin, step)].astype(F32)
    normed = normalize(stream, vectors_ref[0:1], vectors_ref[1:2])[2]
    normed_ref[...] = normed
    columns = own.shape[1]
    packed = matmul(normed, side(own, far, 0)) + bias_ref[:, :columns]
    packed_ref[:, :columns] = packed.astype(BF16)
    packed = matmul(normed, side(own_far, far_far, 0)) + bias_ref[:, columns:]
    packed_ref[:, columns:] = packed.astype(BF16)


def widen_qkv(col, block, arrived, vectors, bias, blocks, after=()):
    half, width = arrived.shape
    rows, columns = half // SEQ * PAD, bias.shape[1]
    steps = 2
    stream = jax.ShapeDtypeStruct((rows, 2 * width), BF16)
    packed = jax.ShapeDtypeStruct((rows, columns), BF16)
    others = [in_hbm(block), in_hbm(arrived), vectors, bias, *blocks]
    return run_kernel(
        qkv_kernel,
        [col, *others],
        after,
        grid=(steps,),
        in_specs=[pl.BlockSpec(memory_space=pltpu.SMEM)] + [whole_spec(o) for o in others],
        out_specs=[whole_spec(stream), row_spec(packed, steps), row_spec(stream, steps)],
        out_shape=[pltpu.HBM(stream.shape, BF16), packed, pltpu.HBM(stream.shape, BF16)],
        scratch_shapes=pad_scratch(half, width),
        **kernel_params(4 * rows * width * columns, 8 * rows * width),
    )


def out_kernel(stream_ref, left_ref, right_ref, vectors_ref, own, own_far, far, far_far, middle_ref, normed_ref):
    attended = side(left_ref, right_ref, 1)
    branch = jnp.concatenate(
        [matmul(attended, side(own, far, 0)), matmul(attended, side(own_far, far_far, 0))], axis=1
    )
    middle = stream_ref[...].astype(F32) + branch + vectors_ref[4:5]
    middle_ref[...] = middle
    normed_ref[...] = normalize(middle, vectors_ref[2:3], vectors_ref[3:4])[2]


def narrow_out(stream, left, right, vectors, blocks, after=()):
    rows, width = stream.shape
    steps = 2
    others = [vectors, *blocks]
    return run_kernel(
        out_kernel,
        [stream, left, right, *others],
        after,
        grid=(steps,),
        in_specs=[row_spec(v, steps) for v in (stream, left, right)] + [whole_spec(o) for o in others],
        out_specs=[row_spec(stream, steps)] * 2,
        out_shape=[
            pltpu.HBM((rows, width), F32),
            jax.ShapeDtypeStruct((rows, width), BF16),
        ],
        **kernel_params(2 * rows * width * width, 10 * rows * width),
    )


def gelu_kernel(acts_ref, own_top, own_low, far_top, far_low, own_bias, far_bias, *outs):
    for top_ref, low_ref, bias_ref, active_ref, slope_ref in (
        (own_top, own_low, own_bias, outs[0], outs[1]),
        (far_top, far_low, far_bias, outs[2], outs[3]),
    ):
        weight = side(top_ref, low_ref, 0)
        for begin in range(0, acts_ref.shape[0], PAD):
            chunk = slice(begin, begin + PAD)
            before = matmul(acts_ref[chunk], weight) + bias_ref[...]
            bell = jnp.exp2((before * before) * -0.7213475204444817)
            size = 1.0 + (0.3275911 * 0.5**0.5) * jnp.abs(before)
            guess = pl.reciprocal(size, approx=True)
            inv = guess * (2.0 - size * guess)
            poly = -0.726576735 + inv * 0.5307027145
            poly = 0.7107068705 + inv * poly
            poly = -0.142248368 + inv * poly
            poly = (0.127414796 + inv * poly) * inv
            tail = poly * bell
            chance = jnp.where(before < 0, tail, 1.0 - tail)
            active_ref[chunk] = (before * chance).astype(BF16)
            slope_ref[chunk] = (chance + before * (bell * 0.3989422804014327)).astype(BF16)


def widen_gelu(acts, blocks, own_bias, far_bias, after=()):
    rows, depth = acts.shape
    units = own_bias.shape[1]
    tile = 256
    wide = pl.BlockSpec((depth // 2, tile), lambda j: (0, j))
    line = pl.BlockSpec((1, tile), lambda j: (0, j))
    out = pl.BlockSpec((rows, tile), lambda j: (0, j))
    return run_kernel(
        gelu_kernel,
        [acts, *blocks, own_bias, far_bias],
        after,
        grid=(units // tile,),
        in_specs=[whole_spec(acts)] + [wide] * 4 + [line] * 2,
        out_specs=[out] * 4,
        out_shape=[pltpu.HBM((rows, units), BF16)] * 4,
        **kernel_params(4 * rows * depth * units, 16 * rows * units),
    )


def slope_kernel(up_ref, own_left, own_right, far_left, far_right, own_slope, far_slope, *outs):
    for left_ref, right_ref, slope_ref, out_ref, sum_ref in (
        (own_left, own_right, own_slope, outs[0], outs[1]),
        (far_left, far_right, far_slope, outs[2], outs[3]),
    ):
        grad = matmul_right(up_ref[...], side(left_ref, right_ref, 1))
        low = (grad * slope_ref[...].astype(F32)).astype(BF16)
        out_ref[...] = low
        sum_ref[...] = jnp.sum(low.astype(F32), axis=0, keepdims=True)


def widen_back(upstream, blocks, own_slope, far_slope, after=()):
    rows, depth = upstream.shape
    units = own_slope.shape[1]
    tile = 256
    deep = pl.BlockSpec((tile, depth // 2), lambda j: (j, 0))
    line = pl.BlockSpec((1, tile), lambda j: (0, j))
    out = pl.BlockSpec((rows, tile), lambda j: (0, j))
    return run_kernel(
        slope_kernel,
        [upstream, *blocks, own_slope, far_slope],
        after,
        grid=(units // tile,),
        in_specs=[whole_spec(upstream)] + [deep] * 4 + [out] * 2,
        out_specs=[out, line, out, line],
        out_shape=[
            pltpu.HBM((rows, units), BF16),
            jax.ShapeDtypeStruct((1, units), F32),
        ]
        * 2,
        **kernel_params(4 * rows * depth * units, 8 * rows * units),
    )


def pack_kernel(*refs):
    col_refs, (qv_ref, fc1_ref, col_out, row_out) = refs[:6], refs[6:]
    for i in range(6):
        col_out[i : i + 1] = col_refs[i][...].reshape(1, -1)
    low = lax.broadcasted_iota(jnp.int32, (1, 128), 1) < HEAD
    for pair in range(qv_ref.shape[0] // 256):
        first = qv_ref[256 * pair : 256 * pair + 128].reshape(1, -1)
        second = qv_ref[256 * pair + 128 : 256 * pair + 256].reshape(1, -1)
        turned = [pltpu.roll(r, HEAD, 1) for r in (first, second)]
        begin = 384 * pair
        row_out[:, begin : begin + 128] = jnp.where(low, first, 0.0)
        row_out[:, begin + 128 : begin + 256] = jnp.where(low, turned[0], turned[1])
        row_out[:, begin + 256 : begin + 384] = jnp.where(low, 0.0, second)
    packed = qv_ref.shape[0] * 3 // 2
    row_out[:, packed:] = fc1_ref[...].reshape(1, -1)


def pack_vectors(col_vectors, qv_bias, fc1_bias):
    values = [in_hbm(v) for v in (*col_vectors, qv_bias, fc1_bias)]
    width = qv_bias.shape[0] * 3 // 2 + fc1_bias.shape[0]
    outs = [
        jax.ShapeDtypeStruct((6, col_vectors[0].shape[0]), F32),
        jax.ShapeDtypeStruct((1, width), F32),
    ]
    return pl.pallas_call(
        pack_kernel,
        grid=(1,),
        in_specs=[whole_spec(v) for v in values],
        out_specs=[whole_spec(o) for o in outs],
        out_shape=outs,
        **kernel_params(1000, 50000),
    )(*values)


def middle_back_kernel(
    own_grad, far_grad, middle_ref, up_ref, vectors_ref,
    own, own_far, far, far_far, out_own, out_own_far, out_far, out_far_far,
    grad_ref, low_ref, own_out, far_out, sums_ref,
):
    left, right = own_grad[...], far_grad[...]
    normed_grad = jnp.concatenate(
        [
            matmul_right(left, own[...]) + matmul_right(right, own_far[...]),
            matmul_right(left, far[...]) + matmul_right(right, far_far[...]),
        ],
        axis=1,
    )
    unit, inverse, _ = normalize(middle_ref[...], vectors_ref[2:3], vectors_ref[3:4])
    part, gain_sum, shift_sum = normalize_back(normed_grad, unit, inverse, vectors_ref[2:3])
    grad = up_ref[...].astype(F32) + part
    low = grad.astype(BF16)
    grad_ref[...] = grad
    low_ref[...] = low
    own_out[...] = matmul_right(low, side(out_own, out_own_far, 1)).astype(BF16)
    far_out[...] = matmul_right(low, side(out_far, out_far_far, 1)).astype(BF16)
    sums = jnp.concatenate(
        [gain_sum, shift_sum, jnp.sum(low.astype(F32), axis=0, keepdims=True)], axis=0
    )

    @pl.when(pl.program_id(0) == 0)
    def _():
        sums_ref[...] = sums

    @pl.when(pl.program_id(0) > 0)
    def _():
        sums_ref[...] += sums


def middle_back(own_grad, far_grad, middle, upstream, vectors, fc1_blocks, out_blocks, after=()):
    rows, width = middle.shape
    steps = 2
    rowed = [own_grad, far_grad, middle, upstream]
    others = [vectors, *fc1_blocks, *out_blocks]
    head_cols = out_blocks[0].shape[0]
    low = jax.ShapeDtypeStruct((rows, width), BF16)
    heads = pltpu.HBM((rows, head_cols), BF16)
    sums = jax.ShapeDtypeStruct((3, width), F32)
    return run_kernel(
        middle_back_kernel,
        [*rowed, *others],
        after,
        grid=(steps,),
        in_specs=[row_spec(r, steps) for r in rowed] + [whole_spec(o) for o in others],
        out_specs=[row_spec(v, steps) for v in (middle, low, heads, heads)] + [whole_spec(sums)],
        out_shape=[pltpu.HBM((rows, width), F32), low, heads, heads, sums],
        **kernel_params(4 * rows * width * own_grad.shape[1], 24 * rows * width),
    )


def cut_images(index, images, values, wide_ref):
    for step in range(wide_ref.shape[0] // SEQ // images):

        @pl.when(index == step)
        def _():
            for image in range(images):
                begin = (step * images + image) * SEQ
                wide_ref[begin : begin + SEQ] = values[image * PAD : image * PAD + SEQ]


def input_back_kernel(
    own_grad, far_grad, stream_ref, middle_grad_ref, vectors_ref,
    own, own_far, far, far_far, keep_ref, give_ref, sums_ref, packed_sums_ref, give_wide,
):
    step = pl.program_id(0)
    images = stream_ref.shape[0] // PAD
    packed_grad = side(own_grad, far_grad, 1)
    normed_grad = jnp.concatenate(
        [
            matmul_right(packed_grad, side(own, own_far, 1)),
            matmul_right(packed_grad, side(far, far_far, 1)),
        ],
        axis=1,
    )
    unit, inverse, _ = normalize(stream_ref[...].astype(F32), vectors_ref[0:1], vectors_ref[1:2])
    part, gain_sum, shift_sum = normalize_back(normed_grad, unit, inverse, vectors_ref[0:1])
    grad = middle_grad_ref[...] + part
    width = keep_ref.shape[1]
    cut_images(step, images, grad[:, :width], keep_ref)
    cut_images(step, images, grad[:, width:], give_wide)
    sums = jnp.concatenate([gain_sum, shift_sum], axis=0)
    packed_sums = jnp.sum(packed_grad.astype(F32), axis=0, keepdims=True)

    @pl.when(step == 0)
    def _():
        sums_ref[...] = sums
        packed_sums_ref[...] = packed_sums

    @pl.when(step > 0)
    def _():
        sums_ref[...] += sums
        packed_sums_ref[...] += packed_sums

    @pl.when(step == pl.num_programs(0) - 1)
    def _():
        give_ref[...] = give_wide[...].astype(BF16)


def input_back(own_grad, far_grad, stream, middle_grad, vectors, blocks, after=()):
    rows, width = stream.shape
    steps = 2
    half = rows // PAD * SEQ
    rowed = [own_grad, far_grad, stream, middle_grad]
    others = [vectors, *blocks]
    outs = [
        pltpu.HBM((half, width // 2), F32),
        pltpu.HBM((half, width // 2), BF16),
        jax.ShapeDtypeStruct((2, width), F32),
        jax.ShapeDtypeStruct((1, 2 * own_grad.shape[1]), F32),
    ]
    return run_kernel(
        input_back_kernel,
        [*rowed, *others],
        after,
        grid=(steps,),
        in_specs=[row_spec(r, steps) for r in rowed] + [whole_spec(o) for o in others],
        out_specs=[whole_spec(o) for o in outs],
        out_shape=outs,
        scratch_shapes=[pltpu.VMEM((half, width // 2), F32)],
        **kernel_params(4 * rows * width * own_grad.shape[1], 20 * rows * width),
    )


def result_kernel(
    own_acts, far_acts, middle_ref, vectors_ref, own, own_far, far, far_far,
    keep_ref, give_ref, keep_wide, give_wide,
):
    step = pl.program_id(0)
    images = middle_ref.shape[0] // PAD
    width = keep_ref.shape[1]
    left, right = own_acts[...], far_acts[...]
    for weights, columns, wide_ref in (
        ((own, far), slice(0, width), keep_wide),
        ((own_far, far_far), slice(width, 2 * width), give_wide),
    ):
        branch = matmul(left, weights[0][...]) + matmul(right, weights[1][...])
        total = middle_ref[:, columns] + branch + vectors_ref[5:6, columns]
        cut_images(step, images, total, wide_ref)

    @pl.when(step == pl.num_programs(0) - 1)
    def _():
        keep_ref[...] = keep_wide[...].astype(BF16)
        give_ref[...] = give_wide[...].astype(BF16)


def narrow_result(own_acts, far_acts, middle, vectors, blocks, after=()):
    rows, width = middle.shape
    steps = 2
    half = rows // PAD * SEQ
    rowed = [in_hbm(own_acts), in_hbm(far_acts), middle]
    others = [vectors, *blocks]
    out = jax.ShapeDtypeStruct((half, width // 2), BF16)
    return run_kernel(
        result_kernel,
        [*rowed, *others],
        after,
        grid=(steps,),
        in_specs=[row_spec(r, steps) for r in rowed] + [whole_spec(o) for o in others],
        out_specs=[whole_spec(out)] * 2,
        out_shape=[out] * 2,
        scratch_shapes=[pltpu.VMEM((half, width // 2), F32)] * 2,
        **kernel_params(4 * rows * width * own_acts.shape[1], 12 * rows * width),
    )


def weight_grad_kernel(split_dim, left_own, left_other, right_own, right_other, keep_ref, send_ref):
    total = matmul_left(side(left_own, left_other, 0), side(right_own, right_other, 0))
    half = total.shape[split_dim] // 2
    if split_dim == 0:
        keep_ref[:half] = total[:half].astype(BF16)
        send_ref[:half] = total[half:].astype(BF16)
        extra = keep_ref.shape[0] - half
        if extra:
            keep_ref[half:] = jnp.zeros((extra, total.shape[1]), BF16)
            send_ref[half:] = jnp.zeros((extra, total.shape[1]), BF16)
    else:
        keep_ref[...] = total[:, :half].astype(BF16)
        send_ref[...] = total[:, half:].astype(BF16)


def weight_grad(left_own, left_other, right_own, right_other, split_dim, tile, extra=0, more=0, after=()):
    rows, height = left_own.shape
    width = right_own.shape[1]
    if split_dim == 0:
        left = pl.BlockSpec((rows, height), lambda j: (0, 0))
        right = pl.BlockSpec((rows, tile), lambda j: (0, j))
        out = pl.BlockSpec((height // 2 + extra, tile), lambda j: (0, j))
        shape, steps = (height // 2 + extra, width + more), width // tile
    else:
        left = pl.BlockSpec((rows, tile), lambda j: (0, j))
        right = pl.BlockSpec((rows, width), lambda j: (0, 0))
        out = pl.BlockSpec((tile, width // 2), lambda j: (j, 0))
        shape, steps = (height, width // 2), height // tile
    return run_kernel(
        partial(weight_grad_kernel, split_dim),
        [in_hbm(v) for v in (left_own, left_other, right_own, right_other)],
        after,
        grid=(steps,),
        in_specs=[left, left, right, right],
        out_specs=[out, out],
        out_shape=[jax.ShapeDtypeStruct(shape, BF16)] * 2,
        **kernel_params(
            4 * rows * height * width, 4 * rows * (height + width) + 3 * height * width
        ),
    )


def out_grad_kernel(left_own, left_other, right_own, right_other, keep_in, send_in, keep_ref, send_ref):
    total = matmul_left(side(left_own, left_other, 0), side(right_own, right_other, 0))
    half = total.shape[1] // 2
    keep_ref[...] = total[:, :half].astype(BF16)
    send_ref[...] = total[:, half:].astype(BF16)


def out_weight_grad(left_own, left_other, right_own, right_other, keep, send, after=()):
    rows, height = left_own.shape
    values = [in_hbm(v) for v in (left_own, left_other, right_own, right_other)]
    place = keep.shape[1] // height - 1
    out = pl.BlockSpec((height, height), lambda i: (0, place))
    unread = pl.BlockSpec(memory_space=pl.ANY)
    return run_kernel(
        out_grad_kernel,
        [*values, keep, send],
        after,
        grid=(1,),
        in_specs=[whole_spec(v) for v in values] + [unread, unread],
        out_specs=[out, out],
        out_shape=[jax.ShapeDtypeStruct(v.shape, v.dtype) for v in (keep, send)],
        input_output_aliases={4: 0, 5: 1},
        **kernel_params(8 * rows * height * height, 4 * rows * height),
    )


def together(*values):
    return lax.optimization_barrier(values)


def move(values, distance):
    size = lax.axis_size("dp")
    return lax.ppermute(values, "dp", [(i, i ^ distance) for i in range(size)])


def bit_of(distance):
    return (lax.axis_index("dp") // distance) % 2


def cut(values, index, parts):
    size = values.shape[0] // parts
    return lax.dynamic_slice_in_dim(values, index * size, size, 0)


def quarter(block):
    return cut(block, lax.axis_index("dp") % 4, 4)


def spread(piece):
    return piece, move(piece, 1), move(piece, 2), move(piece, 3)


def assemble(pieces):
    low, high = bit_of(1) == 1, bit_of(2) == 1
    first = [jnp.where(low, pieces[j ^ 1], pieces[j]) for j in range(4)]
    return jnp.concatenate([jnp.where(high, first[j ^ 2], first[j]) for j in range(4)], axis=0)


def in_order(bit, mine, other):
    return jnp.where(
        bit == 0,
        jnp.concatenate([mine, other], axis=0),
        jnp.concatenate([other, mine], axis=0),
    )


def added(first, second):
    return (first.astype(F32) + second.astype(F32)).astype(BF16)


class GradSum:
    def __init__(self, keep, send):
        self.keep, self.send = keep, send
        self.half = keep.shape[0] // 2
        self.bit = bit_of(1)
        size = lax.axis_size("dp")
        self.middle = [2**k for k in range(1, size.bit_length() - 2)]
        self.last = size // 2

    def start_first(self):
        keep_b, send_b = self.keep[self.half :], self.send[self.half :]
        out_a = swap(self.send[: self.half], "col")
        other = jnp.concatenate([cut(keep_b, 1 - self.bit, 2), cut(send_b, 1 - self.bit, 2)], axis=0)
        return out_a, move(other, 1)

    def start_second(self, arrived):
        from_col, from_dp = arrived
        keep_b, send_b = self.keep[self.half :], self.send[self.half :]
        quarter_rows = self.half // 2
        self.lower = added(cut(keep_b, self.bit, 2), from_dp[:quarter_rows])
        lower_send = added(cut(send_b, self.bit, 2), from_dp[quarter_rows:])
        keep_a = self.keep[: self.half]
        self.upper = added(cut(keep_a, self.bit, 2), cut(from_col, self.bit, 2))
        upper_send = added(cut(keep_a, 1 - self.bit, 2), cut(from_col, 1 - self.bit, 2))
        return swap(lower_send, "col"), move(upper_send, 1)

    def end_second(self, arrived):
        from_col, from_dp = arrived
        self.held = jnp.concatenate(
            [added(self.upper, from_dp), added(self.lower, from_col)], axis=0
        )

    def start_halving(self, distance):
        bit = bit_of(distance)
        self.kept = cut(self.held, bit, 2)
        return move(cut(self.held, 1 - bit, 2), distance)

    def end_halving(self, arrived):
        self.held = added(self.kept, arrived)

    def start_last(self):
        return move(self.held, self.last)

    def end_last(self, arrived):
        self.held = added(self.held, arrived)

    def start_doubling(self, distance):
        return move(self.held, distance)

    def end_doubling(self, distance, arrived):
        self.held = in_order(bit_of(distance), self.held, arrived)

    def start_whole(self):
        return move(self.held, 1)

    def end_whole(self, arrived):
        half = self.half // 2
        upper = in_order(self.bit, self.held[:half], arrived[:half])
        lower = in_order(self.bit, self.held[half:], arrived[half:])
        return jnp.concatenate([upper, lower], axis=0)


def per_device(
    tokens,
    cotangent,
    ln1_gain,
    ln1_bias,
    qkv_weight,
    qv_bias,
    out_weight,
    out_bias,
    ln2_gain,
    ln2_bias,
    fc1_weight,
    fc1_bias,
    fc2_weight,
    fc2_bias,
):
    col = lax.axis_index("col")
    col_scalar = jnp.full((1,), col, jnp.int32)
    half = tokens.shape[0] // 2
    qkv_cols = qkv_weight.shape[1]
    units = fc1_weight.shape[1]

    def give_half(block):
        return lax.dynamic_slice_in_dim(block, (1 - col) * half, half, 0)

    qkv_piece = swap(quarter(qkv_weight), "col")
    col_rows, row_values = pack_vectors(
        (ln1_gain, ln1_bias, ln2_gain, ln2_bias, out_bias, fc2_bias), qv_bias, fc1_bias
    )
    col_other = swap(col_rows, "col")
    row_other = swap(row_values, "row")
    qkv_swap = swap(qkv_weight, "row")
    fc1_out_give = jnp.concatenate([quarter(fc1_weight), quarter(out_weight)], axis=1)
    qkv_piece, col_other, row_other, token_give = together(
        qkv_piece, col_other, row_other, give_half(tokens)
    )
    qkv_pieces = spread(qkv_piece)
    token_other = swap(token_give, "col")
    vectors = jnp.concatenate([col_rows, col_other], axis=1)
    qkv_bias = jnp.concatenate([row_values[:, :qkv_cols], row_other[:, :qkv_cols]], axis=1)

    qkv_pieces, token_other, fc1_out_give, vectors, qkv_bias, fc2_give, cot_give = together(
        qkv_pieces,
        token_other,
        fc1_out_give,
        vectors,
        qkv_bias,
        cut(fc2_weight, bit_of(1), 2),
        give_half(cotangent),
    )
    qkv_far = assemble(qkv_pieces)
    qkv_far_swap = swap(qkv_far, "row")
    fc1_out_piece = swap(fc1_out_give, "col")
    qkv_blocks = [qkv_weight, qkv_swap, qkv_far, qkv_far_swap]
    stream, packed, normed1, end = widen_qkv(
        col_scalar, tokens, token_other, vectors, qkv_bias, qkv_blocks
    )

    end, fc1_out_piece, fc2_give = together(end, fc1_out_piece, fc2_give)
    fc1_out_pieces = spread(fc1_out_piece)
    fc2_piece = swap(fc2_give, "col")
    out_swap = swap(out_weight, "row")
    attended_mine, attended_away, probs, end = attend(packed, end)

    end, fc1_out_pieces, fc2_piece, out_swap, cot_give = together(
        end, fc1_out_pieces, fc2_piece, out_swap, cot_give
    )
    out_far = assemble([m[:, units:] for m in fc1_out_pieces])
    out_far_swap = swap(out_far, "row")
    fc2_wing = move(fc2_piece, 1)
    cot_other = swap(cot_give, "col")
    fc1_far = assemble([m[:, :units] for m in fc1_out_pieces])
    fc1_far_swap = swap(fc1_far, "row")
    fc1_swap = swap(fc1_weight, "row")
    out_blocks = [out_weight, out_far, out_swap, out_far_swap]
    middle, normed2, end = narrow_out(
        stream, attended_mine, attended_away, vectors, out_blocks, end
    )

    end, fc1_swap, fc1_far_swap, fc2_swap = together(end, fc1_swap, fc1_far_swap, fc2_weight)
    fc2_swap = swap(fc2_swap, "row")
    fc1_blocks = [fc1_weight, fc1_far, fc1_swap, fc1_far_swap]
    active, slope, active_far, slope_far, end = widen_gelu(
        normed2, fc1_blocks, row_values[:, qkv_cols:], row_other[:, qkv_cols:], end
    )

    end, fc2_piece, fc2_wing, fc2_swap, cot_other = together(
        end, fc2_piece, fc2_wing, fc2_swap, cot_other
    )
    fc2_away = in_order(bit_of(1), fc2_piece, fc2_wing)
    fc2_away_swap = swap(fc2_away, "row")
    active_other = swap(active_far, "row")
    upstream, fc2_bgrad, end = take_images(col_scalar, cotangent, cot_other, end)
    upstream_other = swap(upstream, "row")
    fc2_blocks = [fc2_weight, fc2_away, fc2_swap, fc2_away_swap]
    before_grad, before_sum, before_far, before_far_sum, end = widen_back(
        upstream, fc2_blocks, slope, slope_far, end
    )

    end, active_other, upstream_other = together(end, active_other, upstream_other)
    before_other = swap(before_far, "row")
    normed2_other = swap(normed2, "row")
    attended_other = swap(attended_away, "row")
    normed1_other = swap(normed1, "row")
    fc2_keep, fc2_send, end = weight_grad(
        active, active_other, upstream, upstream_other, 1, 512, after=end
    )

    sum2 = GradSum(fc2_keep, fc2_send)
    flying2 = sum2.start_first()
    middle_grad, middle_low, attended_grad, attended_grad_far, middle_sums, end = middle_back(
        before_grad,
        before_far,
        middle,
        upstream,
        vectors,
        [fc1_weight, fc1_swap, fc1_far, fc1_far_swap],
        out_blocks,
        end,
    )

    end, flying2, before_other, normed2_other, attended_other, normed1_other = together(
        end, flying2, before_other, normed2_other, attended_other, normed1_other
    )
    flying2 = sum2.start_second(flying2)
    middle_other = swap(middle_low, "row")
    fc1_keep, fc1_send, end = weight_grad(
        normed2, normed2_other, before_grad, before_other, 0, 768, more=384, after=end
    )

    end, flying2, middle_other = together(end, flying2, middle_other)
    sum2.end_second(flying2)
    middle_steps = sum2.middle
    for distance in middle_steps[:-1]:
        sum2.end_halving(sum2.start_halving(distance))
    flying2 = sum2.start_halving(middle_steps[-1])
    fc1_keep, fc1_send, end = out_weight_grad(
        attended_mine, attended_other, middle_low, middle_other, fc1_keep, fc1_send, end
    )

    end, flying2 = together(end, flying2)
    sum1 = GradSum(fc1_keep, fc1_send)
    flying1 = sum1.start_first()
    sum2.end_halving(flying2)
    flying2 = sum2.start_last()
    packed_grad, packed_grad_far, end = attend_back(
        packed, probs, attended_grad, attended_grad_far, end
    )

    end, flying1, flying2 = together(end, flying1, flying2)
    packed_other = swap(packed_grad_far, "row")
    flying1 = sum1.start_second(flying1)
    sum2.end_last(flying2)
    flying2 = sum2.start_doubling(middle_steps[-1])
    input_own, input_give, input_sums, packed_sums, end = input_back(
        packed_grad, packed_grad_far, stream, middle_grad, vectors, qkv_blocks, end
    )

    end, flying1, flying2, packed_other = together(end, flying1, flying2, packed_other)
    sum1.end_second(flying1)
    for distance in middle_steps[:-1]:
        sum1.end_halving(sum1.start_halving(distance))
    flying1 = sum1.start_halving(middle_steps[-1])
    sum2.end_doubling(middle_steps[-1], flying2)
    for distance in reversed(middle_steps[:-1]):
        sum2.end_doubling(distance, sum2.start_doubling(distance))
    flying2 = sum2.start_whole()
    kinds = packed_sums.reshape(-1, 3, HEAD)
    width = input_sums.shape[1]
    qv_grad = jnp.stack([kinds[:, 0], kinds[:, 2]], axis=1).reshape(2, -1, width)
    fc1_bgrad = jnp.stack([before_sum.reshape(-1, width), before_far_sum.reshape(-1, width)])
    by_row = jnp.concatenate([qv_grad, fc1_bgrad], axis=1)
    by_col = jnp.concatenate([input_sums, middle_sums, fc2_bgrad], axis=0)
    row_count = by_row.shape[1]
    small_other = swap(jnp.concatenate([by_row[1], by_col], axis=0), "row")
    qkv_keep, qkv_send, end = weight_grad(
        normed1, normed1_other, packed_grad, packed_other, 0, 384, EXTRA, after=end
    )

    end, flying1, small_other = together(end, flying1, small_other)
    by_row = (by_row[0] + small_other[:row_count]).reshape(-1, qkv_cols)
    by_col = by_col + small_other[row_count:]
    begin = qkv_keep.shape[0] - EXTRA
    both_cols = [
        jnp.concatenate([by_row, half_cols.reshape(-1, qkv_cols)], axis=0).astype(BF16)
        for half_cols in jnp.split(by_col, 2, axis=1)
    ]
    qkv_keep = lax.dynamic_update_slice(qkv_keep, both_cols[0], (begin, 0))
    qkv_send = lax.dynamic_update_slice(qkv_send, both_cols[1], (begin, 0))

    sum0 = GradSum(qkv_keep, qkv_send)
    flying0 = sum0.start_first()
    sum1.end_halving(flying1)
    flying1 = sum1.start_last()
    result_own, result_give, end = narrow_result(
        active, active_far, middle, vectors, fc2_blocks, end
    )

    flying0, result_give = together(flying0, result_give)
    flying0 = sum0.start_second(flying0)

    flying0, flying1, flying2, input_give = together(flying0, flying1, flying2, input_give)
    sum0.end_second(flying0)
    for distance in middle_steps[:-1]:
        sum0.end_halving(sum0.start_halving(distance))
    flying0 = sum0.start_halving(middle_steps[-1])
    sum1.end_last(flying1)
    flying1 = sum1.start_doubling(middle_steps[-1])
    input_other = swap(input_give, "col")
    fc2_wgrad = sum2.end_whole(flying2).astype(F32)

    (flying0,) = together(flying0)
    sum0.end_halving(flying0)
    flying0 = sum0.start_last()
    sum1.end_doubling(middle_steps[-1], flying1)
    for distance in reversed(middle_steps[:-1]):
        sum1.end_doubling(distance, sum1.start_doubling(distance))
    flying1 = sum1.start_whole()

    input_other, result_give = together(input_other, result_give)
    result_other = swap(result_give, "col")
    (flying0,) = together(flying0)
    sum0.end_last(flying0)
    flying0 = sum0.start_doubling(middle_steps[-1])
    input_grad = in_order(col, input_own, input_other.astype(F32))

    (flying0,) = together(flying0)
    sum0.end_doubling(middle_steps[-1], flying0)
    for distance in reversed(middle_steps[:-1]):
        sum0.end_doubling(distance, sum0.start_doubling(distance))
    flying0 = sum0.start_whole()
    fc1_out_grad = sum1.end_whole(flying1)
    result = in_order(col, result_own, result_other)
    qkv_whole = sum0.end_whole(flying0)
    qv_size = qv_bias.shape[0]
    rows_each = by_row.shape[0]
    vector_rows = qkv_whole[begin : begin + 2 * rows_each].astype(F32)
    by_row = vector_rows[:rows_each].reshape(-1)
    by_col = vector_rows[rows_each:].reshape(6, -1)
    return (
        result,
        input_grad,
        by_col[0],
        by_col[1],
        qkv_whole[:begin].astype(F32),
        by_row[:qv_size],
        fc1_out_grad[:, units:].astype(F32),
        by_col[4],
        by_col[2],
        by_col[3],
        fc1_out_grad[:, :units].astype(F32),
        by_row[qv_size:],
        fc2_wgrad,
        by_col[5],
    )


def solution(mesh):
    stream = P(("dp", "row"), "col")
    by_col, by_row = P("col"), P("row")
    wide, deep = P("col", "row"), P("row", "col")
    in_specs = (
        stream, stream, by_col, by_col, wide, by_row, deep, by_col,
        by_col, by_col, wide, by_row, deep, by_col,
    )
    return jax.shard_map(
        per_device, mesh=mesh, in_specs=in_specs, out_specs=in_specs, check_vma=False
    )
```

```python
from functools import partial

import jax
import jax.numpy as jnp
from jax import lax
from jax.experimental import pallas as pl
from jax.experimental.pallas import tpu as pltpu
from jax.sharding import PartitionSpec as P

HEAD = 64
SEQ = 197
PAD = 208
EXTRA = 32
EPSILON = 1e-06
LEFT_INNER = (((0,), (0,)), ((), ()))
RIGHT_INNER = (((1,), (1,)), ((), ()))
BF16 = jnp.bfloat16
F32 = jnp.float32


def swap(values, axis):
    return lax.ppermute(values, axis, [(0, 1), (1, 0)])


def matmul(left, right):
    return jnp.dot(left, right, preferred_element_type=F32)


def matmul_left(left, right):
    return lax.dot_general(left, right, LEFT_INNER, preferred_element_type=F32)


def matmul_right(left, right):
    return lax.dot_general(left, right, RIGHT_INNER, preferred_element_type=F32)


def split_pair(c0, c1, c2):
    low = lax.broadcasted_iota(jnp.int32, c0.shape, 1) < HEAD
    queries = jnp.where(low, c0, c1)
    key_rows = pltpu.roll(jnp.where(low, c2, c0), HEAD, 1)
    values = jnp.where(low, c1, c2)
    return queries, key_rows, values, low


def to_half(staged_ref, own_ref, far_ref):
    first_half = pl.program_id(0) < pl.num_programs(0) // 2

    @pl.when(first_half)
    def _():
        own_ref[...] = staged_ref[...]

    @pl.when(jnp.logical_not(first_half))
    def _():
        far_ref[...] = staged_ref[...]


def run_kernel(kernel, values, after, in_specs, out_specs, out_shape, **settings):
    values, after = list(values), jax.tree.leaves(after)
    count, skip = len(values), len(values) + len(after)
    outs = len(out_shape)

    def body(*refs):
        end_ref = refs[skip + outs]
        end_ref[...] = jnp.zeros_like(end_ref)
        kernel(*refs[:count], *refs[skip : skip + outs], *refs[skip + outs + 1 :])

    unread = [pl.BlockSpec(memory_space=pl.ANY)] * len(after)
    end = jax.ShapeDtypeStruct((8, 128), F32)
    return pl.pallas_call(
        body,
        in_specs=list(in_specs) + unread,
        out_specs=list(out_specs) + [whole_spec(end)],
        out_shape=list(out_shape) + [end],
        **settings,
    )(*values, *after)


def in_hbm(values):
    return pltpu.with_memory_space_constraint(values, pltpu.HBM)


def attend_kernel(packed_ref, own_ref, far_ref, probs_ref, staged_ref):
    images = packed_ref.shape[0] // PAD
    for image in range(images):
        rows = slice(image * PAD, (image + 1) * PAD)
        blocks = [packed_ref[rows, 128 * j : 128 * (j + 1)].astype(F32) for j in range(3)]
        queries, key_rows, values, low = split_pair(*blocks)
        keys_low = key_rows.astype(BF16)
        values_low = values.astype(BF16)
        outs = []
        for head in range(2):
            chosen = low if head == 0 else jnp.logical_not(low)
            masked = jnp.where(chosen, queries * HEAD**-0.5, 0.0).astype(BF16)
            scores = matmul_right(masked, keys_low)
            real = lax.broadcasted_iota(jnp.int32, scores.shape, 1) < SEQ
            scores = jnp.where(real, scores, -1e30)
            raised = jnp.exp(scores - jnp.max(scores, axis=1, keepdims=True))
            probs = (raised * (1.0 / jnp.sum(raised, axis=1, keepdims=True))).astype(BF16)
            probs_ref[0, image, head] = probs
            outs.append(matmul(probs, values_low))
        staged_ref[rows] = jnp.where(low, outs[0], outs[1]).astype(BF16)
    to_half(staged_ref, own_ref, far_ref)


def halves_specs(rows, width, steps):
    half = steps // 2
    return [
        pl.BlockSpec((rows, width), lambda p: (0, jnp.minimum(p, half - 1))),
        pl.BlockSpec((rows, width), lambda p: (0, jnp.maximum(p - half, 0))),
    ]


def attend(packed, after=()):
    rows, columns = packed.shape
    images, pairs = rows // PAD, columns // (6 * HEAD)
    return run_kernel(
        attend_kernel,
        [packed],
        after,
        grid=(pairs,),
        in_specs=[pl.BlockSpec((rows, 6 * HEAD), lambda p: (0, p))],
        out_specs=halves_specs(rows, 2 * HEAD, pairs)
        + [pl.BlockSpec((1, images, 2, PAD, PAD), lambda p: (p, 0, 0, 0, 0))],
        out_shape=[jax.ShapeDtypeStruct((rows, columns // 6), BF16)] * 2
        + [pltpu.HBM((pairs, images, 2, PAD, PAD), BF16)],
        scratch_shapes=[pltpu.VMEM((rows, 2 * HEAD), BF16)],
        compiler_params=pltpu.CompilerParams(vmem_limit_bytes=32 * 2**20),
        cost_estimate=pl.CostEstimate(flops=3 * 10**9, bytes_accessed=12 * 2**20, transcendentals=0),
    )


def attend_back_kernel(packed_ref, probs_ref, own_grad, far_grad, own_ref, far_ref, staged_ref):
    images = packed_ref.shape[0] // PAD
    first_half = pl.program_id(0) < pl.num_programs(0) // 2
    for image in range(images):
        rows = slice(image * PAD, (image + 1) * PAD)
        blocks = [packed_ref[rows, 128 * j : 128 * (j + 1)].astype(F32) for j in range(3)]
        queries, key_rows, values, low = split_pair(*blocks)
        values_low = values.astype(BF16)
        upstream = jnp.where(first_half, own_grad[rows].astype(F32), far_grad[rows].astype(F32))
        query_grad = key_grad = value_grad = 0.0
        for head in range(2):
            chosen = low if head == 0 else jnp.logical_not(low)
            up = jnp.where(chosen, upstream, 0.0).astype(BF16)
            query_head = jnp.where(chosen, queries * HEAD**-0.5, 0.0).astype(BF16)
            key_head = jnp.where(chosen, key_rows * HEAD**-0.5, 0.0).astype(BF16)
            probs = probs_ref[0, image, head]
            value_grad += matmul_left(probs, up)
            prob_grad = matmul_right(up, values_low)
            wide = probs.astype(F32)
            weighted = wide * prob_grad
            score_grad = (
                weighted - wide * jnp.sum(weighted, axis=1, keepdims=True)
            ).astype(BF16)
            query_grad += matmul(score_grad, key_head)
            key_grad += matmul_left(score_grad, query_head)
        key_turned = pltpu.roll(key_grad, HEAD, 1)
        staged_ref[rows, 0:128] = jnp.where(low, query_grad, key_turned).astype(BF16)
        staged_ref[rows, 128:256] = jnp.where(low, value_grad, query_grad).astype(BF16)
        staged_ref[rows, 256:384] = jnp.where(low, key_turned, value_grad).astype(BF16)
    to_half(staged_ref, own_ref, far_ref)


def attend_back(packed, probs, own_grad, far_grad, after=()):
    rows, columns = packed.shape
    images, pairs = rows // PAD, columns // (6 * HEAD)
    return run_kernel(
        attend_back_kernel,
        [packed, probs, own_grad, far_grad],
        after,
        grid=(pairs,),
        in_specs=[
            pl.BlockSpec((rows, 6 * HEAD), lambda p: (0, p)),
            pl.BlockSpec((1, images, 2, PAD, PAD), lambda p: (p, 0, 0, 0, 0)),
        ]
        + halves_specs(rows, 2 * HEAD, pairs),
        out_specs=halves_specs(rows, 6 * HEAD, pairs),
        out_shape=[jax.ShapeDtypeStruct((rows, columns // 2), BF16)] * 2,
        scratch_shapes=[pltpu.VMEM((rows, 6 * HEAD), BF16)],
        compiler_params=pltpu.CompilerParams(vmem_limit_bytes=32 * 2**20),
        cost_estimate=pl.CostEstimate(flops=8 * 10**9, bytes_accessed=16 * 2**20, transcendentals=0),
    )


def normalize(stream, gain_row, shift_row):
    row_mean = jnp.mean(stream, axis=1, keepdims=True)
    centred = stream - row_mean
    inverse = lax.rsqrt(jnp.mean(centred * centred, axis=1, keepdims=True) + EPSILON)
    unit_rows = centred * inverse
    return unit_rows, inverse, (unit_rows * gain_row + shift_row).astype(BF16)


def normalize_back(upstream, unit_rows, inverse, gain_row):
    scaled = upstream * gain_row
    first = jnp.mean(scaled, axis=1, keepdims=True)
    second = jnp.mean(scaled * unit_rows, axis=1, keepdims=True)
    return (
        inverse * (scaled - first - unit_rows * second),
        jnp.sum(upstream * unit_rows, axis=0, keepdims=True),
        jnp.sum(upstream, axis=0, keepdims=True),
    )


def side(first, second, axis):
    return jnp.concatenate([first[...], second[...]], axis=axis)


def whole_spec(values):
    return pl.BlockSpec(values.shape, lambda i: (0,) * len(values.shape))


def row_spec(values, steps):
    return pl.BlockSpec((values.shape[0] // steps, values.shape[1]), lambda i: (i, 0))


def kernel_params(flops, moved):
    return {
        "compiler_params": pltpu.CompilerParams(vmem_limit_bytes=24 * 2**20),
        "cost_estimate": pl.CostEstimate(flops=flops, bytes_accessed=moved, transcendentals=0),
    }


def pad_images(col_ref, block_ref, arrived_ref, out_ref, own_wide, arrived_wide):
    half, width = arrived_ref.shape
    images = half // SEQ
    own_wide[: 2 * half] = block_ref[...].astype(F32)
    arrived_wide[:half] = arrived_ref[...].astype(F32)
    real = lax.broadcasted_iota(jnp.int32, (PAD, width), 0) < SEQ
    for image in range(images):
        rows = slice(image * PAD, (image + 1) * PAD)
        source = image * SEQ
        out_ref[rows, width:] = jnp.where(real, arrived_wide[source : source + PAD], 0.0).astype(BF16)
        for place in range(2):

            @pl.when(col_ref[0] == place)
            def _():
                begin = place * half + source
                out_ref[rows, :width] = jnp.where(real, own_wide[begin : begin + PAD], 0.0).astype(BF16)


def pad_scratch(half, width):
    extra = -(2 * half) % 8 + 16
    return [pltpu.VMEM((2 * half + extra, width), F32), pltpu.VMEM((half + 16 - half % 8, width), F32)]


def take_kernel(col_ref, block_ref, arrived_ref, out_ref, sum_ref, own_wide, arrived_wide):
    pad_images(col_ref, block_ref, arrived_ref, out_ref, own_wide, arrived_wide)
    sum_ref[...] = jnp.sum(out_ref[...].astype(F32), axis=0, keepdims=True)


def take_images(col, block, arrived, after=()):
    half, width = arrived.shape
    rows = half // SEQ * PAD
    return run_kernel(
        take_kernel,
        [col, in_hbm(block), in_hbm(arrived)],
        after,
        grid=(1,),
        in_specs=[pl.BlockSpec(memory_space=pltpu.SMEM), whole_spec(block), whole_spec(arrived)],
        out_specs=[
            pl.BlockSpec((rows, 2 * width), lambda i: (0, 0)),
            pl.BlockSpec((1, 2 * width), lambda i: (0, 0)),
        ],
        out_shape=[
            jax.ShapeDtypeStruct((rows, 2 * width), BF16),
            jax.ShapeDtypeStruct((1, 2 * width), F32),
        ],
        scratch_shapes=pad_scratch(half, width),
        **kernel_params(10**6, 10 * half * width),
    )


def qkv_kernel(
    col_ref, block_ref, arrived_ref, vectors_ref, bias_ref, own, own_far, far, far_far,
    stream_ref, packed_ref, normed_ref, own_wide, arrived_wide,
):
    step, depth = packed_ref.shape[0], own.shape[0]

    @pl.when(pl.program_id(0) == 0)
    def _():
        pad_images(col_ref, block_ref, arrived_ref, stream_ref, own_wide, arrived_wide)

    begin = pl.multiple_of(pl.program_id(0) * step, 16)
    stream = stream_ref[pl.ds(begin, step)].astype(F32)
    normed = normalize(stream, vectors_ref[0:1], vectors_ref[1:2])[2]
    normed_ref[...] = normed
    columns = own.shape[1]
    packed = matmul(normed, side(own, far, 0)) + bias_ref[:, :columns]
    packed_ref[:, :columns] = packed.astype(BF16)
    packed = matmul(normed, side(own_far, far_far, 0)) + bias_ref[:, columns:]
    packed_ref[:, columns:] = packed.astype(BF16)


def widen_qkv(col, block, arrived, vectors, bias, blocks, after=()):
    half, width = arrived.shape
    rows, columns = half // SEQ * PAD, bias.shape[1]
    steps = 2
    stream = jax.ShapeDtypeStruct((rows, 2 * width), BF16)
    packed = jax.ShapeDtypeStruct((rows, columns), BF16)
    others = [in_hbm(block), in_hbm(arrived), vectors, bias, *blocks]
    return run_kernel(
        qkv_kernel,
        [col, *others],
        after,
        grid=(steps,),
        in_specs=[pl.BlockSpec(memory_space=pltpu.SMEM)] + [whole_spec(o) for o in others],
        out_specs=[whole_spec(stream), row_spec(packed, steps), row_spec(stream, steps)],
        out_shape=[pltpu.HBM(stream.shape, BF16), packed, pltpu.HBM(stream.shape, BF16)],
        scratch_shapes=pad_scratch(half, width),
        **kernel_params(4 * rows * width * columns, 8 * rows * width),
    )


def out_kernel(stream_ref, left_ref, right_ref, vectors_ref, own, own_far, far, far_far, middle_ref, normed_ref):
    attended = side(left_ref, right_ref, 1)
    branch = jnp.concatenate(
        [matmul(attended, side(own, far, 0)), matmul(attended, side(own_far, far_far, 0))], axis=1
    )
    middle = stream_ref[...].astype(F32) + branch + vectors_ref[4:5]
    middle_ref[...] = middle
    normed_ref[...] = normalize(middle, vectors_ref[2:3], vectors_ref[3:4])[2]


def narrow_out(stream, left, right, vectors, blocks, after=()):
    rows, width = stream.shape
    steps = 2
    others = [vectors, *blocks]
    return run_kernel(
        out_kernel,
        [stream, left, right, *others],
        after,
        grid=(steps,),
        in_specs=[row_spec(v, steps) for v in (stream, left, right)] + [whole_spec(o) for o in others],
        out_specs=[row_spec(stream, steps)] * 2,
        out_shape=[
            pltpu.HBM((rows, width), F32),
            jax.ShapeDtypeStruct((rows, width), BF16),
        ],
        **kernel_params(2 * rows * width * width, 10 * rows * width),
    )


def gelu_kernel(acts_ref, own_top, own_low, far_top, far_low, own_bias, far_bias, *outs):
    for top_ref, low_ref, bias_ref, active_ref, slope_ref in (
        (own_top, own_low, own_bias, outs[0], outs[1]),
        (far_top, far_low, far_bias, outs[2], outs[3]),
    ):
        weight = side(top_ref, low_ref, 0)
        for begin in range(0, acts_ref.shape[0], PAD):
            chunk = slice(begin, begin + PAD)
            before = matmul(acts_ref[chunk], weight) + bias_ref[...]
            bell = jnp.exp2((before * before) * -0.7213475204444817)
            size = 1.0 + (0.3275911 * 0.5**0.5) * jnp.abs(before)
            guess = pl.reciprocal(size, approx=True)
            inv = guess * (2.0 - size * guess)
            poly = -0.726576735 + inv * 0.5307027145
            poly = 0.7107068705 + inv * poly
            poly = -0.142248368 + inv * poly
            poly = (0.127414796 + inv * poly) * inv
            tail = poly * bell
            chance = jnp.where(before < 0, tail, 1.0 - tail)
            active_ref[chunk] = (before * chance).astype(BF16)
            slope_ref[chunk] = (chance + before * (bell * 0.3989422804014327)).astype(BF16)


def widen_gelu(acts, blocks, own_bias, far_bias, after=()):
    rows, depth = acts.shape
    units = own_bias.shape[1]
    tile = 256
    wide = pl.BlockSpec((depth // 2, tile), lambda j: (0, j))
    line = pl.BlockSpec((1, tile), lambda j: (0, j))
    out = pl.BlockSpec((rows, tile), lambda j: (0, j))
    return run_kernel(
        gelu_kernel,
        [acts, *blocks, own_bias, far_bias],
        after,
        grid=(units // tile,),
        in_specs=[whole_spec(acts)] + [wide] * 4 + [line] * 2,
        out_specs=[out] * 4,
        out_shape=[pltpu.HBM((rows, units), BF16)] * 4,
        **kernel_params(4 * rows * depth * units, 16 * rows * units),
    )


def slope_kernel(up_ref, own_left, own_right, far_left, far_right, own_slope, far_slope, *outs):
    for left_ref, right_ref, slope_ref, out_ref, sum_ref in (
        (own_left, own_right, own_slope, outs[0], outs[1]),
        (far_left, far_right, far_slope, outs[2], outs[3]),
    ):
        grad = matmul_right(up_ref[...], side(left_ref, right_ref, 1))
        low = (grad * slope_ref[...].astype(F32)).astype(BF16)
        out_ref[...] = low
        sum_ref[...] = jnp.sum(low.astype(F32), axis=0, keepdims=True)


def widen_back(upstream, blocks, own_slope, far_slope, after=()):
    rows, depth = upstream.shape
    units = own_slope.shape[1]
    tile = 256
    deep = pl.BlockSpec((tile, depth // 2), lambda j: (j, 0))
    line = pl.BlockSpec((1, tile), lambda j: (0, j))
    out = pl.BlockSpec((rows, tile), lambda j: (0, j))
    return run_kernel(
        slope_kernel,
        [upstream, *blocks, in_hbm(own_slope), in_hbm(far_slope)],
        after,
        grid=(units // tile,),
        in_specs=[whole_spec(upstream)] + [deep] * 4 + [out] * 2,
        out_specs=[out, line, out, line],
        out_shape=[
            pltpu.HBM((rows, units), BF16),
            jax.ShapeDtypeStruct((1, units), F32),
        ]
        * 2,
        **kernel_params(4 * rows * depth * units, 8 * rows * units),
    )


def pack_kernel(*refs):
    col_refs, (qv_ref, fc1_ref, col_out, row_out) = refs[:6], refs[6:]
    for i in range(6):
        col_out[i : i + 1] = col_refs[i][...].reshape(1, -1)
    low = lax.broadcasted_iota(jnp.int32, (1, 128), 1) < HEAD
    for pair in range(qv_ref.shape[0] // 256):
        first = qv_ref[256 * pair : 256 * pair + 128].reshape(1, -1)
        second = qv_ref[256 * pair + 128 : 256 * pair + 256].reshape(1, -1)
        turned = [pltpu.roll(r, HEAD, 1) for r in (first, second)]
        begin = 384 * pair
        row_out[:, begin : begin + 128] = jnp.where(low, first, 0.0)
        row_out[:, begin + 128 : begin + 256] = jnp.where(low, turned[0], turned[1])
        row_out[:, begin + 256 : begin + 384] = jnp.where(low, 0.0, second)
    packed = qv_ref.shape[0] * 3 // 2
    row_out[:, packed:] = fc1_ref[...].reshape(1, -1)


def pack_vectors(col_vectors, qv_bias, fc1_bias):
    values = [in_hbm(v) for v in (*col_vectors, qv_bias, fc1_bias)]
    width = qv_bias.shape[0] * 3 // 2 + fc1_bias.shape[0]
    outs = [
        jax.ShapeDtypeStruct((6, col_vectors[0].shape[0]), F32),
        jax.ShapeDtypeStruct((1, width), F32),
    ]
    return pl.pallas_call(
        pack_kernel,
        grid=(1,),
        in_specs=[whole_spec(v) for v in values],
        out_specs=[whole_spec(o) for o in outs],
        out_shape=outs,
        **kernel_params(1000, 50000),
    )(*values)


def middle_back_kernel(
    own_grad, far_grad, middle_ref, up_ref, vectors_ref,
    own, own_far, far, far_far, out_own, out_own_far, out_far, out_far_far,
    grad_ref, low_ref, own_out, far_out, sums_ref,
):
    left, right = own_grad[...], far_grad[...]
    normed_grad = jnp.concatenate(
        [
            matmul_right(left, own[...]) + matmul_right(right, own_far[...]),
            matmul_right(left, far[...]) + matmul_right(right, far_far[...]),
        ],
        axis=1,
    )
    unit, inverse, _ = normalize(middle_ref[...], vectors_ref[2:3], vectors_ref[3:4])
    part, gain_sum, shift_sum = normalize_back(normed_grad, unit, inverse, vectors_ref[2:3])
    grad = up_ref[...].astype(F32) + part
    low = grad.astype(BF16)
    grad_ref[...] = grad
    low_ref[...] = low
    own_out[...] = matmul_right(low, side(out_own, out_own_far, 1)).astype(BF16)
    far_out[...] = matmul_right(low, side(out_far, out_far_far, 1)).astype(BF16)
    sums = jnp.concatenate(
        [gain_sum, shift_sum, jnp.sum(low.astype(F32), axis=0, keepdims=True)], axis=0
    )

    @pl.when(pl.program_id(0) == 0)
    def _():
        sums_ref[...] = sums

    @pl.when(pl.program_id(0) > 0)
    def _():
        sums_ref[...] += sums


def middle_back(own_grad, far_grad, middle, upstream, vectors, fc1_blocks, out_blocks, after=()):
    rows, width = middle.shape
    steps = 2
    rowed = [own_grad, far_grad, middle, upstream]
    others = [vectors, *fc1_blocks, *out_blocks]
    head_cols = out_blocks[0].shape[0]
    low = jax.ShapeDtypeStruct((rows, width), BF16)
    heads = pltpu.HBM((rows, head_cols), BF16)
    sums = jax.ShapeDtypeStruct((3, width), F32)
    return run_kernel(
        middle_back_kernel,
        [*rowed, *others],
        after,
        grid=(steps,),
        in_specs=[row_spec(r, steps) for r in rowed] + [whole_spec(o) for o in others],
        out_specs=[row_spec(v, steps) for v in (middle, low, heads, heads)] + [whole_spec(sums)],
        out_shape=[pltpu.HBM((rows, width), F32), low, heads, heads, sums],
        **kernel_params(4 * rows * width * own_grad.shape[1], 24 * rows * width),
    )


def cut_images(index, images, values, wide_ref):
    for step in range(wide_ref.shape[0] // SEQ // images):

        @pl.when(index == step)
        def _():
            for image in range(images):
                begin = (step * images + image) * SEQ
                wide_ref[begin : begin + SEQ] = values[image * PAD : image * PAD + SEQ]


def input_back_kernel(
    own_grad, far_grad, stream_ref, middle_grad_ref, vectors_ref,
    own, own_far, far, far_far, keep_ref, give_ref, sums_ref, packed_sums_ref, give_wide,
):
    step = pl.program_id(0)
    images = stream_ref.shape[0] // PAD
    packed_grad = side(own_grad, far_grad, 1)
    normed_grad = jnp.concatenate(
        [
            matmul_right(packed_grad, side(own, own_far, 1)),
            matmul_right(packed_grad, side(far, far_far, 1)),
        ],
        axis=1,
    )
    unit, inverse, _ = normalize(stream_ref[...].astype(F32), vectors_ref[0:1], vectors_ref[1:2])
    part, gain_sum, shift_sum = normalize_back(normed_grad, unit, inverse, vectors_ref[0:1])
    grad = middle_grad_ref[...] + part
    width = keep_ref.shape[1]
    cut_images(step, images, grad[:, :width], keep_ref)
    cut_images(step, images, grad[:, width:], give_wide)
    sums = jnp.concatenate([gain_sum, shift_sum], axis=0)
    packed_sums = jnp.sum(packed_grad.astype(F32), axis=0, keepdims=True)

    @pl.when(step == 0)
    def _():
        sums_ref[...] = sums
        packed_sums_ref[...] = packed_sums

    @pl.when(step > 0)
    def _():
        sums_ref[...] += sums
        packed_sums_ref[...] += packed_sums

    @pl.when(step == pl.num_programs(0) - 1)
    def _():
        give_ref[...] = give_wide[...].astype(BF16)


def input_back(own_grad, far_grad, stream, middle_grad, vectors, blocks, after=()):
    rows, width = stream.shape
    steps = 2
    half = rows // PAD * SEQ
    rowed = [own_grad, far_grad, stream, middle_grad]
    others = [vectors, *blocks]
    outs = [
        pltpu.HBM((half, width // 2), F32),
        pltpu.HBM((half, width // 2), BF16),
        jax.ShapeDtypeStruct((2, width), F32),
        jax.ShapeDtypeStruct((1, 2 * own_grad.shape[1]), F32),
    ]
    return run_kernel(
        input_back_kernel,
        [*rowed, *others],
        after,
        grid=(steps,),
        in_specs=[row_spec(r, steps) for r in rowed] + [whole_spec(o) for o in others],
        out_specs=[whole_spec(o) for o in outs],
        out_shape=outs,
        scratch_shapes=[pltpu.VMEM((half, width // 2), F32)],
        **kernel_params(4 * rows * width * own_grad.shape[1], 20 * rows * width),
    )


def result_kernel(
    own_acts, far_acts, middle_ref, vectors_ref, own, own_far, far, far_far,
    keep_ref, give_ref, keep_wide, give_wide,
):
    step = pl.program_id(0)
    images = middle_ref.shape[0] // PAD
    width = keep_ref.shape[1]
    left, right = own_acts[...], far_acts[...]
    for weights, columns, wide_ref in (
        ((own, far), slice(0, width), keep_wide),
        ((own_far, far_far), slice(width, 2 * width), give_wide),
    ):
        branch = matmul(left, weights[0][...]) + matmul(right, weights[1][...])
        total = middle_ref[:, columns] + branch + vectors_ref[5:6, columns]
        cut_images(step, images, total, wide_ref)

    @pl.when(step == pl.num_programs(0) - 1)
    def _():
        keep_ref[...] = keep_wide[...].astype(BF16)
        give_ref[...] = give_wide[...].astype(BF16)


def narrow_result(own_acts, far_acts, middle, vectors, blocks, after=()):
    rows, width = middle.shape
    steps = 2
    half = rows // PAD * SEQ
    rowed = [in_hbm(own_acts), in_hbm(far_acts), middle]
    others = [vectors, *blocks]
    out = jax.ShapeDtypeStruct((half, width // 2), BF16)
    return run_kernel(
        result_kernel,
        [*rowed, *others],
        after,
        grid=(steps,),
        in_specs=[row_spec(r, steps) for r in rowed] + [whole_spec(o) for o in others],
        out_specs=[whole_spec(out)] * 2,
        out_shape=[out] * 2,
        scratch_shapes=[pltpu.VMEM((half, width // 2), F32)] * 2,
        **kernel_params(4 * rows * width * own_acts.shape[1], 12 * rows * width),
    )


def weight_grad_kernel(split_dim, left_own, left_other, right_own, right_other, keep_ref, send_ref):
    total = matmul_left(side(left_own, left_other, 0), side(right_own, right_other, 0))
    half = total.shape[split_dim] // 2
    if split_dim == 0:
        keep_ref[:half] = total[:half].astype(BF16)
        send_ref[:half] = total[half:].astype(BF16)
        extra = keep_ref.shape[0] - half
        if extra:
            keep_ref[half:] = jnp.zeros((extra, total.shape[1]), BF16)
            send_ref[half:] = jnp.zeros((extra, total.shape[1]), BF16)
    else:
        keep_ref[...] = total[:, :half].astype(BF16)
        send_ref[...] = total[:, half:].astype(BF16)


def weight_grad(left_own, left_other, right_own, right_other, split_dim, tile, extra=0, more=0, after=()):
    rows, height = left_own.shape
    width = right_own.shape[1]
    if split_dim == 0:
        left = pl.BlockSpec((rows, height), lambda j: (0, 0))
        right = pl.BlockSpec((rows, tile), lambda j: (0, j))
        out = pl.BlockSpec((height // 2 + extra, tile), lambda j: (0, j))
        shape, steps = (height // 2 + extra, width + more), width // tile
    else:
        left = pl.BlockSpec((rows, tile), lambda j: (0, j))
        right = pl.BlockSpec((rows, width), lambda j: (0, 0))
        out = pl.BlockSpec((tile, width // 2), lambda j: (j, 0))
        shape, steps = (height, width // 2), height // tile
    return run_kernel(
        partial(weight_grad_kernel, split_dim),
        [in_hbm(v) for v in (left_own, left_other, right_own, right_other)],
        after,
        grid=(steps,),
        in_specs=[left, left, right, right],
        out_specs=[out, out],
        out_shape=[jax.ShapeDtypeStruct(shape, BF16)] * 2,
        **kernel_params(
            4 * rows * height * width, 4 * rows * (height + width) + 3 * height * width
        ),
    )


def out_grad_kernel(left_own, left_other, right_own, right_other, keep_in, send_in, keep_ref, send_ref):
    total = matmul_left(side(left_own, left_other, 0), side(right_own, right_other, 0))
    half = total.shape[1] // 2
    keep_ref[...] = total[:, :half].astype(BF16)
    send_ref[...] = total[:, half:].astype(BF16)


def out_weight_grad(left_own, left_other, right_own, right_other, keep, send, after=()):
    rows, height = left_own.shape
    values = [in_hbm(v) for v in (left_own, left_other, right_own, right_other)]
    place = keep.shape[1] // height - 1
    out = pl.BlockSpec((height, height), lambda i: (0, place))
    unread = pl.BlockSpec(memory_space=pl.ANY)
    return run_kernel(
        out_grad_kernel,
        [*values, keep, send],
        after,
        grid=(1,),
        in_specs=[whole_spec(v) for v in values] + [unread, unread],
        out_specs=[out, out],
        out_shape=[jax.ShapeDtypeStruct(v.shape, v.dtype) for v in (keep, send)],
        input_output_aliases={4: 0, 5: 1},
        **kernel_params(8 * rows * height * height, 4 * rows * height),
    )


def together(*values):
    return lax.optimization_barrier(values)


def move(values, distance):
    size = lax.axis_size("dp")
    return lax.ppermute(values, "dp", [(i, i ^ distance) for i in range(size)])


def bit_of(distance):
    return (lax.axis_index("dp") // distance) % 2


def cut(values, index, parts):
    size = values.shape[0] // parts
    return lax.dynamic_slice_in_dim(values, index * size, size, 0)


def quarter(block):
    return cut(block, lax.axis_index("dp") % 4, 4)


def spread(piece):
    return piece, move(piece, 1), move(piece, 2), move(piece, 3)


def assemble(pieces):
    low, high = bit_of(1) == 1, bit_of(2) == 1
    first = [jnp.where(low, pieces[j ^ 1], pieces[j]) for j in range(4)]
    return jnp.concatenate([jnp.where(high, first[j ^ 2], first[j]) for j in range(4)], axis=0)


def in_order(bit, mine, other):
    return jnp.where(
        bit == 0,
        jnp.concatenate([mine, other], axis=0),
        jnp.concatenate([other, mine], axis=0),
    )


def added(first, second):
    return (first.astype(F32) + second.astype(F32)).astype(BF16)


class GradSum:
    def __init__(self, keep, send):
        self.keep, self.send = keep, send
        self.half = keep.shape[0] // 2
        self.bit = bit_of(1)
        size = lax.axis_size("dp")
        self.middle = [2**k for k in range(1, size.bit_length() - 2)]
        self.last = size // 2

    def start_first(self):
        keep_b, send_b = self.keep[self.half :], self.send[self.half :]
        out_a = swap(self.send[: self.half], "col")
        other = jnp.concatenate([cut(keep_b, 1 - self.bit, 2), cut(send_b, 1 - self.bit, 2)], axis=0)
        return out_a, move(other, 1)

    def start_second(self, arrived):
        from_col, from_dp = arrived
        keep_b, send_b = self.keep[self.half :], self.send[self.half :]
        quarter_rows = self.half // 2
        self.lower = added(cut(keep_b, self.bit, 2), from_dp[:quarter_rows])
        lower_send = added(cut(send_b, self.bit, 2), from_dp[quarter_rows:])
        keep_a = self.keep[: self.half]
        self.upper = added(cut(keep_a, self.bit, 2), cut(from_col, self.bit, 2))
        upper_send = added(cut(keep_a, 1 - self.bit, 2), cut(from_col, 1 - self.bit, 2))
        return swap(lower_send, "col"), move(upper_send, 1)

    def end_second(self, arrived):
        from_col, from_dp = arrived
        self.held = jnp.concatenate(
            [added(self.upper, from_dp), added(self.lower, from_col)], axis=0
        )

    def start_halving(self, distance):
        bit = bit_of(distance)
        self.kept = cut(self.held, bit, 2)
        return move(cut(self.held, 1 - bit, 2), distance)

    def end_halving(self, arrived):
        self.held = added(self.kept, arrived)

    def start_last(self):
        return move(self.held, self.last)

    def end_last(self, arrived):
        self.held = added(self.held, arrived)

    def start_doubling(self, distance):
        return move(self.held, distance)

    def end_doubling(self, distance, arrived):
        self.held = in_order(bit_of(distance), self.held, arrived)

    def start_whole(self):
        return move(self.held, 1)

    def end_whole(self, arrived):
        half = self.half // 2
        upper = in_order(self.bit, self.held[:half], arrived[:half])
        lower = in_order(self.bit, self.held[half:], arrived[half:])
        return jnp.concatenate([upper, lower], axis=0)


def per_device(
    tokens,
    cotangent,
    ln1_gain,
    ln1_bias,
    qkv_weight,
    qv_bias,
    out_weight,
    out_bias,
    ln2_gain,
    ln2_bias,
    fc1_weight,
    fc1_bias,
    fc2_weight,
    fc2_bias,
):
    col = lax.axis_index("col")
    col_scalar = jnp.full((1,), col, jnp.int32)
    half = tokens.shape[0] // 2
    qkv_cols = qkv_weight.shape[1]
    units = fc1_weight.shape[1]

    def give_half(block, place):
        return lax.dynamic_slice_in_dim(block, (1 - place) * half, half, 0)

    qkv_piece = swap(quarter(qkv_weight), "col")
    col_rows, row_values = pack_vectors(
        (ln1_gain, ln1_bias, ln2_gain, ln2_bias, out_bias, fc2_bias), qv_bias, fc1_bias
    )
    col_other = swap(col_rows, "col")
    row_other = swap(row_values, "row")
    qkv_swap = swap(qkv_weight, "row")
    qkv_piece, col_other, row_other, token_give = together(
        qkv_piece, col_other, row_other, give_half(tokens, col)
    )
    qkv_pieces = spread(qkv_piece)
    token_other = swap(token_give, "col")
    vectors = jnp.concatenate([col_rows, col_other], axis=1)
    qkv_bias = jnp.concatenate([row_values[:, :qkv_cols], row_other[:, :qkv_cols]], axis=1)

    first_piece, late_col, late_dp = together(qkv_pieces[1], col, lax.axis_index("dp"))
    qkv_pieces = (qkv_pieces[0], first_piece, *qkv_pieces[2:])
    fc1_give = cut(fc1_weight, late_dp % 4, 4)
    fc2_give = cut(fc2_weight, late_dp % 2, 2)
    cot_give = give_half(cotangent, late_col)
    qkv_pieces, token_other, fc1_give, vectors, qkv_bias, fc2_give, cot_give = together(
        qkv_pieces, token_other, fc1_give, vectors, qkv_bias, fc2_give, cot_give
    )
    qkv_far = assemble(qkv_pieces)
    qkv_far_swap = swap(qkv_far, "row")
    fc1_piece = swap(fc1_give, "col")
    qkv_blocks = [qkv_weight, qkv_swap, qkv_far, qkv_far_swap]
    stream, packed, normed1, end = widen_qkv(
        col_scalar, tokens, token_other, vectors, qkv_bias, qkv_blocks
    )

    end, fc1_piece, fc2_give, out_give = together(end, fc1_piece, fc2_give, out_weight)
    fc1_pieces = spread(fc1_piece)
    out_far = swap(out_give, "col")
    fc2_piece = swap(fc2_give, "col")
    out_swap = swap(out_weight, "row")
    attended_mine, attended_away, probs, end = attend(packed, end)

    end, fc1_pieces, out_far, out_swap = together(end, fc1_pieces, out_far, out_swap)
    out_far_swap = swap(out_far, "row")
    fc1_far = assemble(fc1_pieces)
    fc1_far_swap = swap(fc1_far, "row")
    fc1_swap = swap(fc1_weight, "row")
    out_blocks = [out_weight, out_far, out_swap, out_far_swap]
    middle, normed2, end = narrow_out(
        stream, attended_mine, attended_away, vectors, out_blocks, (end, fc2_piece)
    )

    end, fc1_swap, fc1_far_swap, fc2_piece, fc2_swap, cot_give = together(
        end, fc1_swap, fc1_far_swap, fc2_piece, fc2_weight, cot_give
    )
    fc2_wing = move(fc2_piece, 1)
    cot_other = swap(cot_give, "col")
    fc2_swap = swap(fc2_swap, "row")
    fc1_blocks = [fc1_weight, fc1_far, fc1_swap, fc1_far_swap]
    active, slope, active_far, slope_far, end = widen_gelu(
        normed2, fc1_blocks, row_values[:, qkv_cols:], row_other[:, qkv_cols:], end
    )

    end, fc2_piece, fc2_wing, fc2_swap, cot_other = together(
        end, fc2_piece, fc2_wing, fc2_swap, cot_other
    )
    fc2_away = in_order(bit_of(1), fc2_piece, fc2_wing)
    fc2_away_swap = swap(fc2_away, "row")
    active_other = swap(active_far, "row")
    upstream, fc2_bgrad, end = take_images(col_scalar, cotangent, cot_other, end)
    upstream_other = swap(upstream, "row")
    fc2_blocks = [fc2_weight, fc2_away, fc2_swap, fc2_away_swap]
    before_grad, before_sum, before_far, before_far_sum, end = widen_back(
        upstream, fc2_blocks, slope, slope_far, end
    )

    end, active_other, upstream_other = together(end, active_other, upstream_other)
    before_other = swap(before_far, "row")
    normed2_other = swap(normed2, "row")
    attended_other = swap(attended_away, "row")
    normed1_other = swap(normed1, "row")
    fc2_keep, fc2_send, end = weight_grad(
        active, active_other, upstream, upstream_other, 1, 512, after=end
    )

    sum2 = GradSum(fc2_keep, fc2_send)
    flying2 = sum2.start_first()
    middle_grad, middle_low, attended_grad, attended_grad_far, middle_sums, end = middle_back(
        before_grad,
        before_far,
        middle,
        upstream,
        vectors,
        [fc1_weight, fc1_swap, fc1_far, fc1_far_swap],
        out_blocks,
        end,
    )

    end, flying2, before_other, normed2_other, attended_other, normed1_other = together(
        end, flying2, before_other, normed2_other, attended_other, normed1_other
    )
    flying2 = sum2.start_second(flying2)
    middle_other = swap(middle_low, "row")
    fc1_keep, fc1_send, end = weight_grad(
        normed2, normed2_other, before_grad, before_other, 0, 768, more=384, after=end
    )

    end, flying2, middle_other = together(end, flying2, middle_other)
    sum2.end_second(flying2)
    middle_steps = sum2.middle
    for distance in middle_steps[:-1]:
        sum2.end_halving(sum2.start_halving(distance))
    flying2 = sum2.start_halving(middle_steps[-1])
    fc1_keep, fc1_send, end = out_weight_grad(
        attended_mine, attended_other, middle_low, middle_other, fc1_keep, fc1_send, end
    )

    end, flying2 = together(end, flying2)
    sum1 = GradSum(fc1_keep, fc1_send)
    flying1 = sum1.start_first()
    sum2.end_halving(flying2)
    flying2 = sum2.start_last()
    packed_grad, packed_grad_far, end = attend_back(
        packed, probs, attended_grad, attended_grad_far, end
    )

    end, flying1, flying2 = together(end, flying1, flying2)
    packed_other = swap(packed_grad_far, "row")
    flying1 = sum1.start_second(flying1)
    sum2.end_last(flying2)
    flying2 = sum2.start_doubling(middle_steps[-1])
    input_own, input_give, input_sums, packed_sums, end = input_back(
        packed_grad, packed_grad_far, stream, middle_grad, vectors, qkv_blocks, end
    )

    end, flying1, flying2, packed_other = together(end, flying1, flying2, packed_other)
    sum1.end_second(flying1)
    for distance in middle_steps[:-1]:
        sum1.end_halving(sum1.start_halving(distance))
    flying1 = sum1.start_halving(middle_steps[-1])
    sum2.end_doubling(middle_steps[-1], flying2)
    for distance in reversed(middle_steps[:-1]):
        sum2.end_doubling(distance, sum2.start_doubling(distance))
    flying2 = sum2.start_whole()
    kinds = packed_sums.reshape(-1, 3, HEAD)
    width = input_sums.shape[1]
    qv_grad = jnp.stack([kinds[:, 0], kinds[:, 2]], axis=1).reshape(2, -1, width)
    fc1_bgrad = jnp.stack([before_sum.reshape(-1, width), before_far_sum.reshape(-1, width)])
    by_row = jnp.concatenate([qv_grad, fc1_bgrad], axis=1)
    by_col = jnp.concatenate([input_sums, middle_sums, fc2_bgrad], axis=0)
    row_count = by_row.shape[1]
    small_other = swap(jnp.concatenate([by_row[1], by_col], axis=0), "row")
    qkv_keep, qkv_send, end = weight_grad(
        normed1, normed1_other, packed_grad, packed_other, 0, 384, EXTRA, after=end
    )

    end, flying1, small_other = together(end, flying1, small_other)
    by_row = (by_row[0] + small_other[:row_count]).reshape(-1, qkv_cols)
    by_col = by_col + small_other[row_count:]
    begin = qkv_keep.shape[0] - EXTRA
    both_cols = [
        jnp.concatenate([by_row, half_cols.reshape(-1, qkv_cols)], axis=0).astype(BF16)
        for half_cols in jnp.split(by_col, 2, axis=1)
    ]
    qkv_keep = lax.dynamic_update_slice(qkv_keep, both_cols[0], (begin, 0))
    qkv_send = lax.dynamic_update_slice(qkv_send, both_cols[1], (begin, 0))

    sum0 = GradSum(qkv_keep, qkv_send)
    flying0 = sum0.start_first()
    sum1.end_halving(flying1)
    flying1 = sum1.start_last()
    result_own, result_give, end = narrow_result(
        active, active_far, middle, vectors, fc2_blocks, end
    )

    flying0, result_give = together(flying0, result_give)
    flying0 = sum0.start_second(flying0)

    flying0, flying1, flying2, input_give = together(flying0, flying1, flying2, input_give)
    sum0.end_second(flying0)
    for distance in middle_steps[:-1]:
        sum0.end_halving(sum0.start_halving(distance))
    flying0 = sum0.start_halving(middle_steps[-1])
    sum1.end_last(flying1)
    flying1 = sum1.start_doubling(middle_steps[-1])
    input_other = swap(input_give, "col")
    fc2_wgrad = sum2.end_whole(flying2).astype(F32)

    (flying0,) = together(flying0)
    sum0.end_halving(flying0)
    flying0 = sum0.start_last()
    sum1.end_doubling(middle_steps[-1], flying1)
    for distance in reversed(middle_steps[:-1]):
        sum1.end_doubling(distance, sum1.start_doubling(distance))
    flying1 = sum1.start_whole()

    input_other, result_give = together(input_other, result_give)
    result_other = swap(result_give, "col")
    (flying0,) = together(flying0)
    sum0.end_last(flying0)
    flying0 = sum0.start_doubling(middle_steps[-1])
    input_grad = in_order(col, input_own, input_other.astype(F32))

    (flying0,) = together(flying0)
    sum0.end_doubling(middle_steps[-1], flying0)
    for distance in reversed(middle_steps[:-1]):
        sum0.end_doubling(distance, sum0.start_doubling(distance))
    flying0 = sum0.start_whole()
    fc1_out_grad = sum1.end_whole(flying1)
    result = in_order(col, result_own, result_other)
    fc1_wgrad = fc1_out_grad[:, :units].astype(F32)
    out_wgrad = fc1_out_grad[:, units:].astype(F32)
    flying0, result, fc1_wgrad, out_wgrad = together(flying0, result, fc1_wgrad, out_wgrad)
    qkv_whole = sum0.end_whole(flying0)
    qv_size = qv_bias.shape[0]
    rows_each = by_row.shape[0]
    vector_rows = qkv_whole[begin : begin + 2 * rows_each].astype(F32)
    by_row = vector_rows[:rows_each].reshape(-1)
    by_col = vector_rows[rows_each:].reshape(6, -1)
    return (
        result,
        input_grad,
        by_col[0],
        by_col[1],
        qkv_whole[:begin].astype(F32),
        by_row[:qv_size],
        out_wgrad,
        by_col[4],
        by_col[2],
        by_col[3],
        fc1_wgrad,
        by_row[qv_size:],
        fc2_wgrad,
        by_col[5],
    )


def solution(mesh):
    stream = P(("dp", "row"), "col")
    by_col, by_row = P("col"), P("row")
    wide, deep = P("col", "row"), P("row", "col")
    in_specs = (
        stream, stream, by_col, by_col, wide, by_row, deep, by_col,
        by_col, by_col, wide, by_row, deep, by_col,
    )
    return jax.shard_map(
        per_device, mesh=mesh, in_specs=in_specs, out_specs=in_specs, check_vma=False
    )
```

```python
from functools import partial

import jax
import jax.numpy as jnp
from jax import lax
from jax.experimental import pallas as pl
from jax.experimental.pallas import tpu as pltpu
from jax.sharding import PartitionSpec as P

HEAD = 64
SEQ = 197
PAD = 208
EXTRA = 32
EPSILON = 1e-06
LEFT_INNER = (((0,), (0,)), ((), ()))
RIGHT_INNER = (((1,), (1,)), ((), ()))
BF16 = jnp.bfloat16
F32 = jnp.float32


def swap(values, axis):
    return lax.ppermute(values, axis, [(0, 1), (1, 0)])


def matmul(left, right):
    return jnp.dot(left, right, preferred_element_type=F32)


def matmul_left(left, right):
    return lax.dot_general(left, right, LEFT_INNER, preferred_element_type=F32)


def matmul_right(left, right):
    return lax.dot_general(left, right, RIGHT_INNER, preferred_element_type=F32)


def split_pair(c0, c1, c2):
    low = lax.broadcasted_iota(jnp.int32, c0.shape, 1) < HEAD
    queries = jnp.where(low, c0, c1)
    key_rows = pltpu.roll(jnp.where(low, c2, c0), HEAD, 1)
    values = jnp.where(low, c1, c2)
    return queries, key_rows, values, low


def to_half(staged_ref, own_ref, far_ref):
    first_half = pl.program_id(0) < pl.num_programs(0) // 2

    @pl.when(first_half)
    def _():
        own_ref[...] = staged_ref[...]

    @pl.when(jnp.logical_not(first_half))
    def _():
        far_ref[...] = staged_ref[...]


def run_kernel(kernel, values, after, in_specs, out_specs, out_shape, **settings):
    values, after = list(values), jax.tree.leaves(after)
    count, skip = len(values), len(values) + len(after)
    outs = len(out_shape)

    def body(*refs):
        end_ref = refs[skip + outs]
        end_ref[...] = jnp.zeros_like(end_ref)
        kernel(*refs[:count], *refs[skip : skip + outs], *refs[skip + outs + 1 :])

    unread = [pl.BlockSpec(memory_space=pl.ANY)] * len(after)
    end = jax.ShapeDtypeStruct((8, 128), F32)
    return pl.pallas_call(
        body,
        in_specs=list(in_specs) + unread,
        out_specs=list(out_specs) + [whole_spec(end)],
        out_shape=list(out_shape) + [end],
        **settings,
    )(*values, *after)


def in_hbm(values):
    return pltpu.with_memory_space_constraint(values, pltpu.HBM)


def attend_kernel(packed_ref, own_ref, far_ref, probs_ref, staged_ref):
    images = packed_ref.shape[0] // PAD
    for image in range(images):
        rows = slice(image * PAD, (image + 1) * PAD)
        blocks = [packed_ref[rows, 128 * j : 128 * (j + 1)].astype(F32) for j in range(3)]
        queries, key_rows, values, low = split_pair(*blocks)
        keys_low = key_rows.astype(BF16)
        values_low = values.astype(BF16)
        outs = []
        for head in range(2):
            chosen = low if head == 0 else jnp.logical_not(low)
            masked = jnp.where(chosen, queries * HEAD**-0.5, 0.0).astype(BF16)
            scores = matmul_right(masked, keys_low)
            real = lax.broadcasted_iota(jnp.int32, scores.shape, 1) < SEQ
            scores = jnp.where(real, scores, -1e30)
            raised = jnp.exp(scores - jnp.max(scores, axis=1, keepdims=True))
            probs = (raised * (1.0 / jnp.sum(raised, axis=1, keepdims=True))).astype(BF16)
            probs_ref[0, image, head] = probs
            outs.append(matmul(probs, values_low))
        staged_ref[rows] = jnp.where(low, outs[0], outs[1]).astype(BF16)
    to_half(staged_ref, own_ref, far_ref)


def halves_specs(rows, width, steps):
    half = steps // 2
    return [
        pl.BlockSpec((rows, width), lambda p: (0, jnp.minimum(p, half - 1))),
        pl.BlockSpec((rows, width), lambda p: (0, jnp.maximum(p - half, 0))),
    ]


def attend(packed, after=()):
    rows, columns = packed.shape
    images, pairs = rows // PAD, columns // (6 * HEAD)
    return run_kernel(
        attend_kernel,
        [packed],
        after,
        grid=(pairs,),
        in_specs=[pl.BlockSpec((rows, 6 * HEAD), lambda p: (0, p))],
        out_specs=halves_specs(rows, 2 * HEAD, pairs)
        + [pl.BlockSpec((1, images, 2, PAD, PAD), lambda p: (p, 0, 0, 0, 0))],
        out_shape=[jax.ShapeDtypeStruct((rows, columns // 6), BF16)] * 2
        + [pltpu.HBM((pairs, images, 2, PAD, PAD), BF16)],
        scratch_shapes=[pltpu.VMEM((rows, 2 * HEAD), BF16)],
        compiler_params=pltpu.CompilerParams(vmem_limit_bytes=32 * 2**20),
        cost_estimate=pl.CostEstimate(flops=3 * 10**9, bytes_accessed=12 * 2**20, transcendentals=0),
    )


def attend_back_kernel(packed_ref, probs_ref, own_grad, far_grad, own_ref, far_ref, staged_ref):
    images = packed_ref.shape[0] // PAD
    first_half = pl.program_id(0) < pl.num_programs(0) // 2
    for image in range(images):
        rows = slice(image * PAD, (image + 1) * PAD)
        blocks = [packed_ref[rows, 128 * j : 128 * (j + 1)].astype(F32) for j in range(3)]
        queries, key_rows, values, low = split_pair(*blocks)
        values_low = values.astype(BF16)
        upstream = jnp.where(first_half, own_grad[rows].astype(F32), far_grad[rows].astype(F32))
        query_grad = key_grad = value_grad = 0.0
        for head in range(2):
            chosen = low if head == 0 else jnp.logical_not(low)
            up = jnp.where(chosen, upstream, 0.0).astype(BF16)
            query_head = jnp.where(chosen, queries * HEAD**-0.5, 0.0).astype(BF16)
            key_head = jnp.where(chosen, key_rows * HEAD**-0.5, 0.0).astype(BF16)
            probs = probs_ref[0, image, head]
            value_grad += matmul_left(probs, up)
            prob_grad = matmul_right(up, values_low)
            wide = probs.astype(F32)
            weighted = wide * prob_grad
            score_grad = (
                weighted - wide * jnp.sum(weighted, axis=1, keepdims=True)
            ).astype(BF16)
            query_grad += matmul(score_grad, key_head)
            key_grad += matmul_left(score_grad, query_head)
        key_turned = pltpu.roll(key_grad, HEAD, 1)
        staged_ref[rows, 0:128] = jnp.where(low, query_grad, key_turned).astype(BF16)
        staged_ref[rows, 128:256] = jnp.where(low, value_grad, query_grad).astype(BF16)
        staged_ref[rows, 256:384] = jnp.where(low, key_turned, value_grad).astype(BF16)
    to_half(staged_ref, own_ref, far_ref)


def attend_back(packed, probs, own_grad, far_grad, after=()):
    rows, columns = packed.shape
    images, pairs = rows // PAD, columns // (6 * HEAD)
    return run_kernel(
        attend_back_kernel,
        [packed, probs, own_grad, far_grad],
        after,
        grid=(pairs,),
        in_specs=[
            pl.BlockSpec((rows, 6 * HEAD), lambda p: (0, p)),
            pl.BlockSpec((1, images, 2, PAD, PAD), lambda p: (p, 0, 0, 0, 0)),
        ]
        + halves_specs(rows, 2 * HEAD, pairs),
        out_specs=halves_specs(rows, 6 * HEAD, pairs),
        out_shape=[jax.ShapeDtypeStruct((rows, columns // 2), BF16)] * 2,
        scratch_shapes=[pltpu.VMEM((rows, 6 * HEAD), BF16)],
        compiler_params=pltpu.CompilerParams(vmem_limit_bytes=32 * 2**20),
        cost_estimate=pl.CostEstimate(flops=8 * 10**9, bytes_accessed=16 * 2**20, transcendentals=0),
    )


def normalize(stream, gain_row, shift_row):
    row_mean = jnp.mean(stream, axis=1, keepdims=True)
    centred = stream - row_mean
    inverse = lax.rsqrt(jnp.mean(centred * centred, axis=1, keepdims=True) + EPSILON)
    unit_rows = centred * inverse
    return unit_rows, inverse, (unit_rows * gain_row + shift_row).astype(BF16)


def normalize_back(upstream, unit_rows, inverse, gain_row):
    scaled = upstream * gain_row
    first = jnp.mean(scaled, axis=1, keepdims=True)
    second = jnp.mean(scaled * unit_rows, axis=1, keepdims=True)
    return (
        inverse * (scaled - first - unit_rows * second),
        jnp.sum(upstream * unit_rows, axis=0, keepdims=True),
        jnp.sum(upstream, axis=0, keepdims=True),
    )


def side(first, second, axis):
    return jnp.concatenate([first[...], second[...]], axis=axis)


def whole_spec(values):
    return pl.BlockSpec(values.shape, lambda i: (0,) * len(values.shape))


def row_spec(values, steps):
    return pl.BlockSpec((values.shape[0] // steps, values.shape[1]), lambda i: (i, 0))


def kernel_params(flops, moved):
    return {
        "compiler_params": pltpu.CompilerParams(vmem_limit_bytes=24 * 2**20),
        "cost_estimate": pl.CostEstimate(flops=flops, bytes_accessed=moved, transcendentals=0),
    }


def pad_images(col_ref, block_ref, arrived_ref, out_ref, own_wide, arrived_wide):
    half, width = arrived_ref.shape
    images = half // SEQ
    own_wide[: 2 * half] = block_ref[...].astype(F32)
    arrived_wide[:half] = arrived_ref[...].astype(F32)
    real = lax.broadcasted_iota(jnp.int32, (PAD, width), 0) < SEQ
    for image in range(images):
        rows = slice(image * PAD, (image + 1) * PAD)
        source = image * SEQ
        out_ref[rows, width:] = jnp.where(real, arrived_wide[source : source + PAD], 0.0).astype(BF16)
        for place in range(2):

            @pl.when(col_ref[0] == place)
            def _():
                begin = place * half + source
                out_ref[rows, :width] = jnp.where(real, own_wide[begin : begin + PAD], 0.0).astype(BF16)


def pad_scratch(half, width):
    extra = -(2 * half) % 8 + 16
    return [pltpu.VMEM((2 * half + extra, width), F32), pltpu.VMEM((half + 16 - half % 8, width), F32)]


def take_kernel(col_ref, block_ref, arrived_ref, out_ref, sum_ref, own_wide, arrived_wide):
    pad_images(col_ref, block_ref, arrived_ref, out_ref, own_wide, arrived_wide)
    sum_ref[...] = jnp.sum(out_ref[...].astype(F32), axis=0, keepdims=True)


def take_images(col, block, arrived, after=()):
    half, width = arrived.shape
    rows = half // SEQ * PAD
    return run_kernel(
        take_kernel,
        [col, in_hbm(block), in_hbm(arrived)],
        after,
        grid=(1,),
        in_specs=[pl.BlockSpec(memory_space=pltpu.SMEM), whole_spec(block), whole_spec(arrived)],
        out_specs=[
            pl.BlockSpec((rows, 2 * width), lambda i: (0, 0)),
            pl.BlockSpec((1, 2 * width), lambda i: (0, 0)),
        ],
        out_shape=[
            jax.ShapeDtypeStruct((rows, 2 * width), BF16),
            jax.ShapeDtypeStruct((1, 2 * width), F32),
        ],
        scratch_shapes=pad_scratch(half, width),
        **kernel_params(10**6, 10 * half * width),
    )


def qkv_kernel(
    col_ref, block_ref, arrived_ref, vectors_ref, bias_ref, own, own_far, far, far_far,
    stream_ref, packed_ref, normed_ref, own_wide, arrived_wide,
):
    step, depth = packed_ref.shape[0], own.shape[0]

    @pl.when(pl.program_id(0) == 0)
    def _():
        pad_images(col_ref, block_ref, arrived_ref, stream_ref, own_wide, arrived_wide)

    begin = pl.multiple_of(pl.program_id(0) * step, 16)
    stream = stream_ref[pl.ds(begin, step)].astype(F32)
    normed = normalize(stream, vectors_ref[0:1], vectors_ref[1:2])[2]
    normed_ref[...] = normed
    columns = own.shape[1]
    packed = matmul(normed, side(own, far, 0)) + bias_ref[:, :columns]
    packed_ref[:, :columns] = packed.astype(BF16)
    packed = matmul(normed, side(own_far, far_far, 0)) + bias_ref[:, columns:]
    packed_ref[:, columns:] = packed.astype(BF16)


def widen_qkv(col, block, arrived, vectors, bias, blocks, after=()):
    half, width = arrived.shape
    rows, columns = half // SEQ * PAD, bias.shape[1]
    steps = 2
    stream = jax.ShapeDtypeStruct((rows, 2 * width), BF16)
    packed = jax.ShapeDtypeStruct((rows, columns), BF16)
    others = [in_hbm(block), in_hbm(arrived), vectors, bias, *blocks]
    return run_kernel(
        qkv_kernel,
        [col, *others],
        after,
        grid=(steps,),
        in_specs=[pl.BlockSpec(memory_space=pltpu.SMEM)] + [whole_spec(o) for o in others],
        out_specs=[whole_spec(stream), row_spec(packed, steps), row_spec(stream, steps)],
        out_shape=[pltpu.HBM(stream.shape, BF16), packed, pltpu.HBM(stream.shape, BF16)],
        scratch_shapes=pad_scratch(half, width),
        **kernel_params(4 * rows * width * columns, 8 * rows * width),
    )


def out_kernel(stream_ref, left_ref, right_ref, vectors_ref, own, own_far, far, far_far, middle_ref, normed_ref):
    attended = side(left_ref, right_ref, 1)
    branch = jnp.concatenate(
        [matmul(attended, side(own, far, 0)), matmul(attended, side(own_far, far_far, 0))], axis=1
    )
    middle = stream_ref[...].astype(F32) + branch + vectors_ref[4:5]
    middle_ref[...] = middle
    normed_ref[...] = normalize(middle, vectors_ref[2:3], vectors_ref[3:4])[2]


def narrow_out(stream, left, right, vectors, blocks, after=()):
    rows, width = stream.shape
    steps = 2
    others = [vectors, *blocks]
    return run_kernel(
        out_kernel,
        [stream, left, right, *others],
        after,
        grid=(steps,),
        in_specs=[row_spec(v, steps) for v in (stream, left, right)] + [whole_spec(o) for o in others],
        out_specs=[row_spec(stream, steps)] * 2,
        out_shape=[
            pltpu.HBM((rows, width), F32),
            jax.ShapeDtypeStruct((rows, width), BF16),
        ],
        **kernel_params(2 * rows * width * width, 10 * rows * width),
    )


def gelu_kernel(acts_ref, own_top, own_low, far_top, far_low, own_bias, far_bias, *outs):
    for top_ref, low_ref, bias_ref, active_ref, slope_ref in (
        (own_top, own_low, own_bias, outs[0], outs[1]),
        (far_top, far_low, far_bias, outs[2], outs[3]),
    ):
        weight = side(top_ref, low_ref, 0)
        for begin in range(0, acts_ref.shape[0], PAD):
            chunk = slice(begin, begin + PAD)
            before = matmul(acts_ref[chunk], weight) + bias_ref[...]
            bell = jnp.exp2((before * before) * -0.7213475204444817)
            size = 1.0 + (0.3275911 * 0.5**0.5) * jnp.abs(before)
            guess = pl.reciprocal(size, approx=True)
            inv = guess * (2.0 - size * guess)
            poly = -0.726576735 + inv * 0.5307027145
            poly = 0.7107068705 + inv * poly
            poly = -0.142248368 + inv * poly
            poly = (0.127414796 + inv * poly) * inv
            tail = poly * bell
            chance = jnp.where(before < 0, tail, 1.0 - tail)
            active_ref[chunk] = (before * chance).astype(BF16)
            slope_ref[chunk] = (chance + before * (bell * 0.3989422804014327)).astype(BF16)


def widen_gelu(acts, blocks, own_bias, far_bias, after=()):
    rows, depth = acts.shape
    units = own_bias.shape[1]
    tile = 256
    wide = pl.BlockSpec((depth // 2, tile), lambda j: (0, j))
    line = pl.BlockSpec((1, tile), lambda j: (0, j))
    out = pl.BlockSpec((rows, tile), lambda j: (0, j))
    return run_kernel(
        gelu_kernel,
        [acts, *blocks, own_bias, far_bias],
        after,
        grid=(units // tile,),
        in_specs=[whole_spec(acts)] + [wide] * 4 + [line] * 2,
        out_specs=[out] * 4,
        out_shape=[pltpu.HBM((rows, units), BF16)] * 4,
        **kernel_params(4 * rows * depth * units, 16 * rows * units),
    )


def slope_kernel(up_ref, own_left, own_right, far_left, far_right, own_slope, far_slope, *outs):
    for left_ref, right_ref, slope_ref, out_ref, sum_ref in (
        (own_left, own_right, own_slope, outs[0], outs[1]),
        (far_left, far_right, far_slope, outs[2], outs[3]),
    ):
        grad = matmul_right(up_ref[...], side(left_ref, right_ref, 1))
        low = (grad * slope_ref[...].astype(F32)).astype(BF16)
        out_ref[...] = low
        sum_ref[...] = jnp.sum(low.astype(F32), axis=0, keepdims=True)


def widen_back(upstream, blocks, own_slope, far_slope, after=()):
    rows, depth = upstream.shape
    units = own_slope.shape[1]
    tile = 256
    deep = pl.BlockSpec((tile, depth // 2), lambda j: (j, 0))
    line = pl.BlockSpec((1, tile), lambda j: (0, j))
    out = pl.BlockSpec((rows, tile), lambda j: (0, j))
    return run_kernel(
        slope_kernel,
        [upstream, *blocks, in_hbm(own_slope), in_hbm(far_slope)],
        after,
        grid=(units // tile,),
        in_specs=[whole_spec(upstream)] + [deep] * 4 + [out] * 2,
        out_specs=[out, line, out, line],
        out_shape=[
            pltpu.HBM((rows, units), BF16),
            jax.ShapeDtypeStruct((1, units), F32),
        ]
        * 2,
        **kernel_params(4 * rows * depth * units, 8 * rows * units),
    )


def pack_kernel(*refs):
    col_refs, (qv_ref, fc1_ref, col_out, row_out) = refs[:6], refs[6:]
    for i in range(6):
        col_out[i : i + 1] = col_refs[i][...].reshape(1, -1)
    low = lax.broadcasted_iota(jnp.int32, (1, 128), 1) < HEAD
    for pair in range(qv_ref.shape[0] // 256):
        first = qv_ref[256 * pair : 256 * pair + 128].reshape(1, -1)
        second = qv_ref[256 * pair + 128 : 256 * pair + 256].reshape(1, -1)
        turned = [pltpu.roll(r, HEAD, 1) for r in (first, second)]
        begin = 384 * pair
        row_out[:, begin : begin + 128] = jnp.where(low, first, 0.0)
        row_out[:, begin + 128 : begin + 256] = jnp.where(low, turned[0], turned[1])
        row_out[:, begin + 256 : begin + 384] = jnp.where(low, 0.0, second)
    packed = qv_ref.shape[0] * 3 // 2
    row_out[:, packed:] = fc1_ref[...].reshape(1, -1)


def pack_vectors(col_vectors, qv_bias, fc1_bias):
    values = [in_hbm(v) for v in (*col_vectors, qv_bias, fc1_bias)]
    width = qv_bias.shape[0] * 3 // 2 + fc1_bias.shape[0]
    outs = [
        jax.ShapeDtypeStruct((6, col_vectors[0].shape[0]), F32),
        jax.ShapeDtypeStruct((1, width), F32),
    ]
    return pl.pallas_call(
        pack_kernel,
        grid=(1,),
        in_specs=[whole_spec(v) for v in values],
        out_specs=[whole_spec(o) for o in outs],
        out_shape=outs,
        **kernel_params(1000, 50000),
    )(*values)


def middle_back_kernel(
    own_grad, far_grad, middle_ref, up_ref, vectors_ref,
    own, own_far, far, far_far, out_own, out_own_far, out_far, out_far_far,
    grad_ref, low_ref, own_out, far_out, sums_ref,
):
    left, right = own_grad[...], far_grad[...]
    normed_grad = jnp.concatenate(
        [
            matmul_right(left, own[...]) + matmul_right(right, own_far[...]),
            matmul_right(left, far[...]) + matmul_right(right, far_far[...]),
        ],
        axis=1,
    )
    unit, inverse, _ = normalize(middle_ref[...], vectors_ref[2:3], vectors_ref[3:4])
    part, gain_sum, shift_sum = normalize_back(normed_grad, unit, inverse, vectors_ref[2:3])
    grad = up_ref[...].astype(F32) + part
    low = grad.astype(BF16)
    grad_ref[...] = grad
    low_ref[...] = low
    own_out[...] = matmul_right(low, side(out_own, out_own_far, 1)).astype(BF16)
    far_out[...] = matmul_right(low, side(out_far, out_far_far, 1)).astype(BF16)
    sums = jnp.concatenate(
        [gain_sum, shift_sum, jnp.sum(low.astype(F32), axis=0, keepdims=True)], axis=0
    )

    @pl.when(pl.program_id(0) == 0)
    def _():
        sums_ref[...] = sums

    @pl.when(pl.program_id(0) > 0)
    def _():
        sums_ref[...] += sums


def middle_back(own_grad, far_grad, middle, upstream, vectors, fc1_blocks, out_blocks, after=()):
    rows, width = middle.shape
    steps = 2
    rowed = [own_grad, far_grad, middle, upstream]
    others = [vectors, *fc1_blocks, *out_blocks]
    head_cols = out_blocks[0].shape[0]
    low = jax.ShapeDtypeStruct((rows, width), BF16)
    heads = pltpu.HBM((rows, head_cols), BF16)
    sums = jax.ShapeDtypeStruct((3, width), F32)
    return run_kernel(
        middle_back_kernel,
        [*rowed, *others],
        after,
        grid=(steps,),
        in_specs=[row_spec(r, steps) for r in rowed] + [whole_spec(o) for o in others],
        out_specs=[row_spec(v, steps) for v in (middle, low, heads, heads)] + [whole_spec(sums)],
        out_shape=[pltpu.HBM((rows, width), F32), low, heads, heads, sums],
        **kernel_params(4 * rows * width * own_grad.shape[1], 24 * rows * width),
    )


def cut_images(index, images, values, wide_ref):
    for step in range(wide_ref.shape[0] // SEQ // images):

        @pl.when(index == step)
        def _():
            for image in range(images):
                begin = (step * images + image) * SEQ
                wide_ref[begin : begin + SEQ] = values[image * PAD : image * PAD + SEQ]


def input_back_kernel(
    own_grad, far_grad, stream_ref, middle_grad_ref, vectors_ref,
    own, own_far, far, far_far, keep_ref, give_ref, sums_ref, packed_sums_ref, give_wide,
):
    step = pl.program_id(0)
    images = stream_ref.shape[0] // PAD
    packed_grad = side(own_grad, far_grad, 1)
    normed_grad = jnp.concatenate(
        [
            matmul_right(packed_grad, side(own, own_far, 1)),
            matmul_right(packed_grad, side(far, far_far, 1)),
        ],
        axis=1,
    )
    unit, inverse, _ = normalize(stream_ref[...].astype(F32), vectors_ref[0:1], vectors_ref[1:2])
    part, gain_sum, shift_sum = normalize_back(normed_grad, unit, inverse, vectors_ref[0:1])
    grad = middle_grad_ref[...] + part
    width = keep_ref.shape[1]
    cut_images(step, images, grad[:, :width], keep_ref)
    cut_images(step, images, grad[:, width:], give_wide)
    sums = jnp.concatenate([gain_sum, shift_sum], axis=0)
    packed_sums = jnp.sum(packed_grad.astype(F32), axis=0, keepdims=True)

    @pl.when(step == 0)
    def _():
        sums_ref[...] = sums
        packed_sums_ref[...] = packed_sums

    @pl.when(step > 0)
    def _():
        sums_ref[...] += sums
        packed_sums_ref[...] += packed_sums

    @pl.when(step == pl.num_programs(0) - 1)
    def _():
        give_ref[...] = give_wide[...].astype(BF16)


def input_back(own_grad, far_grad, stream, middle_grad, vectors, blocks, after=()):
    rows, width = stream.shape
    steps = 2
    half = rows // PAD * SEQ
    rowed = [own_grad, far_grad, stream, middle_grad]
    others = [vectors, *blocks]
    outs = [
        pltpu.HBM((half, width // 2), F32),
        pltpu.HBM((half, width // 2), BF16),
        jax.ShapeDtypeStruct((2, width), F32),
        jax.ShapeDtypeStruct((1, 2 * own_grad.shape[1]), F32),
    ]
    return run_kernel(
        input_back_kernel,
        [*rowed, *others],
        after,
        grid=(steps,),
        in_specs=[row_spec(r, steps) for r in rowed] + [whole_spec(o) for o in others],
        out_specs=[whole_spec(o) for o in outs],
        out_shape=outs,
        scratch_shapes=[pltpu.VMEM((half, width // 2), F32)],
        **kernel_params(4 * rows * width * own_grad.shape[1], 20 * rows * width),
    )


def result_kernel(
    own_acts, far_acts, middle_ref, vectors_ref, own, own_far, far, far_far,
    keep_ref, give_ref, keep_wide, give_wide,
):
    step = pl.program_id(0)
    images = middle_ref.shape[0] // PAD
    width = keep_ref.shape[1]
    left, right = own_acts[...], far_acts[...]
    for weights, columns, wide_ref in (
        ((own, far), slice(0, width), keep_wide),
        ((own_far, far_far), slice(width, 2 * width), give_wide),
    ):
        branch = matmul(left, weights[0][...]) + matmul(right, weights[1][...])
        total = middle_ref[:, columns] + branch + vectors_ref[5:6, columns]
        cut_images(step, images, total, wide_ref)

    @pl.when(step == pl.num_programs(0) - 1)
    def _():
        keep_ref[...] = keep_wide[...].astype(BF16)
        give_ref[...] = give_wide[...].astype(BF16)


def narrow_result(own_acts, far_acts, middle, vectors, blocks, after=()):
    rows, width = middle.shape
    steps = 2
    half = rows // PAD * SEQ
    rowed = [in_hbm(own_acts), in_hbm(far_acts), middle]
    others = [vectors, *blocks]
    out = jax.ShapeDtypeStruct((half, width // 2), BF16)
    return run_kernel(
        result_kernel,
        [*rowed, *others],
        after,
        grid=(steps,),
        in_specs=[row_spec(r, steps) for r in rowed] + [whole_spec(o) for o in others],
        out_specs=[whole_spec(out)] * 2,
        out_shape=[out] * 2,
        scratch_shapes=[pltpu.VMEM((half, width // 2), F32)] * 2,
        **kernel_params(4 * rows * width * own_acts.shape[1], 12 * rows * width),
    )


def weight_grad_kernel(split_dim, left_own, left_other, right_own, right_other, keep_ref, send_ref):
    total = matmul_left(side(left_own, left_other, 0), side(right_own, right_other, 0))
    half = total.shape[split_dim] // 2
    if split_dim == 0:
        keep_ref[:half] = total[:half].astype(BF16)
        send_ref[:half] = total[half:].astype(BF16)
        extra = keep_ref.shape[0] - half
        if extra:
            keep_ref[half:] = jnp.zeros((extra, total.shape[1]), BF16)
            send_ref[half:] = jnp.zeros((extra, total.shape[1]), BF16)
    else:
        keep_ref[...] = total[:, :half].astype(BF16)
        send_ref[...] = total[:, half:].astype(BF16)


def weight_grad(left_own, left_other, right_own, right_other, split_dim, tile, extra=0, more=0, after=()):
    rows, height = left_own.shape
    width = right_own.shape[1]
    if split_dim == 0:
        left = pl.BlockSpec((rows, height), lambda j: (0, 0))
        right = pl.BlockSpec((rows, tile), lambda j: (0, j))
        out = pl.BlockSpec((height // 2 + extra, tile), lambda j: (0, j))
        shape, steps = (height // 2 + extra, width + more), width // tile
    else:
        left = pl.BlockSpec((rows, tile), lambda j: (0, j))
        right = pl.BlockSpec((rows, width), lambda j: (0, 0))
        out = pl.BlockSpec((tile, width // 2), lambda j: (j, 0))
        shape, steps = (height, width // 2), height // tile
    return run_kernel(
        partial(weight_grad_kernel, split_dim),
        [in_hbm(v) for v in (left_own, left_other, right_own, right_other)],
        after,
        grid=(steps,),
        in_specs=[left, left, right, right],
        out_specs=[out, out],
        out_shape=[jax.ShapeDtypeStruct(shape, BF16)] * 2,
        **kernel_params(
            4 * rows * height * width, 4 * rows * (height + width) + 3 * height * width
        ),
    )


def out_grad_kernel(left_own, left_other, right_own, right_other, keep_in, send_in, keep_ref, send_ref):
    total = matmul_left(side(left_own, left_other, 0), side(right_own, right_other, 0))
    half = total.shape[1] // 2
    keep_ref[...] = total[:, :half].astype(BF16)
    send_ref[...] = total[:, half:].astype(BF16)


def out_weight_grad(left_own, left_other, right_own, right_other, keep, send, after=()):
    rows, height = left_own.shape
    values = [in_hbm(v) for v in (left_own, left_other, right_own, right_other)]
    place = keep.shape[1] // height - 1
    out = pl.BlockSpec((height, height), lambda i: (0, place))
    unread = pl.BlockSpec(memory_space=pl.ANY)
    return run_kernel(
        out_grad_kernel,
        [*values, keep, send],
        after,
        grid=(1,),
        in_specs=[whole_spec(v) for v in values] + [unread, unread],
        out_specs=[out, out],
        out_shape=[jax.ShapeDtypeStruct(v.shape, v.dtype) for v in (keep, send)],
        input_output_aliases={4: 0, 5: 1},
        **kernel_params(8 * rows * height * height, 4 * rows * height),
    )


def together(*values):
    return lax.optimization_barrier(values)


def move(values, distance):
    size = lax.axis_size("dp")
    return lax.ppermute(values, "dp", [(i, i ^ distance) for i in range(size)])


def bit_of(distance):
    return (lax.axis_index("dp") // distance) % 2


def cut(values, index, parts):
    size = values.shape[0] // parts
    return lax.dynamic_slice_in_dim(values, index * size, size, 0)


def quarter(block):
    return cut(block, lax.axis_index("dp") % 4, 4)


def spread(piece):
    return piece, move(piece, 1), move(piece, 2), move(piece, 3)


def assemble(pieces):
    low, high = bit_of(1) == 1, bit_of(2) == 1
    first = [jnp.where(low, pieces[j ^ 1], pieces[j]) for j in range(4)]
    return jnp.concatenate([jnp.where(high, first[j ^ 2], first[j]) for j in range(4)], axis=0)


def in_order(bit, mine, other):
    return jnp.where(
        bit == 0,
        jnp.concatenate([mine, other], axis=0),
        jnp.concatenate([other, mine], axis=0),
    )


def added(first, second):
    return (first.astype(F32) + second.astype(F32)).astype(BF16)


class GradSum:
    def __init__(self, keep, send):
        self.keep, self.send = keep, send
        self.half = keep.shape[0] // 2
        self.bit = bit_of(1)
        size = lax.axis_size("dp")
        self.middle = [2**k for k in range(1, size.bit_length() - 2)]
        self.last = size // 2

    def start_first(self):
        keep_b, send_b = self.keep[self.half :], self.send[self.half :]
        out_a = swap(self.send[: self.half], "col")
        other = jnp.concatenate([cut(keep_b, 1 - self.bit, 2), cut(send_b, 1 - self.bit, 2)], axis=0)
        return out_a, move(other, 1)

    def start_second(self, arrived):
        from_col, from_dp = arrived
        keep_b, send_b = self.keep[self.half :], self.send[self.half :]
        quarter_rows = self.half // 2
        self.lower = added(cut(keep_b, self.bit, 2), from_dp[:quarter_rows])
        lower_send = added(cut(send_b, self.bit, 2), from_dp[quarter_rows:])
        keep_a = self.keep[: self.half]
        self.upper = added(cut(keep_a, self.bit, 2), cut(from_col, self.bit, 2))
        upper_send = added(cut(keep_a, 1 - self.bit, 2), cut(from_col, 1 - self.bit, 2))
        return swap(lower_send, "col"), move(upper_send, 1)

    def end_second(self, arrived):
        from_col, from_dp = arrived
        self.held = jnp.concatenate(
            [added(self.upper, from_dp), added(self.lower, from_col)], axis=0
        )

    def start_halving(self, distance):
        bit = bit_of(distance)
        self.kept = cut(self.held, bit, 2)
        return move(cut(self.held, 1 - bit, 2), distance)

    def end_halving(self, arrived):
        self.held = added(self.kept, arrived)

    def start_last(self):
        return move(self.held, self.last)

    def end_last(self, arrived):
        self.held = added(self.held, arrived)

    def start_doubling(self, distance):
        return move(self.held, distance)

    def end_doubling(self, distance, arrived):
        self.held = in_order(bit_of(distance), self.held, arrived)

    def start_whole(self):
        return move(self.held, 1)

    def end_whole(self, arrived):
        half = self.half // 2
        upper = in_order(self.bit, self.held[:half], arrived[:half])
        lower = in_order(self.bit, self.held[half:], arrived[half:])
        return jnp.concatenate([upper, lower], axis=0)


def per_device(
    tokens,
    cotangent,
    ln1_gain,
    ln1_bias,
    qkv_weight,
    qv_bias,
    out_weight,
    out_bias,
    ln2_gain,
    ln2_bias,
    fc1_weight,
    fc1_bias,
    fc2_weight,
    fc2_bias,
):
    col = lax.axis_index("col")
    col_scalar = jnp.full((1,), col, jnp.int32)
    half = tokens.shape[0] // 2
    qkv_cols = qkv_weight.shape[1]
    units = fc1_weight.shape[1]

    def give_half(block, place):
        return lax.dynamic_slice_in_dim(block, (1 - place) * half, half, 0)

    qkv_piece = swap(quarter(qkv_weight), "col")
    col_rows, row_values = pack_vectors(
        (ln1_gain, ln1_bias, ln2_gain, ln2_bias, out_bias, fc2_bias), qv_bias, fc1_bias
    )
    col_other = swap(col_rows, "col")
    row_other = swap(row_values, "row")
    qkv_swap = swap(qkv_weight, "row")
    qkv_piece, col_other, row_other, token_give = together(
        qkv_piece, col_other, row_other, give_half(tokens, col)
    )
    qkv_pieces = spread(qkv_piece)
    token_other = swap(token_give, "col")
    vectors = jnp.concatenate([col_rows, col_other], axis=1)
    qkv_bias = jnp.concatenate([row_values[:, :qkv_cols], row_other[:, :qkv_cols]], axis=1)

    first_piece, late_col, late_dp = together(qkv_pieces[1], col, lax.axis_index("dp"))
    qkv_pieces = (qkv_pieces[0], first_piece, *qkv_pieces[2:])
    fc1_give = cut(fc1_weight, late_dp % 4, 4)
    fc2_give = cut(fc2_weight, late_dp % 2, 2)
    cot_give = give_half(cotangent, late_col)
    qkv_pieces, token_other, fc1_give, vectors, qkv_bias, fc2_give, cot_give = together(
        qkv_pieces, token_other, fc1_give, vectors, qkv_bias, fc2_give, cot_give
    )
    qkv_far = assemble(qkv_pieces)
    qkv_far_swap = swap(qkv_far, "row")
    fc1_piece = swap(fc1_give, "col")
    qkv_blocks = [qkv_weight, qkv_swap, qkv_far, qkv_far_swap]
    stream, packed, normed1, end = widen_qkv(
        col_scalar, tokens, token_other, vectors, qkv_bias, qkv_blocks
    )

    end, fc1_piece, fc2_give, out_give = together(end, fc1_piece, fc2_give, out_weight)
    fc1_pieces = spread(fc1_piece)
    out_far = swap(out_give, "col")
    fc2_piece = swap(fc2_give, "col")
    out_swap = swap(out_weight, "row")
    attended_mine, attended_away, probs, end = attend(packed, end)

    end, fc1_pieces, out_far, out_swap, fc2_piece = together(
        end, fc1_pieces, out_far, out_swap, fc2_piece
    )
    fc2_wing = move(fc2_piece, 1)
    out_far_swap = swap(out_far, "row")
    fc1_far = assemble(fc1_pieces)
    fc1_far_swap = swap(fc1_far, "row")
    fc1_swap = swap(fc1_weight, "row")
    out_blocks = [out_weight, out_far, out_swap, out_far_swap]
    middle, normed2, end = narrow_out(
        stream, attended_mine, attended_away, vectors, out_blocks, end
    )

    end, fc1_swap, fc1_far_swap, fc2_swap, cot_give = together(
        end, fc1_swap, fc1_far_swap, fc2_weight, cot_give
    )
    cot_other = swap(cot_give, "col")
    fc2_swap = swap(fc2_swap, "row")
    fc1_blocks = [fc1_weight, fc1_far, fc1_swap, fc1_far_swap]
    active, slope, active_far, slope_far, end = widen_gelu(
        normed2, fc1_blocks, row_values[:, qkv_cols:], row_other[:, qkv_cols:], end
    )

    end, fc2_piece, fc2_wing, fc2_swap, cot_other = together(
        end, fc2_piece, fc2_wing, fc2_swap, cot_other
    )
    fc2_away = in_order(bit_of(1), fc2_piece, fc2_wing)
    fc2_away_swap = swap(fc2_away, "row")
    active_other = swap(active_far, "row")
    upstream, fc2_bgrad, end = take_images(col_scalar, cotangent, cot_other, end)
    upstream_other = swap(upstream, "row")
    fc2_blocks = [fc2_weight, fc2_away, fc2_swap, fc2_away_swap]
    before_grad, before_sum, before_far, before_far_sum, end = widen_back(
        upstream, fc2_blocks, slope, slope_far, end
    )

    end, active_other, upstream_other = together(end, active_other, upstream_other)
    before_other = swap(before_far, "row")
    normed2_other = swap(normed2, "row")
    attended_other = swap(attended_away, "row")
    normed1_other = swap(normed1, "row")
    fc2_keep, fc2_send, end = weight_grad(
        active, active_other, upstream, upstream_other, 1, 512, after=end
    )

    sum2 = GradSum(fc2_keep, fc2_send)
    flying2 = sum2.start_first()
    middle_grad, middle_low, attended_grad, attended_grad_far, middle_sums, end = middle_back(
        before_grad,
        before_far,
        middle,
        upstream,
        vectors,
        [fc1_weight, fc1_swap, fc1_far, fc1_far_swap],
        out_blocks,
        end,
    )

    end, flying2, before_other, normed2_other, attended_other, normed1_other = together(
        end, flying2, before_other, normed2_other, attended_other, normed1_other
    )
    flying2 = sum2.start_second(flying2)
    middle_other = swap(middle_low, "row")
    fc1_keep, fc1_send, end = weight_grad(
        normed2, normed2_other, before_grad, before_other, 0, 768, more=384, after=end
    )

    end, flying2, middle_other = together(end, flying2, middle_other)
    sum2.end_second(flying2)
    middle_steps = sum2.middle
    for distance in middle_steps[:-1]:
        sum2.end_halving(sum2.start_halving(distance))
    flying2 = sum2.start_halving(middle_steps[-1])
    fc1_keep, fc1_send, end = out_weight_grad(
        attended_mine, attended_other, middle_low, middle_other, fc1_keep, fc1_send, end
    )

    end, flying2 = together(end, flying2)
    sum1 = GradSum(fc1_keep, fc1_send)
    flying1 = sum1.start_first()
    sum2.end_halving(flying2)
    flying2 = sum2.start_last()
    packed_grad, packed_grad_far, end = attend_back(
        packed, probs, attended_grad, attended_grad_far, end
    )

    end, flying1, flying2 = together(end, flying1, flying2)
    packed_other = swap(packed_grad_far, "row")
    flying1 = sum1.start_second(flying1)
    sum2.end_last(flying2)
    flying2 = sum2.start_doubling(middle_steps[-1])
    input_own, input_give, input_sums, packed_sums, end = input_back(
        packed_grad, packed_grad_far, stream, middle_grad, vectors, qkv_blocks, end
    )

    end, flying1, flying2, packed_other = together(end, flying1, flying2, packed_other)
    sum1.end_second(flying1)
    for distance in middle_steps[:-1]:
        sum1.end_halving(sum1.start_halving(distance))
    flying1 = sum1.start_halving(middle_steps[-1])
    sum2.end_doubling(middle_steps[-1], flying2)
    for distance in reversed(middle_steps[:-1]):
        sum2.end_doubling(distance, sum2.start_doubling(distance))
    flying2 = sum2.start_whole()
    kinds = packed_sums.reshape(-1, 3, HEAD)
    width = input_sums.shape[1]
    qv_grad = jnp.stack([kinds[:, 0], kinds[:, 2]], axis=1).reshape(2, -1, width)
    fc1_bgrad = jnp.stack([before_sum.reshape(-1, width), before_far_sum.reshape(-1, width)])
    by_row = jnp.concatenate([qv_grad, fc1_bgrad], axis=1)
    by_col = jnp.concatenate([input_sums, middle_sums, fc2_bgrad], axis=0)
    row_count = by_row.shape[1]
    small_other = swap(jnp.concatenate([by_row[1], by_col], axis=0), "row")
    qkv_keep, qkv_send, end = weight_grad(
        normed1, normed1_other, packed_grad, packed_other, 0, 384, EXTRA, after=end
    )

    end, flying1, small_other = together(end, flying1, small_other)
    by_row = (by_row[0] + small_other[:row_count]).reshape(-1, qkv_cols)
    by_col = by_col + small_other[row_count:]
    begin = qkv_keep.shape[0] - EXTRA
    both_cols = [
        jnp.concatenate([by_row, half_cols.reshape(-1, qkv_cols)], axis=0).astype(BF16)
        for half_cols in jnp.split(by_col, 2, axis=1)
    ]
    qkv_keep = lax.dynamic_update_slice(qkv_keep, both_cols[0], (begin, 0))
    qkv_send = lax.dynamic_update_slice(qkv_send, both_cols[1], (begin, 0))

    sum0 = GradSum(qkv_keep, qkv_send)
    flying0 = sum0.start_first()
    sum1.end_halving(flying1)
    flying1 = sum1.start_last()
    result_own, result_give, end = narrow_result(
        active, active_far, middle, vectors, fc2_blocks, end
    )

    flying0, result_give = together(flying0, result_give)
    flying0 = sum0.start_second(flying0)

    flying0, flying1, flying2, input_give = together(flying0, flying1, flying2, input_give)
    sum0.end_second(flying0)
    for distance in middle_steps[:-1]:
        sum0.end_halving(sum0.start_halving(distance))
    flying0 = sum0.start_halving(middle_steps[-1])
    sum1.end_last(flying1)
    flying1 = sum1.start_doubling(middle_steps[-1])
    input_other = swap(input_give, "col")
    fc2_wgrad = sum2.end_whole(flying2).astype(F32)

    (flying0,) = together(flying0)
    sum0.end_halving(flying0)
    flying0 = sum0.start_last()
    sum1.end_doubling(middle_steps[-1], flying1)
    for distance in reversed(middle_steps[:-1]):
        sum1.end_doubling(distance, sum1.start_doubling(distance))
    flying1 = sum1.start_whole()

    input_other, result_give = together(input_other, result_give)
    result_other = swap(result_give, "col")
    (flying0,) = together(flying0)
    sum0.end_last(flying0)
    flying0 = sum0.start_doubling(middle_steps[-1])
    input_grad = in_order(col, input_own, input_other.astype(F32))

    (flying0,) = together(flying0)
    sum0.end_doubling(middle_steps[-1], flying0)
    for distance in reversed(middle_steps[:-1]):
        sum0.end_doubling(distance, sum0.start_doubling(distance))
    flying0 = sum0.start_whole()
    fc1_out_grad = sum1.end_whole(flying1)
    result = in_order(col, result_own, result_other)
    fc1_wgrad = fc1_out_grad[:, :units].astype(F32)
    out_wgrad = fc1_out_grad[:, units:].astype(F32)
    flying0, result, fc1_wgrad, out_wgrad = together(flying0, result, fc1_wgrad, out_wgrad)
    qkv_whole = sum0.end_whole(flying0)
    qv_size = qv_bias.shape[0]
    rows_each = by_row.shape[0]
    vector_rows = qkv_whole[begin : begin + 2 * rows_each].astype(F32)
    by_row = vector_rows[:rows_each].reshape(-1)
    by_col = vector_rows[rows_each:].reshape(6, -1)
    return (
        result,
        input_grad,
        by_col[0],
        by_col[1],
        qkv_whole[:begin].astype(F32),
        by_row[:qv_size],
        out_wgrad,
        by_col[4],
        by_col[2],
        by_col[3],
        fc1_wgrad,
        by_row[qv_size:],
        fc2_wgrad,
        by_col[5],
    )


def solution(mesh):
    stream = P(("dp", "row"), "col")
    by_col, by_row = P("col"), P("row")
    wide, deep = P("col", "row"), P("row", "col")
    in_specs = (
        stream, stream, by_col, by_col, wide, by_row, deep, by_col,
        by_col, by_col, wide, by_row, deep, by_col,
    )
    return jax.shard_map(
        per_device, mesh=mesh, in_specs=in_specs, out_specs=in_specs, check_vma=False
    )
```
